32 devices in a mesh: dp: 8 (over z, core), seq: 4 (over y, x).
Axes of the slice: x: 2, y: 2, z: 4, core: 2. Of those that a mesh axis runs over, the one named last changes fastest.
Arguments:
- queries: bfloat16 [8, 1024, 1024], P('dp', 'seq'), may hold values from -80 to 80
- keys: bfloat16 [8, 1024, 1024], P('dp', 'seq'), may hold values from -80 to 80
- values: bfloat16 [8, 1024, 1024], P('dp', 'seq'), may hold values from -12 to 12
- upstream: bfloat16 [8, 1024, 1024], P('dp', 'seq'), may hold values from -6 to 6
- w_out: bfloat16 [1024, 1024], replicated, may hold values from -0.1875 to 0.1875
- key_blocks: int32 [8, 8, 4], P('dp'), may hold values from 0 to 7, as said below
- block_counts: int32 [8, 8], P('dp'), may hold values from 1 to 4, as said below
Outputs:
- mixed: bfloat16 [8, 1024, 1024], P('dp', 'seq')
- grad_q: bfloat16 [8, 1024, 1024], P('dp', 'seq')
- grad_k: bfloat16 [8, 1024, 1024], P('dp', 'seq')
- grad_v: bfloat16 [8, 1024, 1024], P('dp', 'seq')
- grad_wo: float32 [1024, 1024], P('seq', 'dp')
The draws below stay inside these ranges and needn't reach their ends.
Inputs may be any that keep to these rules, and one draw needn't show every extreme that they name: `key_blocks`: row b of a sequence's lists holds 4 distinct block numbers, the first of them b itself; entries past block_counts are valid numbers and are not used. `block_counts`: every sequence has a query block with exactly 4 used entries.
All inputs are finite; a program needn't handle non-finite values.
Results may differ from the reference program's by a relative error of at most 0.039.
Values may be sent and summed in bfloat16 or wider, within the bound.
A program may use at most 128 MiB of HBM per device.

```python
import math
import jax
import jax.numpy as jnp
from jax import lax

D = 1024
HEADS = 16
REPLICAS = 8
NODES = 1024
BLOCKS = 8
LISTED = 4


def draw_queries(key, part):
    key = jax.random.fold_in(key, 3)
    field = jnp.clip(jax.random.normal(key, (REPLICAS, NODES, D), jnp.float32), -6.0, 6.0)
    return field.astype(jnp.bfloat16)


def draw_keys(key, part):
    key = jax.random.fold_in(key, 4)
    field = jnp.clip(jax.random.normal(key, (REPLICAS, NODES, D), jnp.float32), -6.0, 6.0)
    return field.astype(jnp.bfloat16)


def draw_key_blocks(key, part):
    key = jax.random.fold_in(key, 5)
    split_keys = jax.random.split(key, REPLICAS * BLOCKS)
    shuffled = jax.vmap(lambda single: jax.random.permutation(single, BLOCKS - 1))(split_keys) + 1
    offsets = jnp.concatenate([jnp.zeros((REPLICAS * BLOCKS, 1), jnp.int32), shuffled.astype(jnp.int32)], axis=1)[:, :LISTED]
    starts = jnp.tile(jnp.arange(BLOCKS, dtype=jnp.int32), REPLICAS)[:, None]
    return ((starts + offsets) % BLOCKS).reshape(REPLICAS, BLOCKS, LISTED).astype(jnp.int32)


def draw_block_counts(key, part):
    key = jax.random.fold_in(key, 7)
    first, second = jax.random.split(key)
    counts = jax.random.randint(first, (REPLICAS, BLOCKS), 1, LISTED + 1)
    heavy = jax.random.randint(second, (REPLICAS,), 0, BLOCKS)
    counts = jnp.where(jnp.arange(BLOCKS)[None, :] == heavy[:, None], LISTED, counts)
    return counts.astype(jnp.int32)


def with_spikes(values, key, source, target, shards_of, factor):
    def block_of(position):
        return (jnp.arange(values.shape[position]) // (values.shape[position] // shards_of)).reshape((-1,) + (1,) * (values.ndim - 1 - position))

    near = jax.random.permutation(key, shards_of)[block_of(target)]
    far = (block_of(target) + shards_of // 2) % shards_of
    return jnp.where((block_of(source) == near) | (block_of(source) == far), factor * values, values)


def block_scale(key, shape, cuts, least, top_value):
    def one(dim, shards_of):
        heights = jax.random.uniform(jax.random.fold_in(jax.random.fold_in(key, 6), dim), (shards_of,), jnp.float32, least / len(cuts), top_value / len(cuts))
        return jnp.repeat(jnp.exp(heights), shape[dim] // shards_of).reshape((-1,) + (1,) * (len(shape) - dim - 1))

    gain = one(*cuts[0])
    for cut in cuts[1:]:
        gain = gain * one(*cut)
    return gain


def scatter_about(key, extent, scale, reach, shards=(), held_as=jnp.bfloat16):
    level = block_scale(key, extent, shards, -0.22, 0.18) if shards else 1.0
    drawn = jax.random.normal(key, extent, jnp.float32) * scale * level
    return jnp.minimum(jnp.maximum(drawn, -reach), reach).astype(held_as)


def noise_with(rng, dims, deviation, bound, pieces, heavy, kind=jnp.bfloat16):
    entries = deviation * jax.random.normal(rng, dims, jnp.float32)
    if pieces:
        entries = entries * block_scale(rng, dims, pieces, -0.22, 0.18)
    return jnp.clip(with_spikes(entries, jax.random.fold_in(rng, 3), *heavy), -bound, bound).astype(kind)


def setup_inputs(seed: int = 0) -> dict:
    splits = jax.random.split(jax.random.key(seed), 8)
    queries = draw_queries(jax.random.fold_in(splits[7], 71), 0)
    keys = draw_keys(jax.random.fold_in(splits[7], 71), 0)
    values = scatter_about(splits[2], (REPLICAS, NODES, D), 3.0, 12.0, ((0, 8), (1, 4)))
    upstream = noise_with(splits[3], (REPLICAS, NODES, D), 1.0, 6.0, ((0, 8), (1, 4)), (0, 2, 8, 2.0))
    w_out = scatter_about(splits[4], (D, D), D ** -0.5, 0.1875)
    key_blocks = draw_key_blocks(jax.random.fold_in(splits[7], 71), 0)
    block_counts = draw_block_counts(jax.random.fold_in(splits[7], 71), 0)
    return dict(queries=queries, keys=keys, values=values, upstream=upstream, w_out=w_out, key_blocks=key_blocks, block_counts=block_counts)


blocks_per_step = 4

def product(form, left, right):
    return jnp.einsum(form, left.astype(jnp.float32), right.astype(jnp.float32), precision=lax.Precision.HIGHEST)

def block_attention(head_q, head_k, head_v, head_g, key_lists, key_counts):
    node_count, head_count, head_width = head_q.shape
    block_count, listed = key_lists.shape
    block_rows = node_count // block_count
    steps_count = block_count // blocks_per_step
    score_scale = 1.0 / math.sqrt(head_width)
    query_groups = head_q.reshape(steps_count, blocks_per_step, block_rows, head_count, head_width)
    grad_groups = head_g.reshape(steps_count, blocks_per_step, block_rows, head_count, head_width)
    key_table = head_k.reshape(block_count, block_rows, head_count, head_width)
    value_table = head_v.reshape(block_count, block_rows, head_count, head_width)
    list_groups = key_lists.reshape(steps_count, blocks_per_step, listed)
    count_groups = key_counts.reshape(steps_count, blocks_per_step)
    slot_index = jnp.arange(listed, dtype=jnp.int32)

    def one_step(accumulated, inputs):
        key_acc, value_acc = accumulated
        query_part, grad_part, list_part, count_part = inputs
        keys_near = key_table[list_part]
        values_near = value_table[list_part]
        scores = product('gqnd,gjknd->gnqjk', query_part, keys_near) * score_scale
        usable = (slot_index[None, :] < count_part[:, None])[:, None, None, :, None]
        scores = jnp.where(usable, scores, -jnp.inf)
        highest = lax.optimization_barrier(jnp.max(scores, axis=(3, 4), keepdims=True))
        raised = jnp.exp(scores - highest)
        probability = raised / lax.optimization_barrier(jnp.sum(raised, axis=(3, 4), keepdims=True))
        weights = probability.astype(jnp.bfloat16)
        attended = product('gnqjk,gjknd->gqnd', weights, values_near).astype(jnp.bfloat16)
        row_delta = lax.optimization_barrier(jnp.sum(grad_part.astype(jnp.float32) * attended.astype(jnp.float32), axis=3))
        grad_scores = product('gqnd,gjknd->gnqjk', grad_part, values_near)
        shifted = grad_scores - jnp.transpose(row_delta, (0, 2, 1))[:, :, :, None, None]
        grad_logits = (probability * shifted).astype(jnp.bfloat16)
        grad_query = (product('gnqjk,gjknd->gqnd', grad_logits, keys_near) * score_scale).astype(jnp.bfloat16)
        key_terms = product('gnqjk,gqnd->gjknd', grad_logits, query_part) * score_scale
        value_terms = product('gnqjk,gqnd->gjknd', weights, grad_part)
        flat_list = list_part.reshape(-1)
        key_acc = key_acc.at[flat_list].add(key_terms.reshape(-1, block_rows, head_count, head_width))
        value_acc = value_acc.at[flat_list].add(value_terms.reshape(-1, block_rows, head_count, head_width))
        return ((key_acc, value_acc), (attended, grad_query))
    empty = jnp.zeros((block_count, block_rows, head_count, head_width), jnp.float32)
    (key_acc, value_acc), (attended, grad_query) = lax.scan(one_step, (empty, empty), (query_groups, grad_groups, list_groups, count_groups))
    shape = (node_count, head_count, head_width)
    return (attended.reshape(shape), grad_query.reshape(shape), key_acc.astype(jnp.bfloat16).reshape(shape), value_acc.astype(jnp.bfloat16).reshape(shape))

def reference(queries, keys, values, upstream, w_out, key_blocks, block_counts):
    replica_count, node_count, width = queries.shape
    head_width = width // HEADS
    up_flat = upstream.reshape(-1, width)
    grad_att = jnp.dot(up_flat, w_out.T, preferred_element_type=jnp.float32).astype(jnp.bfloat16)

    def split_heads(array):
        return array.reshape(replica_count, node_count, HEADS, head_width)

    def per_replica(inputs):
        return block_attention(*inputs)
    attended, grad_query, grad_key, grad_value = lax.map(per_replica, (split_heads(queries), split_heads(keys), split_heads(values), split_heads(grad_att.reshape(replica_count, node_count, width)), key_blocks, block_counts))
    full_shape = (replica_count, node_count, width)
    att_flat = attended.reshape(-1, width)
    mixed = jnp.dot(att_flat, w_out, preferred_element_type=jnp.float32).astype(jnp.bfloat16).reshape(full_shape)
    grad_wo = jnp.dot(att_flat.T, up_flat, preferred_element_type=jnp.float32) * (1.0 / math.sqrt(replica_count * node_count))
    return (mixed, grad_query.reshape(full_shape), grad_key.reshape(full_shape), grad_value.reshape(full_shape), grad_wo)
```

```python
import functools
import math

import jax
import jax.numpy as jnp
from jax import lax
from jax.experimental import pallas as pl
from jax.experimental.pallas import tpu as pltpu
from jax.sharding import PartitionSpec as P

HEADS = 16


blocks_per_step = 4


def product(form, left, right):
    return jnp.einsum(form, left, right, preferred_element_type=jnp.float32)


def inner_rows(left, right):
    return lax.dot_general(
        left, right, (((0,), (0,)), ((), ())), preferred_element_type=jnp.float32
    )


def block_attention(head_q, head_k, head_v, head_g, key_lists, key_counts):
    node_count, head_count, head_width = head_q.shape
    block_count, listed = key_lists.shape
    block_rows = node_count // block_count
    steps_count = block_count // blocks_per_step
    score_scale = 1.0 / math.sqrt(head_width)
    query_groups = head_q.reshape(steps_count, blocks_per_step, block_rows, head_count, head_width)
    grad_groups = head_g.reshape(steps_count, blocks_per_step, block_rows, head_count, head_width)
    key_table = head_k.reshape(block_count, block_rows, head_count, head_width)
    value_table = head_v.reshape(block_count, block_rows, head_count, head_width)
    list_groups = key_lists.reshape(steps_count, blocks_per_step, listed)
    count_groups = key_counts.reshape(steps_count, blocks_per_step)
    slot_index = jnp.arange(listed, dtype=jnp.int32)

    def one_step(accumulated, inputs):
        key_acc, value_acc = accumulated
        query_part, grad_part, list_part, count_part = inputs
        keys_near = key_table[list_part]
        values_near = value_table[list_part]
        scores = product("gqnd,gjknd->gnqjk", query_part, keys_near) * score_scale
        usable = (slot_index[None, :] < count_part[:, None])[:, None, None, :, None]
        scores = jnp.where(usable, scores, -jnp.inf)
        highest = jnp.max(scores, axis=(3, 4), keepdims=True)
        raised = jnp.exp(scores - highest)
        probability = raised / jnp.sum(raised, axis=(3, 4), keepdims=True)
        weights = probability.astype(jnp.bfloat16)
        attended = product("gnqjk,gjknd->gqnd", weights, values_near).astype(jnp.bfloat16)
        row_delta = jnp.sum(grad_part.astype(jnp.float32) * attended.astype(jnp.float32), axis=3)
        grad_scores = product("gqnd,gjknd->gnqjk", grad_part, values_near)
        shifted = grad_scores - jnp.transpose(row_delta, (0, 2, 1))[:, :, :, None, None]
        grad_logits = (probability * shifted).astype(jnp.bfloat16)
        grad_query = (product("gnqjk,gjknd->gqnd", grad_logits, keys_near) * score_scale).astype(
            jnp.bfloat16
        )
        key_terms = product("gnqjk,gqnd->gjknd", grad_logits, query_part) * score_scale
        value_terms = product("gnqjk,gqnd->gjknd", weights, grad_part)
        flat_list = list_part.reshape(-1)
        key_acc = key_acc.at[flat_list].add(
            key_terms.reshape(-1, block_rows, head_count, head_width)
        )
        value_acc = value_acc.at[flat_list].add(
            value_terms.reshape(-1, block_rows, head_count, head_width)
        )
        return ((key_acc, value_acc), (attended, grad_query))

    empty = jnp.zeros((block_count, block_rows, head_count, head_width), jnp.float32)
    (key_acc, value_acc), (attended, grad_query) = lax.scan(
        one_step, (empty, empty), (query_groups, grad_groups, list_groups, count_groups)
    )
    shape = (node_count, head_count, head_width)
    return (
        attended.reshape(shape),
        grad_query.reshape(shape),
        key_acc.astype(jnp.bfloat16).reshape(shape),
        value_acc.astype(jnp.bfloat16).reshape(shape),
    )


def project_back(up_rows, w_out):
    return lax.dot_general(
        up_rows, w_out, (((1,), (1,)), ((), ())), preferred_element_type=jnp.float32
    ).astype(jnp.bfloat16)


def local_plain(queries, keys, values, upstream, w_out, key_blocks, block_counts):
    local_rows = queries.shape[1]
    width = queries.shape[2]
    head_width = width // HEADS
    up_rows = upstream[0]

    def split_heads(array):
        return array.reshape(local_rows, HEADS, head_width)

    query_heads = split_heads(queries[0])
    key_heads = split_heads(keys[0])
    value_heads = split_heads(values[0])
    grad_att = project_back(up_rows, w_out)
    head_q, head_k, head_v, head_g = (
        lax.all_to_all(query_heads, "seq", split_axis=1, concat_axis=0, tiled=True),
        lax.all_to_all(key_heads, "seq", split_axis=1, concat_axis=0, tiled=True),
        lax.all_to_all(value_heads, "seq", split_axis=1, concat_axis=0, tiled=True),
        lax.all_to_all(split_heads(grad_att), "seq", split_axis=1, concat_axis=0, tiled=True),
    )
    attended, grad_query, grad_key, grad_value = block_attention(
        head_q, head_k, head_v, head_g, key_blocks[0], block_counts[0]
    )
    node_att, node_gq, node_gk, node_gv = (
        lax.all_to_all(attended, "seq", split_axis=0, concat_axis=1, tiled=True),
        lax.all_to_all(grad_query, "seq", split_axis=0, concat_axis=1, tiled=True),
        lax.all_to_all(grad_key, "seq", split_axis=0, concat_axis=1, tiled=True),
        lax.all_to_all(grad_value, "seq", split_axis=0, concat_axis=1, tiled=True),
    )
    att_nodes = node_att.reshape(local_rows, width)
    mixed = jnp.dot(att_nodes, w_out, preferred_element_type=jnp.float32).astype(jnp.bfloat16)
    factor = 1.0 / math.sqrt(lax.axis_size("dp") * lax.axis_size("seq") * local_rows)
    summed = lax.psum_scatter(
        inner_rows(att_nodes, up_rows), "seq", scatter_dimension=0, tiled=True
    )
    grad_wo = lax.psum_scatter(summed, "dp", scatter_dimension=1, tiled=True)
    full_shape = (1, local_rows, width)
    return (
        mixed.reshape(full_shape),
        node_gq.reshape(full_shape),
        node_gk.reshape(full_shape),
        node_gv.reshape(full_shape),
        grad_wo * factor,
    )


MESH = pl.DeviceIdType.MESH
LANES = 128
MASKED = -1e30


def dot_nt(left, right):
    return lax.dot_general(
        left, right, (((1,), (1,)), ((), ())), preferred_element_type=jnp.float32
    )


def fused(
    peers, head_width, list_ref, count_ref, q_ref, k_ref, v_ref, u_ref, w_ref,
    mixed_ref, gq_ref, gk_ref, gv_ref, gw_ref,
    head_q, head_g, keys2, values2, g_local, out_stage, key_sum, value_sum, att_nodes,
    send_in, recv_in, send_out, recv_out, own_sem,
):
    me = lax.axis_index("seq")
    rows = q_ref.shape[0]
    chunks = head_q.shape[0]
    nodes = head_q.shape[1]
    blocks, listed = list_ref.shape
    block_rows = nodes // blocks
    per_device = blocks // peers
    span = chunks * LANES
    score_scale = 1.0 / math.sqrt(head_width)
    bf16, f32 = jnp.bfloat16, jnp.float32

    barrier = pltpu.get_barrier_semaphore()
    for p in range(1, peers):
        pl.semaphore_signal(
            barrier, inc=1, device_id={"seq": lax.rem(me + p, peers)}, device_id_type=MESH
        )
    pl.semaphore_wait(barrier, peers - 1)

    own_rows = pl.ds(pl.multiple_of(me * rows, rows), rows)

    def columns(device, c):
        return pl.ds(pl.multiple_of(device * span + c * LANES, LANES), LANES)

    sources = (q_ref, k_ref, v_ref, g_local)
    targets = (head_q, keys2, values2, head_g)

    def landing(a, c):
        if a in (1, 2):
            return targets[a].at[c, own_rows, pl.ds(0, LANES)]
        return targets[a].at[c, own_rows]

    def inward(a, c, p):
        device = lax.rem(me + p, peers)
        return pltpu.make_async_remote_copy(
            src_ref=sources[a].at[:, columns(device, c)],
            dst_ref=landing(a, c),
            send_sem=send_in.at[c, a, p - 1],
            recv_sem=recv_in.at[c, a, p - 1],
            device_id={"seq": device},
            device_id_type=MESH,
        )

    def own_copy(a, c):
        return pltpu.make_async_copy(
            sources[a].at[:, columns(me, c)], landing(a, c), own_sem.at[c, a]
        )

    def start_in(a, c):
        for p in range(1, peers):
            inward(a, c, p).start()
        own_copy(a, c).start()

    def finish_in(a, c):
        for p in range(1, peers):
            inward(a, c, p).wait()
        own_copy(a, c).wait()

    returns = (att_nodes, gq_ref, gk_ref, gv_ref)

    def outward(a, c, p):
        device = lax.rem(me + p, peers)
        return pltpu.make_async_remote_copy(
            src_ref=out_stage.at[c, a, pl.ds(pl.multiple_of(device * rows, rows), rows)],
            dst_ref=returns[a].at[:, columns(me, c)],
            send_sem=send_out.at[c, a, p - 1],
            recv_sem=recv_out.at[c, a, p - 1],
            device_id={"seq": device},
            device_id_type=MESH,
        )

    def keep_own(a, c):
        returns[a][:, columns(me, c)] = out_stage[c, a, own_rows, :]

    def grad_att(c):
        def one(device, carry):
            cols = columns(device, c)
            g_local[:, cols] = dot_nt(u_ref[...], w_ref[cols, :]).astype(bf16)
            return carry

        lax.fori_loop(0, peers, one, 0)

    lane = lax.broadcasted_iota(jnp.int32, (block_rows, LANES), 1)
    lane2 = lax.broadcasted_iota(jnp.int32, (2 * block_rows, LANES), 1)
    first = lane < head_width

    def stacked(x):
        return jnp.concatenate([jnp.where(first, x, 0.0), jnp.where(first, 0.0, x)], axis=0)

    def merged(x):
        return jnp.where(first, x[:block_rows], x[block_rows:])

    def attend(c):
        key_sum[...] = jnp.zeros_like(key_sum)
        value_sum[...] = jnp.zeros_like(value_sum)

        def one_block(i, carry):
            p = i // per_device + 1
            b = lax.rem(me + p, peers) * per_device + lax.rem(i, per_device)
            here = pl.ds(pl.multiple_of(b * block_rows, block_rows), block_rows)
            q = head_q[c, here, :].astype(f32) * score_scale
            g = head_g[c, here, :].astype(f32)
            count = count_ref[b]
            used = lane2 < 0
            for j in range(listed):
                used = used | (lane2 == jnp.where(j < count, list_ref[b, j], -1))
            q_pair = stacked(q)
            g_pair = stacked(g)
            left = jnp.concatenate([q_pair, jnp.where(used, 0.0, MASKED)], axis=1).astype(bf16)
            scores = dot_nt(left, keys2[c])
            raised = jnp.exp(scores - jnp.max(scores, axis=1, keepdims=True))
            weights = raised.astype(bf16)
            summed = jnp.dot(weights, values2[c], preferred_element_type=f32)
            inverse = 1.0 / summed[:, LANES:LANES + 1]
            attended = merged(summed[:, :LANES] * inverse).astype(bf16)
            delta = jnp.sum(
                g_pair * jnp.concatenate([attended, attended], axis=0).astype(f32),
                axis=1, keepdims=True,
            )
            high = delta.astype(bf16).astype(f32)
            middle = (delta - high).astype(bf16).astype(f32)
            low = delta - high - middle
            shift = jnp.where(
                lane2 == 0, -high, jnp.where(lane2 == 1, -middle, jnp.where(lane2 == 2, -low, 0.0))
            )
            right = jnp.concatenate([g_pair, shift], axis=1).astype(bf16)
            shifted = dot_nt(right, values2[c])
            logits = (raised * shifted).astype(bf16)
            grad_q = jnp.dot(logits, keys2[c, :, :LANES], preferred_element_type=f32)
            grad_q = merged(grad_q * (inverse * score_scale))
            key_sum[...] += inner_rows((q_pair * inverse).astype(bf16), logits)
            value_sum[...] += inner_rows((g_pair * inverse).astype(bf16), weights)
            out_stage[c, 0, here, :] = attended
            out_stage[c, 1, here, :] = grad_q.astype(bf16)

            @pl.when((lax.rem(i, per_device) == per_device - 1) & (p < peers))
            def _():
                outward(0, c, p).start()
                outward(1, c, p).start()

            return carry

        lax.fori_loop(0, blocks, one_block, 0)
        out_stage[c, 2] = key_sum[...].T.astype(bf16)
        out_stage[c, 3] = value_sum[...].T.astype(bf16)
        for p in range(1, peers):
            outward(2, c, p).start()
            outward(3, c, p).start()
        for a in range(4):
            keep_own(a, c)

    for a in range(3):
        start_in(a, 0)
    grad_att(0)
    start_in(3, 0)
    for c in range(1, chunks):
        grad_att(c)
    block_of = lax.broadcasted_iota(jnp.int32, (nodes, LANES), 0) // block_rows
    node_lane = lax.broadcasted_iota(jnp.int32, (nodes, LANES), 1)
    for c in range(chunks):
        keys2[c, :, LANES:] = jnp.where(node_lane == block_of, 1.0, 0.0).astype(bf16)
        values2[c, :, LANES:] = jnp.where(node_lane < 3, 1.0, 0.0).astype(bf16)
    for c in range(chunks):
        for a in range(4):
            if a == 3 and c + 1 < chunks:
                for later in range(4):
                    start_in(later, c + 1)
            finish_in(a, c)
        attend(c)
    for c in range(chunks):
        for p in range(1, peers):
            outward(0, c, p).wait()
    mixed_ref[...] = jnp.dot(att_nodes[...], w_ref[...], preferred_element_type=f32).astype(bf16)
    gw_ref[...] = inner_rows(att_nodes[...], u_ref[...])
    for c in range(chunks):
        for a in range(1, 4):
            for p in range(1, peers):
                outward(a, c, p).wait()


def local_fused(queries, keys, values, upstream, w_out, key_blocks, block_counts):
    rows, width = queries.shape[1:]
    peers = lax.axis_size("seq")
    chunks = width // peers // LANES
    nodes = rows * peers
    bf16, f32 = jnp.bfloat16, jnp.float32
    vmem = pl.BlockSpec(memory_space=pltpu.VMEM)
    smem = pl.BlockSpec(memory_space=pltpu.SMEM)
    part = jax.ShapeDtypeStruct((rows, width), bf16)
    mixed, grad_q, grad_k, grad_v, partial = pl.pallas_call(
        functools.partial(fused, peers, width // HEADS),
        out_shape=(part, part, part, part, jax.ShapeDtypeStruct((width, width), f32)),
        in_specs=[smem, smem] + [vmem] * 5,
        out_specs=[vmem] * 5,
        scratch_shapes=[
            pltpu.VMEM((chunks, nodes, LANES), bf16),
            pltpu.VMEM((chunks, nodes, LANES), bf16),
            pltpu.VMEM((chunks, nodes, 2 * LANES), bf16),
            pltpu.VMEM((chunks, nodes, 2 * LANES), bf16),
            pltpu.VMEM((rows, width), bf16),
            pltpu.VMEM((chunks, 4, nodes, LANES), bf16),
            pltpu.VMEM((LANES, nodes), f32),
            pltpu.VMEM((LANES, nodes), f32),
            pltpu.VMEM((rows, width), bf16),
            pltpu.SemaphoreType.DMA((chunks, 4, peers - 1)),
            pltpu.SemaphoreType.DMA((chunks, 4, peers - 1)),
            pltpu.SemaphoreType.DMA((chunks, 4, peers - 1)),
            pltpu.SemaphoreType.DMA((chunks, 4, peers - 1)),
            pltpu.SemaphoreType.DMA((chunks, 4)),
        ],
        compiler_params=pltpu.CompilerParams(
            collective_id=0, has_side_effects=True, vmem_limit_bytes=56 * 1024 * 1024
        ),
        name="graph_attention",
    )(key_blocks[0], block_counts[0], queries[0], keys[0], values[0], upstream[0], w_out)
    factor = 1.0 / math.sqrt(lax.axis_size("dp") * nodes)
    summed = lax.psum_scatter(partial, "seq", scatter_dimension=0, tiled=True)
    grad_wo = lax.psum_scatter(summed, "dp", scatter_dimension=1, tiled=True)
    return mixed[None], grad_q[None], grad_k[None], grad_v[None], grad_wo * factor


def local(queries, keys, values, upstream, w_out, key_blocks, block_counts):
    width = queries.shape[2]
    peers = lax.axis_size("seq")
    pair = 2 * (width // HEADS) == LANES and width % (peers * LANES) == 0
    whole_blocks = key_blocks.shape[1] % peers == 0 and key_blocks.shape[1] <= LANES
    chosen = local_fused if pair and whole_blocks else local_plain
    return chosen(queries, keys, values, upstream, w_out, key_blocks, block_counts)


def solution(mesh):
    placed = (
        P("dp", "seq", None),
        P("dp", "seq", None),
        P("dp", "seq", None),
        P("dp", "seq", None),
        P(),
        P("dp", None, None),
        P("dp", None),
    )
    return jax.shard_map(
        local,
        mesh=mesh,
        in_specs=placed,
        out_specs=(
            P("dp", "seq", None),
            P("dp", "seq", None),
            P("dp", "seq", None),
            P("dp", "seq", None),
            P("seq", "dp"),
        ),
        check_vma=False,
    )
```

```python
import functools
import math

import jax
import jax.numpy as jnp
from jax import lax
from jax.experimental import pallas as pl
from jax.experimental.pallas import tpu as pltpu
from jax.sharding import PartitionSpec as P

HEADS = 16


blocks_per_step = 4


def product(form, left, right):
    return jnp.einsum(form, left, right, preferred_element_type=jnp.float32)


def inner_rows(left, right):
    return lax.dot_general(
        left, right, (((0,), (0,)), ((), ())), preferred_element_type=jnp.float32
    )


def block_attention(head_q, head_k, head_v, head_g, key_lists, key_counts):
    node_count, head_count, head_width = head_q.shape
    block_count, listed = key_lists.shape
    block_rows = node_count // block_count
    steps_count = block_count // blocks_per_step
    score_scale = 1.0 / math.sqrt(head_width)
    query_groups = head_q.reshape(steps_count, blocks_per_step, block_rows, head_count, head_width)
    grad_groups = head_g.reshape(steps_count, blocks_per_step, block_rows, head_count, head_width)
    key_table = head_k.reshape(block_count, block_rows, head_count, head_width)
    value_table = head_v.reshape(block_count, block_rows, head_count, head_width)
    list_groups = key_lists.reshape(steps_count, blocks_per_step, listed)
    count_groups = key_counts.reshape(steps_count, blocks_per_step)
    slot_index = jnp.arange(listed, dtype=jnp.int32)

    def one_step(accumulated, inputs):
        key_acc, value_acc = accumulated
        query_part, grad_part, list_part, count_part = inputs
        keys_near = key_table[list_part]
        values_near = value_table[list_part]
        scores = product("gqnd,gjknd->gnqjk", query_part, keys_near) * score_scale
        usable = (slot_index[None, :] < count_part[:, None])[:, None, None, :, None]
        scores = jnp.where(usable, scores, -jnp.inf)
        highest = jnp.max(scores, axis=(3, 4), keepdims=True)
        raised = jnp.exp(scores - highest)
        probability = raised / jnp.sum(raised, axis=(3, 4), keepdims=True)
        weights = probability.astype(jnp.bfloat16)
        attended = product("gnqjk,gjknd->gqnd", weights, values_near).astype(jnp.bfloat16)
        row_delta = jnp.sum(grad_part.astype(jnp.float32) * attended.astype(jnp.float32), axis=3)
        grad_scores = product("gqnd,gjknd->gnqjk", grad_part, values_near)
        shifted = grad_scores - jnp.transpose(row_delta, (0, 2, 1))[:, :, :, None, None]
        grad_logits = (probability * shifted).astype(jnp.bfloat16)
        grad_query = (product("gnqjk,gjknd->gqnd", grad_logits, keys_near) * score_scale).astype(
            jnp.bfloat16
        )
        key_terms = product("gnqjk,gqnd->gjknd", grad_logits, query_part) * score_scale
        value_terms = product("gnqjk,gqnd->gjknd", weights, grad_part)
        flat_list = list_part.reshape(-1)
        key_acc = key_acc.at[flat_list].add(
            key_terms.reshape(-1, block_rows, head_count, head_width)
        )
        value_acc = value_acc.at[flat_list].add(
            value_terms.reshape(-1, block_rows, head_count, head_width)
        )
        return ((key_acc, value_acc), (attended, grad_query))

    empty = jnp.zeros((block_count, block_rows, head_count, head_width), jnp.float32)
    (key_acc, value_acc), (attended, grad_query) = lax.scan(
        one_step, (empty, empty), (query_groups, grad_groups, list_groups, count_groups)
    )
    shape = (node_count, head_count, head_width)
    return (
        attended.reshape(shape),
        grad_query.reshape(shape),
        key_acc.astype(jnp.bfloat16).reshape(shape),
        value_acc.astype(jnp.bfloat16).reshape(shape),
    )


def project_back(up_rows, w_out):
    return lax.dot_general(
        up_rows, w_out, (((1,), (1,)), ((), ())), preferred_element_type=jnp.float32
    ).astype(jnp.bfloat16)


def local_plain(queries, keys, values, upstream, w_out, key_blocks, block_counts):
    local_rows = queries.shape[1]
    width = queries.shape[2]
    head_width = width // HEADS
    up_rows = upstream[0]

    def split_heads(array):
        return array.reshape(local_rows, HEADS, head_width)

    query_heads = split_heads(queries[0])
    key_heads = split_heads(keys[0])
    value_heads = split_heads(values[0])
    grad_att = project_back(up_rows, w_out)
    head_q, head_k, head_v, head_g = (
        lax.all_to_all(query_heads, "seq", split_axis=1, concat_axis=0, tiled=True),
        lax.all_to_all(key_heads, "seq", split_axis=1, concat_axis=0, tiled=True),
        lax.all_to_all(value_heads, "seq", split_axis=1, concat_axis=0, tiled=True),
        lax.all_to_all(split_heads(grad_att), "seq", split_axis=1, concat_axis=0, tiled=True),
    )
    attended, grad_query, grad_key, grad_value = block_attention(
        head_q, head_k, head_v, head_g, key_blocks[0], block_counts[0]
    )
    node_att, node_gq, node_gk, node_gv = (
        lax.all_to_all(attended, "seq", split_axis=0, concat_axis=1, tiled=True),
        lax.all_to_all(grad_query, "seq", split_axis=0, concat_axis=1, tiled=True),
        lax.all_to_all(grad_key, "seq", split_axis=0, concat_axis=1, tiled=True),
        lax.all_to_all(grad_value, "seq", split_axis=0, concat_axis=1, tiled=True),
    )
    att_nodes = node_att.reshape(local_rows, width)
    mixed = jnp.dot(att_nodes, w_out, preferred_element_type=jnp.float32).astype(jnp.bfloat16)
    factor = 1.0 / math.sqrt(lax.axis_size("dp") * lax.axis_size("seq") * local_rows)
    summed = lax.psum_scatter(
        inner_rows(att_nodes, up_rows), "seq", scatter_dimension=0, tiled=True
    )
    grad_wo = lax.psum_scatter(summed, "dp", scatter_dimension=1, tiled=True)
    full_shape = (1, local_rows, width)
    return (
        mixed.reshape(full_shape),
        node_gq.reshape(full_shape),
        node_gk.reshape(full_shape),
        node_gv.reshape(full_shape),
        grad_wo * factor,
    )


MESH = pl.DeviceIdType.MESH
LANES = 128
MASKED = -1e30


def dot_nt(left, right):
    return lax.dot_general(
        left, right, (((1,), (1,)), ((), ())), preferred_element_type=jnp.float32
    )


def fused(
    peers, levels, head_width, factor, list_ref, count_ref, q_ref, k_ref, v_ref, u_ref, w_ref,
    mixed_ref, gq_ref, gk_ref, gv_ref, gw_ref,
    head_q, head_g, keys2, values2, g_local, out_stage, key_sum, value_sum, att_nodes,
    gw_other, gw_own, gw_core, gw_level, gw_levels, gw_seq, gw_seqs,
    send_in, recv_in, send_out, recv_out, own_sem,
    send_core, recv_core, send_level, recv_level, send_seq, recv_seq,
):
    me = lax.axis_index("seq")
    replica = lax.axis_index("dp")
    core = lax.rem(replica, 2)
    level = replica // 2
    rows = q_ref.shape[0]
    chunks = head_q.shape[0]
    nodes = head_q.shape[1]
    blocks, listed = list_ref.shape
    block_rows = nodes // blocks
    per_device = blocks // peers
    span = chunks * LANES
    score_scale = 1.0 / math.sqrt(head_width)
    bf16, f32 = jnp.bfloat16, jnp.float32

    barrier = pltpu.get_barrier_semaphore()
    for p in range(1, peers):
        pl.semaphore_signal(
            barrier, inc=1, device_id={"seq": lax.rem(me + p, peers)}, device_id_type=MESH
        )
    other_core = level * 2 + 1 - core

    def level_at(p):
        return lax.rem(level + p, levels)

    pl.semaphore_signal(barrier, inc=1, device_id={"dp": other_core}, device_id_type=MESH)
    for p in range(1, levels):
        pl.semaphore_signal(
            barrier, inc=1, device_id={"dp": level_at(p) * 2 + core}, device_id_type=MESH
        )
    pl.semaphore_wait(barrier, peers + levels - 1)

    own_rows = pl.ds(pl.multiple_of(me * rows, rows), rows)

    def columns(device, c):
        return pl.ds(pl.multiple_of(device * span + c * LANES, LANES), LANES)

    sources = (q_ref, k_ref, v_ref, g_local)
    targets = (head_q, keys2, values2, head_g)

    def landing(a, c):
        if a in (1, 2):
            return targets[a].at[c, own_rows, pl.ds(0, LANES)]
        return targets[a].at[c, own_rows]

    def inward(a, c, p):
        device = lax.rem(me + p, peers)
        return pltpu.make_async_remote_copy(
            src_ref=sources[a].at[:, columns(device, c)],
            dst_ref=landing(a, c),
            send_sem=send_in.at[c, a, p - 1],
            recv_sem=recv_in.at[c, a, p - 1],
            device_id={"seq": device},
            device_id_type=MESH,
        )

    def own_copy(a, c):
        return pltpu.make_async_copy(
            sources[a].at[:, columns(me, c)], landing(a, c), own_sem.at[c, a]
        )

    def start_in(a, c):
        for p in range(1, peers):
            inward(a, c, p).start()
        own_copy(a, c).start()

    def finish_in(a, c):
        for p in range(1, peers):
            inward(a, c, p).wait()
        own_copy(a, c).wait()

    returns = (att_nodes, gq_ref, gk_ref, gv_ref)

    def outward(a, c, p):
        device = lax.rem(me + p, peers)
        return pltpu.make_async_remote_copy(
            src_ref=out_stage.at[c, a, pl.ds(pl.multiple_of(device * rows, rows), rows)],
            dst_ref=returns[a].at[:, columns(me, c)],
            send_sem=send_out.at[c, a, p - 1],
            recv_sem=recv_out.at[c, a, p - 1],
            device_id={"seq": device},
            device_id_type=MESH,
        )

    def keep_own(a, c):
        returns[a][:, columns(me, c)] = out_stage[c, a, own_rows, :]

    def grad_att(c):
        def one(device, carry):
            cols = columns(device, c)
            g_local[:, cols] = dot_nt(u_ref[...], w_ref[cols, :]).astype(bf16)
            return carry

        lax.fori_loop(0, peers, one, 0)

    lane = lax.broadcasted_iota(jnp.int32, (block_rows, LANES), 1)
    lane2 = lax.broadcasted_iota(jnp.int32, (2 * block_rows, LANES), 1)
    first = lane < head_width

    def stacked(x):
        return jnp.concatenate([jnp.where(first, x, 0.0), jnp.where(first, 0.0, x)], axis=0)

    def merged(x):
        return jnp.where(first, x[:block_rows], x[block_rows:])

    def core_copy(c):
        return pltpu.make_async_remote_copy(
            src_ref=gw_other.at[c], dst_ref=gw_core.at[c],
            send_sem=send_core.at[c], recv_sem=recv_core.at[c],
            device_id={"dp": other_core}, device_id_type=MESH,
        )

    def level_copy(c, p):
        return pltpu.make_async_remote_copy(
            src_ref=gw_level.at[c, level_at(p)], dst_ref=gw_levels.at[c, p - 1],
            send_sem=send_level.at[c, p - 1], recv_sem=recv_level.at[c, p - 1],
            device_id={"dp": level_at(p) * 2 + core}, device_id_type=MESH,
        )

    def seq_copy(c, p):
        device = lax.rem(me + p, peers)
        return pltpu.make_async_remote_copy(
            src_ref=gw_seq.at[c, pl.ds(pl.multiple_of(device * LANES, LANES), LANES)],
            dst_ref=gw_seqs.at[c, p - 1],
            send_sem=send_seq.at[c, p - 1], recv_sem=recv_seq.at[c, p - 1],
            device_id={"seq": device}, device_id_type=MESH,
        )

    def gw_partial(c):
        for p in range(1, peers):
            outward(0, c, p).wait()

        def up_columns(which):
            return jnp.concatenate(
                [
                    u_ref[:, pl.ds(pl.multiple_of((at * 2 + which) * LANES, LANES), LANES)]
                    for at in range(levels)
                ],
                axis=1,
            )

        def one(device, carry):
            place = pl.ds(pl.multiple_of(device * LANES, LANES), LANES)
            att = att_nodes[:, columns(device, c)]
            theirs = inner_rows(att, up_columns(1 - core)).astype(bf16)
            ours = inner_rows(att, up_columns(core))
            for at in range(levels):
                cut = slice(at * LANES, (at + 1) * LANES)
                gw_other[c, at, place, :] = theirs[:, cut]
                gw_own[c, at, place, :] = ours[:, cut]
            return carry

        lax.fori_loop(0, peers, one, 0)
        core_copy(c).start()

    def gw_across_levels(c):
        core_copy(c).wait()

        def one(at, carry):
            total = gw_own[c, at] + gw_core[c, at].astype(f32)
            gw_own[c, at] = total
            gw_level[c, at] = total.astype(bf16)
            return carry

        lax.fori_loop(0, levels, one, 0)
        for p in range(1, levels):
            level_copy(c, p).start()

    def gw_across_seq(c):
        total = gw_own[c, level]
        for p in range(1, levels):
            level_copy(c, p).wait()
            total = total + gw_levels[c, p - 1].astype(f32)
        gw_own[c, level] = total
        gw_seq[c] = total.astype(bf16)
        for p in range(1, peers):
            seq_copy(c, p).start()

    def gw_finish(c):
        total = gw_own[c, level, pl.ds(pl.multiple_of(me * LANES, LANES), LANES), :]
        for p in range(1, peers):
            seq_copy(c, p).wait()
            total = total + gw_seqs[c, p - 1].astype(f32)
        gw_ref[c * LANES:(c + 1) * LANES, :] = total * factor

    def attend(c, between):
        key_sum[...] = jnp.zeros_like(key_sum)
        value_sum[...] = jnp.zeros_like(value_sum)

        def one_block(i, carry):
            p = i // per_device + 1
            b = lax.rem(me + p, peers) * per_device + lax.rem(i, per_device)
            here = pl.ds(pl.multiple_of(b * block_rows, block_rows), block_rows)
            q = head_q[c, here, :].astype(f32) * score_scale
            g = head_g[c, here, :].astype(f32)
            count = count_ref[b]
            used = lane2 < 0
            for j in range(listed):
                used = used | (lane2 == jnp.where(j < count, list_ref[b, j], -1))
            q_pair = stacked(q)
            g_pair = stacked(g)
            left = jnp.concatenate([q_pair, jnp.where(used, 0.0, MASKED)], axis=1).astype(bf16)
            scores = dot_nt(left, keys2[c])
            raised = jnp.exp(scores - jnp.max(scores, axis=1, keepdims=True))
            weights = raised.astype(bf16)
            summed = jnp.dot(weights, values2[c], preferred_element_type=f32)
            inverse = 1.0 / summed[:, LANES:LANES + 1]
            attended = merged(summed[:, :LANES] * inverse).astype(bf16)
            delta = jnp.sum(
                g_pair * jnp.concatenate([attended, attended], axis=0).astype(f32),
                axis=1, keepdims=True,
            )
            high = delta.astype(bf16).astype(f32)
            middle = (delta - high).astype(bf16).astype(f32)
            low = delta - high - middle
            shift = jnp.where(
                lane2 == 0, -high, jnp.where(lane2 == 1, -middle, jnp.where(lane2 == 2, -low, 0.0))
            )
            right = jnp.concatenate([g_pair, shift], axis=1).astype(bf16)
            shifted = dot_nt(right, values2[c])
            logits = (raised * shifted).astype(bf16)
            grad_q = jnp.dot(logits, keys2[c, :, :LANES], preferred_element_type=f32)
            grad_q = merged(grad_q * (inverse * score_scale))
            key_sum[...] += inner_rows((q_pair * inverse).astype(bf16), logits)
            value_sum[...] += inner_rows((g_pair * inverse).astype(bf16), weights)
            out_stage[c, 0, here, :] = attended
            out_stage[c, 1, here, :] = grad_q.astype(bf16)

            @pl.when((lax.rem(i, per_device) == per_device - 1) & (p < peers))
            def _():
                outward(0, c, p).start()
                outward(1, c, p).start()

            for at, step in between:
                pl.when(i == at)(step)
            return carry

        lax.fori_loop(0, blocks, one_block, 0)
        out_stage[c, 2] = key_sum[...].T.astype(bf16)
        out_stage[c, 3] = value_sum[...].T.astype(bf16)
        for p in range(1, peers):
            outward(2, c, p).start()
            outward(3, c, p).start()
        for a in range(4):
            keep_own(a, c)

    for a in range(3):
        start_in(a, 0)
    grad_att(0)
    start_in(3, 0)
    for c in range(1, chunks):
        grad_att(c)
    block_of = lax.broadcasted_iota(jnp.int32, (nodes, LANES), 0) // block_rows
    node_lane = lax.broadcasted_iota(jnp.int32, (nodes, LANES), 1)
    for c in range(chunks):
        keys2[c, :, LANES:] = jnp.where(node_lane == block_of, 1.0, 0.0).astype(bf16)
        values2[c, :, LANES:] = jnp.where(node_lane < 3, 1.0, 0.0).astype(bf16)
    for c in range(chunks):
        for a in range(4):
            if a == 3 and c + 1 < chunks:
                for later in range(4):
                    start_in(later, c + 1)
            finish_in(a, c)
        between = []
        if c > 0:
            between = [
                (blocks // 4, functools.partial(gw_partial, c - 1)),
                (blocks // 2, functools.partial(gw_across_levels, c - 1)),
                (blocks - 2, functools.partial(gw_across_seq, c - 1)),
            ]
        attend(c, between)
        if c > 0:
            gw_finish(c - 1)
    gw_partial(chunks - 1)
    mixed_ref[...] = jnp.dot(att_nodes[...], w_ref[...], preferred_element_type=f32).astype(bf16)
    gw_across_levels(chunks - 1)
    for c in range(chunks):
        for a in range(1, 4):
            for p in range(1, peers):
                outward(a, c, p).wait()
    gw_across_seq(chunks - 1)
    gw_finish(chunks - 1)


def local_fused(queries, keys, values, upstream, w_out, key_blocks, block_counts):
    rows, width = queries.shape[1:]
    peers = lax.axis_size("seq")
    chunks = width // peers // LANES
    nodes = rows * peers
    bf16, f32 = jnp.bfloat16, jnp.float32
    replicas = lax.axis_size("dp")
    levels = replicas // 2
    factor = 1.0 / math.sqrt(replicas * nodes)
    vmem = pl.BlockSpec(memory_space=pltpu.VMEM)
    smem = pl.BlockSpec(memory_space=pltpu.SMEM)
    part = jax.ShapeDtypeStruct((rows, width), bf16)
    mixed, grad_q, grad_k, grad_v, grad_wo = pl.pallas_call(
        functools.partial(fused, peers, levels, width // HEADS, factor),
        out_shape=(part, part, part, part, jax.ShapeDtypeStruct((chunks * LANES, width // replicas), f32)),
        in_specs=[smem, smem] + [vmem] * 5,
        out_specs=[vmem] * 5,
        scratch_shapes=[
            pltpu.VMEM((chunks, nodes, LANES), bf16),
            pltpu.VMEM((chunks, nodes, LANES), bf16),
            pltpu.VMEM((chunks, nodes, 2 * LANES), bf16),
            pltpu.VMEM((chunks, nodes, 2 * LANES), bf16),
            pltpu.VMEM((rows, width), bf16),
            pltpu.VMEM((chunks, 4, nodes, LANES), bf16),
            pltpu.VMEM((LANES, nodes), f32),
            pltpu.VMEM((LANES, nodes), f32),
            pltpu.VMEM((rows, width), bf16),
            pltpu.VMEM((chunks, levels, peers * LANES, LANES), bf16),
            pltpu.VMEM((chunks, levels, peers * LANES, LANES), f32),
            pltpu.VMEM((chunks, levels, peers * LANES, LANES), bf16),
            pltpu.VMEM((chunks, levels, peers * LANES, LANES), bf16),
            pltpu.VMEM((chunks, levels - 1, peers * LANES, LANES), bf16),
            pltpu.VMEM((chunks, peers * LANES, LANES), bf16),
            pltpu.VMEM((chunks, peers - 1, LANES, LANES), bf16),
            pltpu.SemaphoreType.DMA((chunks, 4, peers - 1)),
            pltpu.SemaphoreType.DMA((chunks, 4, peers - 1)),
            pltpu.SemaphoreType.DMA((chunks, 4, peers - 1)),
            pltpu.SemaphoreType.DMA((chunks, 4, peers - 1)),
            pltpu.SemaphoreType.DMA((chunks, 4)),
            pltpu.SemaphoreType.DMA((chunks,)),
            pltpu.SemaphoreType.DMA((chunks,)),
            pltpu.SemaphoreType.DMA((chunks, levels - 1)),
            pltpu.SemaphoreType.DMA((chunks, levels - 1)),
            pltpu.SemaphoreType.DMA((chunks, peers - 1)),
            pltpu.SemaphoreType.DMA((chunks, peers - 1)),
        ],
        compiler_params=pltpu.CompilerParams(
            collective_id=0, has_side_effects=True, vmem_limit_bytes=56 * 1024 * 1024
        ),
        name="graph_attention",
    )(key_blocks[0], block_counts[0], queries[0], keys[0], values[0], upstream[0], w_out)
    return mixed[None], grad_q[None], grad_k[None], grad_v[None], grad_wo


def local(queries, keys, values, upstream, w_out, key_blocks, block_counts):
    width = queries.shape[2]
    peers = lax.axis_size("seq")
    pair = 2 * (width // HEADS) == LANES and width % (peers * LANES) == 0
    whole_blocks = key_blocks.shape[1] % peers == 0 and key_blocks.shape[1] <= LANES
    columns_fit = lax.axis_size("dp") * LANES == width
    chosen = local_fused if pair and whole_blocks and columns_fit else local_plain
    return chosen(queries, keys, values, upstream, w_out, key_blocks, block_counts)


def solution(mesh):
    placed = (
        P("dp", "seq", None),
        P("dp", "seq", None),
        P("dp", "seq", None),
        P("dp", "seq", None),
        P(),
        P("dp", None, None),
        P("dp", None),
    )
    return jax.shard_map(
        local,
        mesh=mesh,
        in_specs=placed,
        out_specs=(
            P("dp", "seq", None),
            P("dp", "seq", None),
            P("dp", "seq", None),
            P("dp", "seq", None),
            P("seq", "dp"),
        ),
        check_vma=False,
    )
```

```python
import functools
import math

import jax
import jax.numpy as jnp
from jax import lax
from jax.experimental import pallas as pl
from jax.experimental.pallas import tpu as pltpu
from jax.sharding import PartitionSpec as P

HEADS = 16


blocks_per_step = 4


def product(form, left, right):
    return jnp.einsum(form, left, right, preferred_element_type=jnp.float32)


def inner_rows(left, right):
    return lax.dot_general(
        left, right, (((0,), (0,)), ((), ())), preferred_element_type=jnp.float32
    )


def block_attention(head_q, head_k, head_v, head_g, key_lists, key_counts):
    node_count, head_count, head_width = head_q.shape
    block_count, listed = key_lists.shape
    block_rows = node_count // block_count
    steps_count = block_count // blocks_per_step
    score_scale = 1.0 / math.sqrt(head_width)
    query_groups = head_q.reshape(steps_count, blocks_per_step, block_rows, head_count, head_width)
    grad_groups = head_g.reshape(steps_count, blocks_per_step, block_rows, head_count, head_width)
    key_table = head_k.reshape(block_count, block_rows, head_count, head_width)
    value_table = head_v.reshape(block_count, block_rows, head_count, head_width)
    list_groups = key_lists.reshape(steps_count, blocks_per_step, listed)
    count_groups = key_counts.reshape(steps_count, blocks_per_step)
    slot_index = jnp.arange(listed, dtype=jnp.int32)

    def one_step(accumulated, inputs):
        key_acc, value_acc = accumulated
        query_part, grad_part, list_part, count_part = inputs
        keys_near = key_table[list_part]
        values_near = value_table[list_part]
        scores = product("gqnd,gjknd->gnqjk", query_part, keys_near) * score_scale
        usable = (slot_index[None, :] < count_part[:, None])[:, None, None, :, None]
        scores = jnp.where(usable, scores, -jnp.inf)
        highest = jnp.max(scores, axis=(3, 4), keepdims=True)
        raised = jnp.exp(scores - highest)
        probability = raised / jnp.sum(raised, axis=(3, 4), keepdims=True)
        weights = probability.astype(jnp.bfloat16)
        attended = product("gnqjk,gjknd->gqnd", weights, values_near).astype(jnp.bfloat16)
        row_delta = jnp.sum(grad_part.astype(jnp.float32) * attended.astype(jnp.float32), axis=3)
        grad_scores = product("gqnd,gjknd->gnqjk", grad_part, values_near)
        shifted = grad_scores - jnp.transpose(row_delta, (0, 2, 1))[:, :, :, None, None]
        grad_logits = (probability * shifted).astype(jnp.bfloat16)
        grad_query = (product("gnqjk,gjknd->gqnd", grad_logits, keys_near) * score_scale).astype(
            jnp.bfloat16
        )
        key_terms = product("gnqjk,gqnd->gjknd", grad_logits, query_part) * score_scale
        value_terms = product("gnqjk,gqnd->gjknd", weights, grad_part)
        flat_list = list_part.reshape(-1)
        key_acc = key_acc.at[flat_list].add(
            key_terms.reshape(-1, block_rows, head_count, head_width)
        )
        value_acc = value_acc.at[flat_list].add(
            value_terms.reshape(-1, block_rows, head_count, head_width)
        )
        return ((key_acc, value_acc), (attended, grad_query))

    empty = jnp.zeros((block_count, block_rows, head_count, head_width), jnp.float32)
    (key_acc, value_acc), (attended, grad_query) = lax.scan(
        one_step, (empty, empty), (query_groups, grad_groups, list_groups, count_groups)
    )
    shape = (node_count, head_count, head_width)
    return (
        attended.reshape(shape),
        grad_query.reshape(shape),
        key_acc.astype(jnp.bfloat16).reshape(shape),
        value_acc.astype(jnp.bfloat16).reshape(shape),
    )


def project_back(up_rows, w_out):
    return lax.dot_general(
        up_rows, w_out, (((1,), (1,)), ((), ())), preferred_element_type=jnp.float32
    ).astype(jnp.bfloat16)


def local_plain(queries, keys, values, upstream, w_out, key_blocks, block_counts):
    local_rows = queries.shape[1]
    width = queries.shape[2]
    head_width = width // HEADS
    up_rows = upstream[0]

    def split_heads(array):
        return array.reshape(local_rows, HEADS, head_width)

    query_heads = split_heads(queries[0])
    key_heads = split_heads(keys[0])
    value_heads = split_heads(values[0])
    grad_att = project_back(up_rows, w_out)
    head_q, head_k, head_v, head_g = (
        lax.all_to_all(query_heads, "seq", split_axis=1, concat_axis=0, tiled=True),
        lax.all_to_all(key_heads, "seq", split_axis=1, concat_axis=0, tiled=True),
        lax.all_to_all(value_heads, "seq", split_axis=1, concat_axis=0, tiled=True),
        lax.all_to_all(split_heads(grad_att), "seq", split_axis=1, concat_axis=0, tiled=True),
    )
    attended, grad_query, grad_key, grad_value = block_attention(
        head_q, head_k, head_v, head_g, key_blocks[0], block_counts[0]
    )
    node_att, node_gq, node_gk, node_gv = (
        lax.all_to_all(attended, "seq", split_axis=0, concat_axis=1, tiled=True),
        lax.all_to_all(grad_query, "seq", split_axis=0, concat_axis=1, tiled=True),
        lax.all_to_all(grad_key, "seq", split_axis=0, concat_axis=1, tiled=True),
        lax.all_to_all(grad_value, "seq", split_axis=0, concat_axis=1, tiled=True),
    )
    att_nodes = node_att.reshape(local_rows, width)
    mixed = jnp.dot(att_nodes, w_out, preferred_element_type=jnp.float32).astype(jnp.bfloat16)
    factor = 1.0 / math.sqrt(lax.axis_size("dp") * lax.axis_size("seq") * local_rows)
    summed = lax.psum_scatter(
        inner_rows(att_nodes, up_rows), "seq", scatter_dimension=0, tiled=True
    )
    grad_wo = lax.psum_scatter(summed, "dp", scatter_dimension=1, tiled=True)
    full_shape = (1, local_rows, width)
    return (
        mixed.reshape(full_shape),
        node_gq.reshape(full_shape),
        node_gk.reshape(full_shape),
        node_gv.reshape(full_shape),
        grad_wo * factor,
    )


MESH = pl.DeviceIdType.MESH
LANES = 128
MASKED = -1e30


def dot_nt(left, right):
    return lax.dot_general(
        left, right, (((1,), (1,)), ((), ())), preferred_element_type=jnp.float32
    )


def fused(
    peers, levels, head_width, factor, list_ref, count_ref, q_ref, k_ref, v_ref, u_ref, w_ref,
    mixed_ref, gq_ref, gk_ref, gv_ref, gw_ref,
    head_q, head_g, keys2, values2, g_local, out_stage, key_sum, value_sum, att_nodes,
    kept_weights, kept_inverse, kept_logits,
    gw_other, gw_own, gw_core, gw_level, gw_levels, gw_seq, gw_seqs,
    send_in, recv_in, send_out, recv_out, own_sem,
    send_core, recv_core, send_level, recv_level, send_seq, recv_seq,
):
    me = lax.axis_index("seq")
    replica = lax.axis_index("dp")
    core = lax.rem(replica, 2)
    level = replica // 2
    rows = q_ref.shape[0]
    chunks = head_q.shape[0]
    nodes = head_q.shape[1]
    blocks, listed = list_ref.shape
    block_rows = nodes // blocks
    per_device = blocks // peers
    span = chunks * LANES
    score_scale = 1.0 / math.sqrt(head_width)
    bf16, f32 = jnp.bfloat16, jnp.float32

    barrier = pltpu.get_barrier_semaphore()
    for p in range(1, peers):
        pl.semaphore_signal(
            barrier, inc=1, device_id={"seq": lax.rem(me + p, peers)}, device_id_type=MESH
        )
    other_core = level * 2 + 1 - core

    def level_at(p):
        return lax.rem(level + p, levels)

    pl.semaphore_signal(barrier, inc=1, device_id={"dp": other_core}, device_id_type=MESH)
    for p in range(1, levels):
        pl.semaphore_signal(
            barrier, inc=1, device_id={"dp": level_at(p) * 2 + core}, device_id_type=MESH
        )
    pl.semaphore_wait(barrier, peers + levels - 1)

    own_rows = pl.ds(pl.multiple_of(me * rows, rows), rows)

    def columns(device, c):
        return pl.ds(pl.multiple_of(device * span + c * LANES, LANES), LANES)

    sources = (q_ref, k_ref, v_ref, g_local)
    targets = (head_q, keys2, values2, head_g)

    def landing(a, c):
        if a in (1, 2):
            return targets[a][c].at[pl.ds(me * per_device, per_device), :, pl.ds(0, LANES)]
        return targets[a].at[c, own_rows]

    def leaving(a, device, c):
        if a in (1, 2):
            return sources[a].at[:, :, columns(device, c)]
        return sources[a].at[:, columns(device, c)]

    def inward(a, c, p):
        device = lax.rem(me + p, peers)
        return pltpu.make_async_remote_copy(
            src_ref=leaving(a, device, c),
            dst_ref=landing(a, c),
            send_sem=send_in.at[c, a, p - 1],
            recv_sem=recv_in.at[c, a, p - 1],
            device_id={"seq": device},
            device_id_type=MESH,
        )

    def own_copy(a, c):
        return pltpu.make_async_copy(
            leaving(a, me, c), landing(a, c), own_sem.at[c, a]
        )

    def start_in(a, c):
        for p in range(1, peers):
            inward(a, c, p).start()
        own_copy(a, c).start()

    def finish_in(a, c):
        for p in range(1, peers):
            inward(a, c, p).wait()
        own_copy(a, c).wait()

    returns = (att_nodes, gq_ref, gk_ref, gv_ref)

    def outward(a, c, p):
        device = lax.rem(me + p, peers)
        return pltpu.make_async_remote_copy(
            src_ref=out_stage.at[c, a, pl.ds(pl.multiple_of(device * rows, rows), rows)],
            dst_ref=returns[a].at[:, columns(me, c)],
            send_sem=send_out.at[c, a, p - 1],
            recv_sem=recv_out.at[c, a, p - 1],
            device_id={"seq": device},
            device_id_type=MESH,
        )

    def keep_own(a, c):
        returns[a][:, columns(me, c)] = out_stage[c, a, own_rows, :]

    def grad_att(c):
        def one(device, carry):
            cols = columns(device, c)
            g_local[:, cols] = dot_nt(u_ref[...], w_ref[cols, :]).astype(bf16)
            return carry

        lax.fori_loop(0, peers, one, 0)

    lane = lax.broadcasted_iota(jnp.int32, (block_rows, LANES), 1)
    lane2 = lax.broadcasted_iota(jnp.int32, (2 * block_rows, LANES), 1)
    first = lane < head_width

    def stacked(x):
        return jnp.concatenate([jnp.where(first, x, 0.0), jnp.where(first, 0.0, x)], axis=0)

    def merged(x):
        return jnp.where(first, x[:block_rows], x[block_rows:])

    def core_copy(c):
        return pltpu.make_async_remote_copy(
            src_ref=gw_other.at[c], dst_ref=gw_core.at[c],
            send_sem=send_core.at[c], recv_sem=recv_core.at[c],
            device_id={"dp": other_core}, device_id_type=MESH,
        )

    def level_copy(c, p):
        return pltpu.make_async_remote_copy(
            src_ref=gw_level.at[c, level_at(p)], dst_ref=gw_levels.at[c, p - 1],
            send_sem=send_level.at[c, p - 1], recv_sem=recv_level.at[c, p - 1],
            device_id={"dp": level_at(p) * 2 + core}, device_id_type=MESH,
        )

    def seq_copy(c, p):
        device = lax.rem(me + p, peers)
        return pltpu.make_async_remote_copy(
            src_ref=gw_seq.at[c, pl.ds(pl.multiple_of(device * LANES, LANES), LANES)],
            dst_ref=gw_seqs.at[c, p - 1],
            send_sem=send_seq.at[c, p - 1], recv_sem=recv_seq.at[c, p - 1],
            device_id={"seq": device}, device_id_type=MESH,
        )

    def gw_partial(c):
        for p in range(1, peers):
            outward(0, c, p).wait()

        def up_columns(which):
            return jnp.concatenate(
                [
                    u_ref[:, pl.ds(pl.multiple_of((at * 2 + which) * LANES, LANES), LANES)]
                    for at in range(levels)
                ],
                axis=1,
            )

        def one(device, carry):
            place = pl.ds(pl.multiple_of(device * LANES, LANES), LANES)
            att = att_nodes[:, columns(device, c)]
            theirs = inner_rows(att, up_columns(1 - core)).astype(bf16)
            ours = inner_rows(att, up_columns(core))
            for at in range(levels):
                cut = slice(at * LANES, (at + 1) * LANES)
                gw_other[c, at, place, :] = theirs[:, cut]
                gw_own[c, at, place, :] = ours[:, cut]
            return carry

        lax.fori_loop(0, peers, one, 0)
        core_copy(c).start()

    def gw_across_levels(c):
        core_copy(c).wait()

        def one(at, carry):
            total = gw_own[c, at] + gw_core[c, at].astype(f32)
            gw_own[c, at] = total
            gw_level[c, at] = total.astype(bf16)
            return carry

        lax.fori_loop(0, levels, one, 0)
        for p in range(1, levels):
            level_copy(c, p).start()

    def gw_across_seq(c):
        total = gw_own[c, level]
        for p in range(1, levels):
            level_copy(c, p).wait()
            total = total + gw_levels[c, p - 1].astype(f32)
        gw_own[c, level] = total
        gw_seq[c] = total.astype(bf16)
        for p in range(1, peers):
            seq_copy(c, p).start()

    def gw_finish(c):
        total = gw_own[c, level, pl.ds(pl.multiple_of(me * LANES, LANES), LANES), :]
        for p in range(1, peers):
            seq_copy(c, p).wait()
            total = total + gw_seqs[c, p - 1].astype(f32)
        gw_ref[c * LANES:(c + 1) * LANES, :] = total * factor

    def dest_blocks(p):
        device = lax.rem(me + p, peers)
        return [device * per_device + at for at in range(per_device)]

    def rows_of(b):
        return pl.ds(pl.multiple_of(b * block_rows, block_rows), block_rows)

    def listed_rows(table, b):
        return jnp.concatenate([table[list_ref[b, j]] for j in range(listed)], axis=0)

    def run_between(p, between):
        for at, step in between:
            pl.when(p == at)(step)

    def forward(c):
        def one_group(step, carry):
            p = step + 1
            group = dest_blocks(p)
            lefts = []
            for b in group:
                q = head_q[c, rows_of(b), :].astype(f32) * score_scale
                count = count_ref[b]
                used = lane2 < 0
                for j in range(listed):
                    used = used | (lane2 == jnp.where(j < count, list_ref[b, j], -1))
                bias = jnp.where(used, 0.0, MASKED)
                lefts.append(jnp.concatenate([stacked(q), bias], axis=1).astype(bf16))
            scores = [dot_nt(left, listed_rows(keys2[c], b)) for left, b in zip(lefts, group)]
            tops = [jnp.max(score, axis=1, keepdims=True) for score in scores]
            weights = [jnp.exp(score - top).astype(bf16) for score, top in zip(scores, tops)]
            sums = [
                jnp.dot(weight, listed_rows(values2[c], b), preferred_element_type=f32)
                for weight, b in zip(weights, group)
            ]
            for b, weight, summed in zip(group, weights, sums):
                for j in range(listed):
                    kept_weights[c, b, j] = weight[:, j * block_rows:(j + 1) * block_rows]
                inverse = 1.0 / summed[:, LANES:LANES + 1]
                kept_inverse[c, b] = jnp.broadcast_to(inverse, (2 * block_rows, LANES))
                out_stage[c, 0, rows_of(b), :] = merged(summed[:, :LANES] * inverse).astype(bf16)

            @pl.when(p < peers)
            def _():
                outward(0, c, p).start()

            return carry

        lax.fori_loop(0, peers, one_group, 0)
        keep_own(0, c)

    def backward(c, between):
        key_sum[...] = jnp.zeros_like(key_sum)
        value_sum[...] = jnp.zeros_like(value_sum)

        def one_group(step, carry):
            p = step + 1
            group = dest_blocks(p)
            q_sides, g_sides, rights = [], [], []
            for b in group:
                inverse = kept_inverse[c, b]
                q_pair = stacked(head_q[c, rows_of(b), :].astype(f32) * score_scale)
                g_pair = stacked(head_g[c, rows_of(b), :].astype(f32))
                attended = out_stage[c, 0, rows_of(b), :].astype(f32)
                delta = jnp.sum(
                    g_pair * jnp.concatenate([attended, attended], axis=0), axis=1, keepdims=True
                )
                high = delta.astype(bf16).astype(f32)
                middle = (delta - high).astype(bf16).astype(f32)
                low = delta - high - middle
                shift = jnp.where(
                    lane2 == 0, -high,
                    jnp.where(lane2 == 1, -middle, jnp.where(lane2 == 2, -low, 0.0)),
                )
                q_sides.append((q_pair * inverse).astype(bf16))
                g_sides.append((g_pair * inverse).astype(bf16))
                rights.append(jnp.concatenate([g_pair, shift], axis=1).astype(bf16))
            shifted = [dot_nt(right, listed_rows(values2[c], b)) for right, b in zip(rights, group)]
            for at, b in enumerate(group):
                for j in range(listed):
                    cut = slice(j * block_rows, (j + 1) * block_rows)
                    kept_logits[at, j] = (
                        kept_weights[c, b, j].astype(f32) * shifted[at][:, cut]
                    ).astype(bf16)
            wide_logits, wide_weights = [], []
            for at, b in enumerate(group):
                logits = jnp.concatenate([kept_logits[at, j] for j in range(listed)], axis=1)
                grad_q = jnp.dot(
                    logits, listed_rows(keys2[c], b)[:, :LANES],
                    preferred_element_type=f32,
                )
                grad_q = merged(grad_q * (kept_inverse[c, b] * score_scale))
                out_stage[c, 1, rows_of(b), :] = grad_q.astype(bf16)
                slots = []
                for key_block in range(blocks):
                    slot = jnp.int32(listed)
                    for j in range(listed):
                        slot = jnp.where(list_ref[b, j] == key_block, j, slot)
                    slots.append(slot)
                wide_logits.append(jnp.concatenate([kept_logits[at, i] for i in slots], axis=1))
                wide_weights.append(jnp.concatenate([kept_weights[c, b, i] for i in slots], axis=1))
            key_sum[...] += inner_rows(
                jnp.concatenate(q_sides, axis=0), jnp.concatenate(wide_logits, axis=0)
            )
            value_sum[...] += inner_rows(
                jnp.concatenate(g_sides, axis=0), jnp.concatenate(wide_weights, axis=0)
            )

            @pl.when(p < peers)
            def _():
                outward(1, c, p).start()

            run_between(p, between)
            return carry

        lax.fori_loop(0, peers, one_group, 0)
        out_stage[c, 2] = key_sum[...].T.astype(bf16)
        for p in range(1, peers):
            outward(2, c, p).start()
        out_stage[c, 3] = value_sum[...].T.astype(bf16)
        for p in range(1, peers):
            outward(3, c, p).start()
        for a in range(1, 4):
            keep_own(a, c)

    def project():
        mixed_ref[...] = jnp.dot(
            att_nodes[...], w_ref[...], preferred_element_type=f32
        ).astype(bf16)

    for a in range(3):
        start_in(a, 0)
    for c in range(chunks):
        grad_att(c)
    block_of = lax.broadcasted_iota(jnp.int32, (blocks, block_rows, LANES), 0)
    node_lane = lax.broadcasted_iota(jnp.int32, (blocks, block_rows, LANES), 2)
    for c in range(chunks):
        keys2[c][:, :, LANES:] = jnp.where(node_lane == block_of, 1.0, 0.0).astype(bf16)
        values2[c][:, :, LANES:] = jnp.where(node_lane < 3, 1.0, 0.0).astype(bf16)
    nothing = jnp.zeros((2 * block_rows, block_rows), bf16)
    for c in range(chunks):
        for b in range(blocks):
            kept_weights[c, b, listed] = nothing
    for at in range(per_device):
        kept_logits[at, listed] = nothing
    for c in range(chunks):
        for a in range(3):
            finish_in(a, c)
            if a == 1:
                if c + 1 < chunks:
                    for later in range(3):
                        start_in(later, c + 1)
                else:
                    for every in range(chunks):
                        start_in(3, every)
        forward(c)
    last = chunks - 1
    for c in range(chunks):
        finish_in(3, c)
        between = []
        if c == 0:
            between.append((1, functools.partial(gw_partial, 0)))
            between.append((2, functools.partial(gw_across_levels, 0)))
        if c > 0:
            between.append((1, functools.partial(gw_across_seq, c - 1)))
        if c + 1 < chunks:
            between.append((3, functools.partial(gw_partial, c + 1)))
            between.append((4, functools.partial(gw_across_levels, c + 1)))
        if c == last:
            between.append((2, project))
        backward(c, between)
    for c in range(chunks):
        for a in range(1, 4):
            for p in range(1, peers):
                outward(a, c, p).wait()
    gw_across_seq(last)
    for c in range(chunks):
        gw_finish(c)


def local_fused(queries, keys, values, upstream, w_out, key_blocks, block_counts):
    rows, width = queries.shape[1:]
    peers = lax.axis_size("seq")
    chunks = width // peers // LANES
    nodes = rows * peers
    bf16, f32 = jnp.bfloat16, jnp.float32
    replicas = lax.axis_size("dp")
    levels = replicas // 2
    blocks, listed = key_blocks.shape[1:]
    block_rows = nodes // blocks
    by_block = (blocks // peers, block_rows, width)
    factor = 1.0 / math.sqrt(replicas * nodes)
    vmem = pl.BlockSpec(memory_space=pltpu.VMEM)
    smem = pl.BlockSpec(memory_space=pltpu.SMEM)
    part = jax.ShapeDtypeStruct((rows, width), bf16)
    mixed, grad_q, grad_k, grad_v, grad_wo = pl.pallas_call(
        functools.partial(fused, peers, levels, width // HEADS, factor),
        out_shape=(part, part, part, part, jax.ShapeDtypeStruct((chunks * LANES, width // replicas), f32)),
        in_specs=[smem, smem] + [vmem] * 5,
        out_specs=[vmem] * 5,
        scratch_shapes=[
            pltpu.VMEM((chunks, nodes, LANES), bf16),
            pltpu.VMEM((chunks, nodes, LANES), bf16),
            tuple(pltpu.VMEM((blocks, block_rows, 2 * LANES), bf16) for _ in range(chunks)),
            tuple(pltpu.VMEM((blocks, block_rows, 2 * LANES), bf16) for _ in range(chunks)),
            pltpu.VMEM((rows, width), bf16),
            pltpu.VMEM((chunks, 4, nodes, LANES), bf16),
            pltpu.VMEM((LANES, nodes), f32),
            pltpu.VMEM((LANES, nodes), f32),
            pltpu.VMEM((rows, width), bf16),
            pltpu.VMEM((chunks, blocks, listed + 1, 2 * block_rows, block_rows), bf16),
            pltpu.VMEM((chunks, blocks, 2 * block_rows, LANES), f32),
            pltpu.VMEM((blocks // peers, listed + 1, 2 * block_rows, block_rows), bf16),
            pltpu.VMEM((chunks, levels, peers * LANES, LANES), bf16),
            pltpu.VMEM((chunks, levels, peers * LANES, LANES), f32),
            pltpu.VMEM((chunks, levels, peers * LANES, LANES), bf16),
            pltpu.VMEM((chunks, levels, peers * LANES, LANES), bf16),
            pltpu.VMEM((chunks, levels - 1, peers * LANES, LANES), bf16),
            pltpu.VMEM((chunks, peers * LANES, LANES), bf16),
            pltpu.VMEM((chunks, peers - 1, LANES, LANES), bf16),
            pltpu.SemaphoreType.DMA((chunks, 4, peers - 1)),
            pltpu.SemaphoreType.DMA((chunks, 4, peers - 1)),
            pltpu.SemaphoreType.DMA((chunks, 4, peers - 1)),
            pltpu.SemaphoreType.DMA((chunks, 4, peers - 1)),
            pltpu.SemaphoreType.DMA((chunks, 4)),
            pltpu.SemaphoreType.DMA((chunks,)),
            pltpu.SemaphoreType.DMA((chunks,)),
            pltpu.SemaphoreType.DMA((chunks, levels - 1)),
            pltpu.SemaphoreType.DMA((chunks, levels - 1)),
            pltpu.SemaphoreType.DMA((chunks, peers - 1)),
            pltpu.SemaphoreType.DMA((chunks, peers - 1)),
        ],
        compiler_params=pltpu.CompilerParams(
            collective_id=0, has_side_effects=True, vmem_limit_bytes=56 * 1024 * 1024
        ),
        name="graph_attention",
    )(
        key_blocks[0], block_counts[0], queries[0], keys.reshape(by_block),
        values.reshape(by_block), upstream[0], w_out,
    )
    return mixed[None], grad_q[None], grad_k[None], grad_v[None], grad_wo


def local(queries, keys, values, upstream, w_out, key_blocks, block_counts):
    width = queries.shape[2]
    peers = lax.axis_size("seq")
    pair = 2 * (width // HEADS) == LANES and width % (peers * LANES) == 0
    whole_blocks = key_blocks.shape[1] % peers == 0 and key_blocks.shape[1] <= LANES
    columns_fit = lax.axis_size("dp") * LANES == width
    chosen = local_fused if pair and whole_blocks and columns_fit else local_plain
    return chosen(queries, keys, values, upstream, w_out, key_blocks, block_counts)


def solution(mesh):
    placed = (
        P("dp", "seq", None),
        P("dp", "seq", None),
        P("dp", "seq", None),
        P("dp", "seq", None),
        P(),
        P("dp", None, None),
        P("dp", None),
    )
    return jax.shard_map(
        local,
        mesh=mesh,
        in_specs=placed,
        out_specs=(
            P("dp", "seq", None),
            P("dp", "seq", None),
            P("dp", "seq", None),
            P("dp", "seq", None),
            P("seq", "dp"),
        ),
        check_vma=False,
    )
```

```python
import functools
import math

import jax
import jax.numpy as jnp
from jax import lax
from jax.experimental import pallas as pl
from jax.experimental.pallas import tpu as pltpu
from jax.sharding import PartitionSpec as P

HEADS = 16


blocks_per_step = 4


def product(form, left, right):
    return jnp.einsum(form, left, right, preferred_element_type=jnp.float32)


def inner_rows(left, right):
    return lax.dot_general(
        left, right, (((0,), (0,)), ((), ())), preferred_element_type=jnp.float32
    )


def block_attention(head_q, head_k, head_v, head_g, key_lists, key_counts):
    node_count, head_count, head_width = head_q.shape
    block_count, listed = key_lists.shape
    block_rows = node_count // block_count
    steps_count = block_count // blocks_per_step
    score_scale = 1.0 / math.sqrt(head_width)
    query_groups = head_q.reshape(steps_count, blocks_per_step, block_rows, head_count, head_width)
    grad_groups = head_g.reshape(steps_count, blocks_per_step, block_rows, head_count, head_width)
    key_table = head_k.reshape(block_count, block_rows, head_count, head_width)
    value_table = head_v.reshape(block_count, block_rows, head_count, head_width)
    list_groups = key_lists.reshape(steps_count, blocks_per_step, listed)
    count_groups = key_counts.reshape(steps_count, blocks_per_step)
    slot_index = jnp.arange(listed, dtype=jnp.int32)

    def one_step(accumulated, inputs):
        key_acc, value_acc = accumulated
        query_part, grad_part, list_part, count_part = inputs
        keys_near = key_table[list_part]
        values_near = value_table[list_part]
        scores = product("gqnd,gjknd->gnqjk", query_part, keys_near) * score_scale
        usable = (slot_index[None, :] < count_part[:, None])[:, None, None, :, None]
        scores = jnp.where(usable, scores, -jnp.inf)
        highest = jnp.max(scores, axis=(3, 4), keepdims=True)
        raised = jnp.exp(scores - highest)
        probability = raised / jnp.sum(raised, axis=(3, 4), keepdims=True)
        weights = probability.astype(jnp.bfloat16)
        attended = product("gnqjk,gjknd->gqnd", weights, values_near).astype(jnp.bfloat16)
        row_delta = jnp.sum(grad_part.astype(jnp.float32) * attended.astype(jnp.float32), axis=3)
        grad_scores = product("gqnd,gjknd->gnqjk", grad_part, values_near)
        shifted = grad_scores - jnp.transpose(row_delta, (0, 2, 1))[:, :, :, None, None]
        grad_logits = (probability * shifted).astype(jnp.bfloat16)
        grad_query = (product("gnqjk,gjknd->gqnd", grad_logits, keys_near) * score_scale).astype(
            jnp.bfloat16
        )
        key_terms = product("gnqjk,gqnd->gjknd", grad_logits, query_part) * score_scale
        value_terms = product("gnqjk,gqnd->gjknd", weights, grad_part)
        flat_list = list_part.reshape(-1)
        key_acc = key_acc.at[flat_list].add(
            key_terms.reshape(-1, block_rows, head_count, head_width)
        )
        value_acc = value_acc.at[flat_list].add(
            value_terms.reshape(-1, block_rows, head_count, head_width)
        )
        return ((key_acc, value_acc), (attended, grad_query))

    empty = jnp.zeros((block_count, block_rows, head_count, head_width), jnp.float32)
    (key_acc, value_acc), (attended, grad_query) = lax.scan(
        one_step, (empty, empty), (query_groups, grad_groups, list_groups, count_groups)
    )
    shape = (node_count, head_count, head_width)
    return (
        attended.reshape(shape),
        grad_query.reshape(shape),
        key_acc.astype(jnp.bfloat16).reshape(shape),
        value_acc.astype(jnp.bfloat16).reshape(shape),
    )


def project_back(up_rows, w_out):
    return lax.dot_general(
        up_rows, w_out, (((1,), (1,)), ((), ())), preferred_element_type=jnp.float32
    ).astype(jnp.bfloat16)


def local_plain(queries, keys, values, upstream, w_out, key_blocks, block_counts):
    local_rows = queries.shape[1]
    width = queries.shape[2]
    head_width = width // HEADS
    up_rows = upstream[0]

    def split_heads(array):
        return array.reshape(local_rows, HEADS, head_width)

    query_heads = split_heads(queries[0])
    key_heads = split_heads(keys[0])
    value_heads = split_heads(values[0])
    grad_att = project_back(up_rows, w_out)
    head_q, head_k, head_v, head_g = (
        lax.all_to_all(query_heads, "seq", split_axis=1, concat_axis=0, tiled=True),
        lax.all_to_all(key_heads, "seq", split_axis=1, concat_axis=0, tiled=True),
        lax.all_to_all(value_heads, "seq", split_axis=1, concat_axis=0, tiled=True),
        lax.all_to_all(split_heads(grad_att), "seq", split_axis=1, concat_axis=0, tiled=True),
    )
    attended, grad_query, grad_key, grad_value = block_attention(
        head_q, head_k, head_v, head_g, key_blocks[0], block_counts[0]
    )
    node_att, node_gq, node_gk, node_gv = (
        lax.all_to_all(attended, "seq", split_axis=0, concat_axis=1, tiled=True),
        lax.all_to_all(grad_query, "seq", split_axis=0, concat_axis=1, tiled=True),
        lax.all_to_all(grad_key, "seq", split_axis=0, concat_axis=1, tiled=True),
        lax.all_to_all(grad_value, "seq", split_axis=0, concat_axis=1, tiled=True),
    )
    att_nodes = node_att.reshape(local_rows, width)
    mixed = jnp.dot(att_nodes, w_out, preferred_element_type=jnp.float32).astype(jnp.bfloat16)
    factor = 1.0 / math.sqrt(lax.axis_size("dp") * lax.axis_size("seq") * local_rows)
    summed = lax.psum_scatter(
        inner_rows(att_nodes, up_rows), "seq", scatter_dimension=0, tiled=True
    )
    grad_wo = lax.psum_scatter(summed, "dp", scatter_dimension=1, tiled=True)
    full_shape = (1, local_rows, width)
    return (
        mixed.reshape(full_shape),
        node_gq.reshape(full_shape),
        node_gk.reshape(full_shape),
        node_gv.reshape(full_shape),
        grad_wo * factor,
    )


MESH = pl.DeviceIdType.MESH
LANES = 128
MASKED = -1e30


def dot_nt(left, right):
    return lax.dot_general(
        left, right, (((1,), (1,)), ((), ())), preferred_element_type=jnp.float32
    )


def fused(
    peers, levels, head_width, factor, list_ref, count_ref, q_ref, k_ref, v_ref, u_hbm, w_hbm,
    mixed_hbm, gq_ref, gk_ref, gv_ref, gw_ref,
    head_q, head_g, keys2, values2, g_local, out_stage, key_sum, value_sum, att_nodes,
    kept_weights, kept_inverse, kept_logits, u_ref, w_ref, mixed_ref,
    gw_other, gw_own, gw_core, gw_level, gw_levels, gw_seq, gw_seqs,
    send_in, recv_in, send_out, recv_out, own_sem,
    send_core, recv_core, send_level, recv_level, send_seq, recv_seq,
    load_sem, own_out, mixed_sem,
):
    me = lax.axis_index("seq")
    replica = lax.axis_index("dp")
    core = lax.rem(replica, 2)
    level = replica // 2
    rows = q_ref.shape[0]
    chunks = head_q.shape[0]
    nodes = head_q.shape[1]
    listed, blocks = list_ref.shape
    block_rows = nodes // blocks
    per_device = blocks // peers
    span = chunks * LANES
    score_scale = 1.0 / math.sqrt(head_width)
    bf16, f32 = jnp.bfloat16, jnp.float32

    u_load = pltpu.make_async_copy(u_hbm, u_ref, load_sem.at[0])
    w_load = pltpu.make_async_copy(w_hbm, w_ref, load_sem.at[1])
    barrier = pltpu.get_barrier_semaphore()
    for p in range(1, peers):
        pl.semaphore_signal(
            barrier, inc=1, device_id={"seq": lax.rem(me + p, peers)}, device_id_type=MESH
        )
    other_core = level * 2 + 1 - core

    def level_at(p):
        return lax.rem(level + p, levels)

    pl.semaphore_signal(barrier, inc=1, device_id={"dp": other_core}, device_id_type=MESH)
    for p in range(1, levels):
        pl.semaphore_signal(
            barrier, inc=1, device_id={"dp": level_at(p) * 2 + core}, device_id_type=MESH
        )
    pl.semaphore_wait(barrier, peers + levels - 1)

    own_rows = pl.ds(pl.multiple_of(me * rows, rows), rows)

    def columns(device, c):
        return pl.ds(pl.multiple_of(device * span + c * LANES, LANES), LANES)

    sources = (q_ref, k_ref, v_ref, g_local)
    targets = (head_q, keys2, values2, head_g)

    def landing(a, c):
        if a in (1, 2):
            return targets[a][c].at[pl.ds(me * per_device, per_device), :, pl.ds(0, LANES)]
        return targets[a].at[c, own_rows]

    def leaving(a, device, c):
        if a in (1, 2):
            return sources[a].at[:, :, columns(device, c)]
        return sources[a].at[:, columns(device, c)]

    def inward(a, c, p):
        device = lax.rem(me + p, peers)
        return pltpu.make_async_remote_copy(
            src_ref=leaving(a, device, c),
            dst_ref=landing(a, c),
            send_sem=send_in.at[c, a, p - 1],
            recv_sem=recv_in.at[c, a, p - 1],
            device_id={"seq": device},
            device_id_type=MESH,
        )

    def own_copy(a, c):
        return pltpu.make_async_copy(
            leaving(a, me, c), landing(a, c), own_sem.at[c, a]
        )

    def start_in(a, c):
        for p in range(1, peers):
            inward(a, c, p).start()
        own_copy(a, c).start()

    def finish_in(a, c):
        for p in range(1, peers):
            inward(a, c, p).wait()
        own_copy(a, c).wait()

    returns = (att_nodes, gq_ref, gk_ref, gv_ref)

    def outward(a, c, p):
        device = lax.rem(me + p, peers)
        return pltpu.make_async_remote_copy(
            src_ref=out_stage.at[c, a, pl.ds(pl.multiple_of(device * rows, rows), rows)],
            dst_ref=returns[a].at[:, columns(me, c)],
            send_sem=send_out.at[c, a, p - 1],
            recv_sem=recv_out.at[c, a, p - 1],
            device_id={"seq": device},
            device_id_type=MESH,
        )

    def keep_own(a, c):
        return pltpu.make_async_copy(
            out_stage.at[c, a, own_rows], returns[a].at[:, columns(me, c)], own_out.at[c, a]
        )

    def grad_att(c):
        def one(device, carry):
            cols = columns(device, c)
            g_local[:, cols] = dot_nt(u_ref[...], w_ref[cols, :]).astype(bf16)
            return carry

        lax.fori_loop(0, peers, one, 0)

    lane = lax.broadcasted_iota(jnp.int32, (block_rows, LANES), 1)
    lane2 = lax.broadcasted_iota(jnp.int32, (2 * block_rows, LANES), 1)
    first = lane < head_width

    def stacked(x):
        return jnp.concatenate([jnp.where(first, x, 0.0), jnp.where(first, 0.0, x)], axis=0)

    def merged(x):
        return jnp.where(first, x[:block_rows], x[block_rows:])

    def core_copy(c):
        return pltpu.make_async_remote_copy(
            src_ref=gw_other.at[c], dst_ref=gw_core.at[c],
            send_sem=send_core.at[c], recv_sem=recv_core.at[c],
            device_id={"dp": other_core}, device_id_type=MESH,
        )

    def level_copy(c, p):
        return pltpu.make_async_remote_copy(
            src_ref=gw_level.at[c, level_at(p)], dst_ref=gw_levels.at[c, p - 1],
            send_sem=send_level.at[c, p - 1], recv_sem=recv_level.at[c, p - 1],
            device_id={"dp": level_at(p) * 2 + core}, device_id_type=MESH,
        )

    def seq_copy(c, p):
        device = lax.rem(me + p, peers)
        return pltpu.make_async_remote_copy(
            src_ref=gw_seq.at[c, pl.ds(pl.multiple_of(device * LANES, LANES), LANES)],
            dst_ref=gw_seqs.at[c, p - 1],
            send_sem=send_seq.at[c, p - 1], recv_sem=recv_seq.at[c, p - 1],
            device_id={"seq": device}, device_id_type=MESH,
        )

    def gw_partial(c):
        for p in range(1, peers):
            outward(0, c, p).wait()
        keep_own(0, c).wait()

        def up_columns(which):
            return jnp.concatenate(
                [
                    u_ref[:, pl.ds(pl.multiple_of((at * 2 + which) * LANES, LANES), LANES)]
                    for at in range(levels)
                ],
                axis=1,
            )

        def one(device, carry):
            place = pl.ds(pl.multiple_of(device * LANES, LANES), LANES)
            att = att_nodes[:, columns(device, c)]
            theirs = inner_rows(att, up_columns(1 - core)).astype(bf16)
            ours = inner_rows(att, up_columns(core))
            for at in range(levels):
                cut = slice(at * LANES, (at + 1) * LANES)
                gw_other[c, at, place, :] = theirs[:, cut]
                gw_own[c, at, place, :] = ours[:, cut]
            return carry

        lax.fori_loop(0, peers, one, 0)
        core_copy(c).start()

    def gw_across_levels(c):
        core_copy(c).wait()

        def one(at, carry):
            total = gw_own[c, at] + gw_core[c, at].astype(f32)
            gw_own[c, at] = total
            gw_level[c, at] = total.astype(bf16)
            return carry

        lax.fori_loop(0, levels, one, 0)
        for p in range(1, levels):
            level_copy(c, p).start()

    def gw_across_seq(c):
        total = gw_own[c, level]
        for p in range(1, levels):
            level_copy(c, p).wait()
            total = total + gw_levels[c, p - 1].astype(f32)
        gw_own[c, level] = total
        gw_seq[c] = total.astype(bf16)
        for p in range(1, peers):
            seq_copy(c, p).start()

    def gw_finish(c):
        total = gw_own[c, level, pl.ds(pl.multiple_of(me * LANES, LANES), LANES), :]
        for p in range(1, peers):
            seq_copy(c, p).wait()
            total = total + gw_seqs[c, p - 1].astype(f32)
        gw_ref[c * LANES:(c + 1) * LANES, :] = total * factor

    def dest_blocks(p):
        device = lax.rem(me + p, peers)
        return [device * per_device + at for at in range(per_device)]

    def rows_of(b):
        return pl.ds(pl.multiple_of(b * block_rows, block_rows), block_rows)

    def listed_rows(table, b):
        return jnp.concatenate([table[list_ref[j, b]] for j in range(listed)], axis=0)

    def run_between(p, between):
        for at, step in between:
            pl.when(p == at)(step)

    def forward(c, between):
        def one_group(step, carry):
            p = step + 1
            group = dest_blocks(p)
            lefts = []
            for b in group:
                q = head_q[c, rows_of(b), :].astype(f32) * score_scale
                count = count_ref[b]
                used = lane2 < 0
                for j in range(listed):
                    used = used | (lane2 == jnp.where(j < count, list_ref[j, b], -1))
                bias = jnp.where(used, 0.0, MASKED)
                lefts.append(jnp.concatenate([stacked(q), bias], axis=1).astype(bf16))
            scores = [dot_nt(left, listed_rows(keys2[c], b)) for left, b in zip(lefts, group)]
            tops = [jnp.max(score, axis=1, keepdims=True) for score in scores]
            weights = [jnp.exp(score - top).astype(bf16) for score, top in zip(scores, tops)]
            sums = [
                jnp.dot(weight, listed_rows(values2[c], b), preferred_element_type=f32)
                for weight, b in zip(weights, group)
            ]
            for b, weight, summed in zip(group, weights, sums):
                for j in range(listed):
                    kept_weights[c, b, j] = weight[:, j * block_rows:(j + 1) * block_rows]
                inverse = 1.0 / summed[:, LANES:LANES + 1]
                kept_inverse[c, b] = jnp.broadcast_to(inverse, (2 * block_rows, LANES))
                out_stage[c, 0, rows_of(b), :] = merged(summed[:, :LANES] * inverse).astype(bf16)

            @pl.when(p < peers)
            def _():
                outward(0, c, p).start()

            run_between(p, between)
            return carry

        lax.fori_loop(0, peers, one_group, 0)
        keep_own(0, c).start()

    def backward(c, between):
        key_sum[...] = jnp.zeros_like(key_sum)
        value_sum[...] = jnp.zeros_like(value_sum)

        def one_group(step, carry):
            p = step + 1
            group = dest_blocks(p)
            q_sides, g_sides, rights = [], [], []
            for b in group:
                inverse = kept_inverse[c, b]
                q_pair = stacked(head_q[c, rows_of(b), :].astype(f32) * score_scale)
                g_pair = stacked(head_g[c, rows_of(b), :].astype(f32))
                attended = out_stage[c, 0, rows_of(b), :].astype(f32)
                delta = jnp.sum(
                    g_pair * jnp.concatenate([attended, attended], axis=0), axis=1, keepdims=True
                )
                high = delta.astype(bf16).astype(f32)
                middle = (delta - high).astype(bf16).astype(f32)
                low = delta - high - middle
                shift = jnp.where(
                    lane2 == 0, -high,
                    jnp.where(lane2 == 1, -middle, jnp.where(lane2 == 2, -low, 0.0)),
                )
                q_sides.append((q_pair * inverse).astype(bf16))
                g_sides.append((g_pair * inverse).astype(bf16))
                rights.append(jnp.concatenate([g_pair, shift], axis=1).astype(bf16))
            shifted = [dot_nt(right, listed_rows(values2[c], b)) for right, b in zip(rights, group)]
            for at, b in enumerate(group):
                for j in range(listed):
                    cut = slice(j * block_rows, (j + 1) * block_rows)
                    kept_logits[at, j] = (
                        kept_weights[c, b, j].astype(f32) * shifted[at][:, cut]
                    ).astype(bf16)
            wide_logits, wide_weights = [], []
            for at, b in enumerate(group):
                logits = jnp.concatenate([kept_logits[at, j] for j in range(listed)], axis=1)
                grad_q = jnp.dot(
                    logits, listed_rows(keys2[c], b)[:, :LANES],
                    preferred_element_type=f32,
                )
                grad_q = merged(grad_q * (kept_inverse[c, b] * score_scale))
                out_stage[c, 1, rows_of(b), :] = grad_q.astype(bf16)
                slots = []
                for key_block in range(blocks):
                    slot = jnp.int32(listed)
                    for j in range(listed):
                        slot = jnp.where(list_ref[j, b] == key_block, j, slot)
                    slots.append(slot)
                wide_logits.append(jnp.concatenate([kept_logits[at, i] for i in slots], axis=1))
                wide_weights.append(jnp.concatenate([kept_weights[c, b, i] for i in slots], axis=1))
            key_sum[...] += inner_rows(
                jnp.concatenate(q_sides, axis=0), jnp.concatenate(wide_logits, axis=0)
            )
            value_sum[...] += inner_rows(
                jnp.concatenate(g_sides, axis=0), jnp.concatenate(wide_weights, axis=0)
            )

            @pl.when(p < peers)
            def _():
                outward(1, c, p).start()

            run_between(p, between)
            return carry

        lax.fori_loop(0, peers, one_group, 0)
        out_stage[c, 2] = key_sum[...].T.astype(bf16)
        for p in range(1, peers):
            outward(2, c, p).start()
        out_stage[c, 3] = value_sum[...].T.astype(bf16)
        for p in range(1, peers):
            outward(3, c, p).start()
        for a in range(1, 4):
            keep_own(a, c).start()

    def project():
        mixed_ref[...] = jnp.dot(
            att_nodes[...], w_ref[...], preferred_element_type=f32
        ).astype(bf16)
        pltpu.make_async_copy(mixed_ref, mixed_hbm, mixed_sem.at[0]).start()

    for a in range(3):
        start_in(a, 0)
    u_load.start()
    w_load.start()
    u_load.wait()
    w_load.wait()
    for c in range(chunks):
        grad_att(c)
    block_of = lax.broadcasted_iota(jnp.int32, (blocks, block_rows, LANES), 0)
    node_lane = lax.broadcasted_iota(jnp.int32, (blocks, block_rows, LANES), 2)
    for c in range(chunks):
        keys2[c][:, :, LANES:] = jnp.where(node_lane == block_of, 1.0, 0.0).astype(bf16)
        values2[c][:, :, LANES:] = jnp.where(node_lane < 3, 1.0, 0.0).astype(bf16)
    nothing = jnp.zeros((2 * block_rows, block_rows), bf16)
    for c in range(chunks):
        for b in range(blocks):
            kept_weights[c, b, listed] = nothing
    for at in range(per_device):
        kept_logits[at, listed] = nothing
    for c in range(chunks):
        for a in range(3):
            finish_in(a, c)
            if a == 1:
                if c + 1 < chunks:
                    for later in range(3):
                        start_in(later, c + 1)
                else:
                    for every in range(chunks):
                        start_in(3, every)
        between = []
        if c > 0:
            between.append((2, functools.partial(gw_partial, c - 1)))
            between.append((4, functools.partial(gw_across_levels, c - 1)))
        forward(c, between)
    last = chunks - 1
    for c in range(chunks):
        finish_in(3, c)
        between = []
        if c == 0:
            between.append((2, functools.partial(gw_partial, last)))
            between.append((3, functools.partial(gw_across_levels, last)))
            between.append((4, project))
        else:
            between.append((1, functools.partial(gw_across_seq, c - 1)))
        backward(c, between)
    gw_across_seq(last)
    for c in range(chunks):
        gw_finish(c)
    pltpu.make_async_copy(mixed_ref, mixed_hbm, mixed_sem.at[0]).wait()
    for c in range(chunks):
        for a in range(1, 4):
            for p in range(1, peers):
                outward(a, c, p).wait()
            keep_own(a, c).wait()


def copy_out(count, *refs):
    sources, targets, sems = refs[:count], refs[count:2 * count], refs[2 * count]
    copies = [
        pltpu.make_async_copy(sources[i], targets[i], sems.at[i]) for i in range(count)
    ]
    for copy in copies:
        copy.start()
    for copy in copies:
        copy.wait()


def local_fused(queries, keys, values, upstream, w_out, key_blocks, block_counts):
    rows, width = queries.shape[1:]
    peers = lax.axis_size("seq")
    chunks = width // peers // LANES
    nodes = rows * peers
    bf16, f32 = jnp.bfloat16, jnp.float32
    replicas = lax.axis_size("dp")
    levels = replicas // 2
    blocks, listed = key_blocks.shape[1:]
    block_rows = nodes // blocks
    by_block = (blocks // peers, block_rows, width)
    factor = 1.0 / math.sqrt(replicas * nodes)
    vmem = pl.BlockSpec(memory_space=pltpu.VMEM)
    anywhere = pl.BlockSpec(memory_space=pl.ANY)
    smem = pl.BlockSpec(memory_space=pltpu.SMEM)
    part = jax.ShapeDtypeStruct((rows, width), bf16)
    results = pl.pallas_call(
        functools.partial(fused, peers, levels, width // HEADS, factor),
        out_shape=(part, part, part, part, jax.ShapeDtypeStruct((chunks * LANES, width // replicas), f32)),
        in_specs=[smem, smem] + [anywhere] * 5,
        out_specs=[anywhere] * 4 + [vmem],
        scratch_shapes=[
            pltpu.VMEM((chunks, nodes, LANES), bf16),
            pltpu.VMEM((chunks, nodes, LANES), bf16),
            tuple(pltpu.VMEM((blocks, block_rows, 2 * LANES), bf16) for _ in range(chunks)),
            tuple(pltpu.VMEM((blocks, block_rows, 2 * LANES), bf16) for _ in range(chunks)),
            pltpu.VMEM((rows, width), bf16),
            pltpu.VMEM((chunks, 4, nodes, LANES), bf16),
            pltpu.VMEM((LANES, nodes), f32),
            pltpu.VMEM((LANES, nodes), f32),
            pltpu.VMEM((rows, width), bf16),
            pltpu.VMEM((chunks, blocks, listed + 1, 2 * block_rows, block_rows), bf16),
            pltpu.VMEM((chunks, blocks, 2 * block_rows, LANES), f32),
            pltpu.VMEM((blocks // peers, listed + 1, 2 * block_rows, block_rows), bf16),
            pltpu.VMEM((rows, width), bf16),
            pltpu.VMEM((width, width), bf16),
            pltpu.VMEM((rows, width), bf16),
            pltpu.VMEM((chunks, levels, peers * LANES, LANES), bf16),
            pltpu.VMEM((chunks, levels, peers * LANES, LANES), f32),
            pltpu.VMEM((chunks, levels, peers * LANES, LANES), bf16),
            pltpu.VMEM((chunks, levels, peers * LANES, LANES), bf16),
            pltpu.VMEM((chunks, levels - 1, peers * LANES, LANES), bf16),
            pltpu.VMEM((chunks, peers * LANES, LANES), bf16),
            pltpu.VMEM((chunks, peers - 1, LANES, LANES), bf16),
            pltpu.SemaphoreType.DMA((chunks, 4, peers - 1)),
            pltpu.SemaphoreType.DMA((chunks, 4, peers - 1)),
            pltpu.SemaphoreType.DMA((chunks, 4, peers - 1)),
            pltpu.SemaphoreType.DMA((chunks, 4, peers - 1)),
            pltpu.SemaphoreType.DMA((chunks, 4)),
            pltpu.SemaphoreType.DMA((chunks,)),
            pltpu.SemaphoreType.DMA((chunks,)),
            pltpu.SemaphoreType.DMA((chunks, levels - 1)),
            pltpu.SemaphoreType.DMA((chunks, levels - 1)),
            pltpu.SemaphoreType.DMA((chunks, peers - 1)),
            pltpu.SemaphoreType.DMA((chunks, peers - 1)),
            pltpu.SemaphoreType.DMA((2,)),
            pltpu.SemaphoreType.DMA((chunks, 4)),
            pltpu.SemaphoreType.DMA((1,)),
        ],
        compiler_params=pltpu.CompilerParams(
            collective_id=0, has_side_effects=True, vmem_limit_bytes=56 * 1024 * 1024
        ),
        name="graph_attention",
    )(
        key_blocks[0].T, block_counts[0], queries[0], keys.reshape(by_block),
        values.reshape(by_block), upstream[0], w_out,
    )
    count = len(results)
    mixed, grad_q, grad_k, grad_v, grad_wo = pl.pallas_call(
        functools.partial(copy_out, count),
        out_shape=[jax.ShapeDtypeStruct(result.shape, result.dtype) for result in results],
        in_specs=[anywhere] * count,
        out_specs=[anywhere] * count,
        scratch_shapes=[pltpu.SemaphoreType.DMA((count,))],
        compiler_params=pltpu.CompilerParams(vmem_limit_bytes=56 * 1024 * 1024),
        name="copy_out",
    )(*results)
    return mixed[None], grad_q[None], grad_k[None], grad_v[None], grad_wo


def local(queries, keys, values, upstream, w_out, key_blocks, block_counts):
    width = queries.shape[2]
    peers = lax.axis_size("seq")
    pair = 2 * (width // HEADS) == LANES and width % (peers * LANES) == 0
    whole_blocks = key_blocks.shape[1] % peers == 0 and key_blocks.shape[1] <= LANES
    whole_blocks = whole_blocks and peers >= 4
    columns_fit = lax.axis_size("dp") * LANES == width
    chosen = local_fused if pair and whole_blocks and columns_fit else local_plain
    return chosen(queries, keys, values, upstream, w_out, key_blocks, block_counts)


def solution(mesh):
    placed = (
        P("dp", "seq", None),
        P("dp", "seq", None),
        P("dp", "seq", None),
        P("dp", "seq", None),
        P(),
        P("dp", None, None),
        P("dp", None),
    )
    return jax.shard_map(
        local,
        mesh=mesh,
        in_specs=placed,
        out_specs=(
            P("dp", "seq", None),
            P("dp", "seq", None),
            P("dp", "seq", None),
            P("dp", "seq", None),
            P("seq", "dp"),
        ),
        check_vma=False,
    )
```

```python
import functools
import math

import jax
import jax.numpy as jnp
from jax import lax
from jax.experimental import pallas as pl
from jax.experimental.pallas import tpu as pltpu
from jax.sharding import PartitionSpec as P

HEADS = 16


blocks_per_step = 4


def product(form, left, right):
    return jnp.einsum(form, left, right, preferred_element_type=jnp.float32)


def inner_rows(left, right):
    return lax.dot_general(
        left, right, (((0,), (0,)), ((), ())), preferred_element_type=jnp.float32
    )


def block_attention(head_q, head_k, head_v, head_g, key_lists, key_counts):
    node_count, head_count, head_width = head_q.shape
    block_count, listed = key_lists.shape
    block_rows = node_count // block_count
    steps_count = block_count // blocks_per_step
    score_scale = 1.0 / math.sqrt(head_width)
    query_groups = head_q.reshape(steps_count, blocks_per_step, block_rows, head_count, head_width)
    grad_groups = head_g.reshape(steps_count, blocks_per_step, block_rows, head_count, head_width)
    key_table = head_k.reshape(block_count, block_rows, head_count, head_width)
    value_table = head_v.reshape(block_count, block_rows, head_count, head_width)
    list_groups = key_lists.reshape(steps_count, blocks_per_step, listed)
    count_groups = key_counts.reshape(steps_count, blocks_per_step)
    slot_index = jnp.arange(listed, dtype=jnp.int32)

    def one_step(accumulated, inputs):
        key_acc, value_acc = accumulated
        query_part, grad_part, list_part, count_part = inputs
        keys_near = key_table[list_part]
        values_near = value_table[list_part]
        scores = product("gqnd,gjknd->gnqjk", query_part, keys_near) * score_scale
        usable = (slot_index[None, :] < count_part[:, None])[:, None, None, :, None]
        scores = jnp.where(usable, scores, -jnp.inf)
        highest = jnp.max(scores, axis=(3, 4), keepdims=True)
        raised = jnp.exp(scores - highest)
        probability = raised / jnp.sum(raised, axis=(3, 4), keepdims=True)
        weights = probability.astype(jnp.bfloat16)
        attended = product("gnqjk,gjknd->gqnd", weights, values_near).astype(jnp.bfloat16)
        row_delta = jnp.sum(grad_part.astype(jnp.float32) * attended.astype(jnp.float32), axis=3)
        grad_scores = product("gqnd,gjknd->gnqjk", grad_part, values_near)
        shifted = grad_scores - jnp.transpose(row_delta, (0, 2, 1))[:, :, :, None, None]
        grad_logits = (probability * shifted).astype(jnp.bfloat16)
        grad_query = (product("gnqjk,gjknd->gqnd", grad_logits, keys_near) * score_scale).astype(
            jnp.bfloat16
        )
        key_terms = product("gnqjk,gqnd->gjknd", grad_logits, query_part) * score_scale
        value_terms = product("gnqjk,gqnd->gjknd", weights, grad_part)
        flat_list = list_part.reshape(-1)
        key_acc = key_acc.at[flat_list].add(
            key_terms.reshape(-1, block_rows, head_count, head_width)
        )
        value_acc = value_acc.at[flat_list].add(
            value_terms.reshape(-1, block_rows, head_count, head_width)
        )
        return ((key_acc, value_acc), (attended, grad_query))

    empty = jnp.zeros((block_count, block_rows, head_count, head_width), jnp.float32)
    (key_acc, value_acc), (attended, grad_query) = lax.scan(
        one_step, (empty, empty), (query_groups, grad_groups, list_groups, count_groups)
    )
    shape = (node_count, head_count, head_width)
    return (
        attended.reshape(shape),
        grad_query.reshape(shape),
        key_acc.astype(jnp.bfloat16).reshape(shape),
        value_acc.astype(jnp.bfloat16).reshape(shape),
    )


def project_back(up_rows, w_out):
    return lax.dot_general(
        up_rows, w_out, (((1,), (1,)), ((), ())), preferred_element_type=jnp.float32
    ).astype(jnp.bfloat16)


def local_plain(queries, keys, values, upstream, w_out, key_blocks, block_counts):
    local_rows = queries.shape[1]
    width = queries.shape[2]
    head_width = width // HEADS
    up_rows = upstream[0]

    def split_heads(array):
        return array.reshape(local_rows, HEADS, head_width)

    query_heads = split_heads(queries[0])
    key_heads = split_heads(keys[0])
    value_heads = split_heads(values[0])
    grad_att = project_back(up_rows, w_out)
    head_q, head_k, head_v, head_g = (
        lax.all_to_all(query_heads, "seq", split_axis=1, concat_axis=0, tiled=True),
        lax.all_to_all(key_heads, "seq", split_axis=1, concat_axis=0, tiled=True),
        lax.all_to_all(value_heads, "seq", split_axis=1, concat_axis=0, tiled=True),
        lax.all_to_all(split_heads(grad_att), "seq", split_axis=1, concat_axis=0, tiled=True),
    )
    attended, grad_query, grad_key, grad_value = block_attention(
        head_q, head_k, head_v, head_g, key_blocks[0], block_counts[0]
    )
    node_att, node_gq, node_gk, node_gv = (
        lax.all_to_all(attended, "seq", split_axis=0, concat_axis=1, tiled=True),
        lax.all_to_all(grad_query, "seq", split_axis=0, concat_axis=1, tiled=True),
        lax.all_to_all(grad_key, "seq", split_axis=0, concat_axis=1, tiled=True),
        lax.all_to_all(grad_value, "seq", split_axis=0, concat_axis=1, tiled=True),
    )
    att_nodes = node_att.reshape(local_rows, width)
    mixed = jnp.dot(att_nodes, w_out, preferred_element_type=jnp.float32).astype(jnp.bfloat16)
    factor = 1.0 / math.sqrt(lax.axis_size("dp") * lax.axis_size("seq") * local_rows)
    summed = lax.psum_scatter(
        inner_rows(att_nodes, up_rows), "seq", scatter_dimension=0, tiled=True
    )
    grad_wo = lax.psum_scatter(summed, "dp", scatter_dimension=1, tiled=True)
    full_shape = (1, local_rows, width)
    return (
        mixed.reshape(full_shape),
        node_gq.reshape(full_shape),
        node_gk.reshape(full_shape),
        node_gv.reshape(full_shape),
        grad_wo * factor,
    )


MESH = pl.DeviceIdType.MESH
LANES = 128
MASKED = -1e30


def dot_nt(left, right):
    return lax.dot_general(
        left, right, (((1,), (1,)), ((), ())), preferred_element_type=jnp.float32
    )


def fused(
    peers, levels, head_width, factor, list_ref, count_ref, q_hbm, k_hbm, v_hbm, u_hbm, w_hbm,
    mixed_hbm, gq_hbm, gk_hbm, gv_hbm, gw_ref,
    head_q, head_g, keys2, values2, g_local, out_stage, key_sum, value_sum, att_nodes,
    kept_weights, kept_inverse, kept_logits,
    q_ref, k_ref, v_ref, u_ref, w_ref, mixed_ref, gq_ref, gk_ref, gv_ref,
    gw_other, gw_own, gw_core, gw_level, gw_levels, gw_seq, gw_seqs,
    send_in, recv_in, send_out, recv_out, own_sem,
    send_core, recv_core, send_level, recv_level, send_seq, recv_seq,
    load_sem, own_out, mixed_sem,
):
    me = lax.axis_index("seq")
    replica = lax.axis_index("dp")
    core = lax.rem(replica, 2)
    level = replica // 2
    rows = q_ref.shape[0]
    chunks = head_q.shape[0]
    nodes = head_q.shape[1]
    listed, blocks = list_ref.shape
    block_rows = nodes // blocks
    per_device = blocks // peers
    span = chunks * LANES
    score_scale = 1.0 / math.sqrt(head_width)
    bf16, f32 = jnp.bfloat16, jnp.float32

    loads = [
        pltpu.make_async_copy(there, here, load_sem.at[at])
        for at, (there, here) in enumerate(
            [(q_hbm, q_ref), (k_hbm, k_ref), (v_hbm, v_ref), (u_hbm, u_ref), (w_hbm, w_ref)]
        )
    ]
    for load in loads:
        load.start()
    barrier = pltpu.get_barrier_semaphore()
    for p in range(1, peers):
        pl.semaphore_signal(
            barrier, inc=1, device_id={"seq": lax.rem(me + p, peers)}, device_id_type=MESH
        )
    other_core = level * 2 + 1 - core

    def level_at(p):
        return lax.rem(level + p, levels)

    pl.semaphore_signal(barrier, inc=1, device_id={"dp": other_core}, device_id_type=MESH)
    for p in range(1, levels):
        pl.semaphore_signal(
            barrier, inc=1, device_id={"dp": level_at(p) * 2 + core}, device_id_type=MESH
        )
    pl.semaphore_wait(barrier, peers + levels - 1)

    own_rows = pl.ds(pl.multiple_of(me * rows, rows), rows)

    def columns(device, c):
        return pl.ds(pl.multiple_of(device * span + c * LANES, LANES), LANES)

    sources = (q_ref, k_ref, v_ref, g_local)
    targets = (head_q, keys2, values2, head_g)

    def landing(a, c):
        if a in (1, 2):
            return targets[a][c].at[pl.ds(me * per_device, per_device), :, pl.ds(0, LANES)]
        return targets[a].at[c, own_rows]

    def leaving(a, device, c):
        if a in (1, 2):
            return sources[a].at[:, :, columns(device, c)]
        return sources[a].at[:, columns(device, c)]

    def inward(a, c, p):
        device = lax.rem(me + p, peers)
        return pltpu.make_async_remote_copy(
            src_ref=leaving(a, device, c),
            dst_ref=landing(a, c),
            send_sem=send_in.at[c, a, p - 1],
            recv_sem=recv_in.at[c, a, p - 1],
            device_id={"seq": device},
            device_id_type=MESH,
        )

    def own_copy(a, c):
        return pltpu.make_async_copy(
            leaving(a, me, c), landing(a, c), own_sem.at[c, a]
        )

    def start_in(a, c):
        for p in range(1, peers):
            inward(a, c, p).start()
        own_copy(a, c).start()

    def finish_in(a, c):
        for p in range(1, peers):
            inward(a, c, p).wait()
        own_copy(a, c).wait()

    returns = (att_nodes, gq_ref, gk_ref, gv_ref)

    def outward(a, c, p):
        device = lax.rem(me + p, peers)
        return pltpu.make_async_remote_copy(
            src_ref=out_stage.at[c, a, pl.ds(pl.multiple_of(device * rows, rows), rows)],
            dst_ref=returns[a].at[:, columns(me, c)],
            send_sem=send_out.at[c, a, p - 1],
            recv_sem=recv_out.at[c, a, p - 1],
            device_id={"seq": device},
            device_id_type=MESH,
        )

    def keep_own(a, c):
        return pltpu.make_async_copy(
            out_stage.at[c, a, own_rows], returns[a].at[:, columns(me, c)], own_out.at[c, a]
        )

    def grad_att(c):
        def one(device, carry):
            cols = columns(device, c)
            g_local[:, cols] = dot_nt(u_ref[...], w_ref[cols, :]).astype(bf16)
            return carry

        lax.fori_loop(0, peers, one, 0)

    lane = lax.broadcasted_iota(jnp.int32, (block_rows, LANES), 1)
    lane2 = lax.broadcasted_iota(jnp.int32, (2 * block_rows, LANES), 1)
    first = lane < head_width

    def stacked(x):
        return jnp.concatenate([jnp.where(first, x, 0.0), jnp.where(first, 0.0, x)], axis=0)

    def merged(x):
        return jnp.where(first, x[:block_rows], x[block_rows:])

    def core_copy(c):
        return pltpu.make_async_remote_copy(
            src_ref=gw_other.at[c], dst_ref=gw_core.at[c],
            send_sem=send_core.at[c], recv_sem=recv_core.at[c],
            device_id={"dp": other_core}, device_id_type=MESH,
        )

    def level_copy(c, p):
        return pltpu.make_async_remote_copy(
            src_ref=gw_level.at[c, level_at(p)], dst_ref=gw_levels.at[c, p - 1],
            send_sem=send_level.at[c, p - 1], recv_sem=recv_level.at[c, p - 1],
            device_id={"dp": level_at(p) * 2 + core}, device_id_type=MESH,
        )

    def seq_copy(c, p):
        device = lax.rem(me + p, peers)
        return pltpu.make_async_remote_copy(
            src_ref=gw_seq.at[c, pl.ds(pl.multiple_of(device * LANES, LANES), LANES)],
            dst_ref=gw_seqs.at[c, p - 1],
            send_sem=send_seq.at[c, p - 1], recv_sem=recv_seq.at[c, p - 1],
            device_id={"seq": device}, device_id_type=MESH,
        )

    def gw_partial(c):
        for p in range(1, peers):
            outward(0, c, p).wait()
        keep_own(0, c).wait()

        def up_columns(which):
            return jnp.concatenate(
                [
                    u_ref[:, pl.ds(pl.multiple_of((at * 2 + which) * LANES, LANES), LANES)]
                    for at in range(levels)
                ],
                axis=1,
            )

        def one(device, carry):
            place = pl.ds(pl.multiple_of(device * LANES, LANES), LANES)
            att = att_nodes[:, columns(device, c)]
            theirs = inner_rows(att, up_columns(1 - core)).astype(bf16)
            ours = inner_rows(att, up_columns(core))
            for at in range(levels):
                cut = slice(at * LANES, (at + 1) * LANES)
                gw_other[c, at, place, :] = theirs[:, cut]
                gw_own[c, at, place, :] = ours[:, cut]
            return carry

        lax.fori_loop(0, peers, one, 0)
        core_copy(c).start()

    def gw_across_levels(c):
        core_copy(c).wait()

        def one(at, carry):
            total = gw_own[c, at] + gw_core[c, at].astype(f32)
            gw_own[c, at] = total
            gw_level[c, at] = total.astype(bf16)
            return carry

        lax.fori_loop(0, levels, one, 0)
        for p in range(1, levels):
            level_copy(c, p).start()

    def gw_across_seq(c):
        total = gw_own[c, level]
        for p in range(1, levels):
            level_copy(c, p).wait()
            total = total + gw_levels[c, p - 1].astype(f32)
        gw_own[c, level] = total
        gw_seq[c] = total.astype(bf16)
        for p in range(1, peers):
            seq_copy(c, p).start()

    def gw_finish(c):
        total = gw_own[c, level, pl.ds(pl.multiple_of(me * LANES, LANES), LANES), :]
        for p in range(1, peers):
            seq_copy(c, p).wait()
            total = total + gw_seqs[c, p - 1].astype(f32)
        gw_ref[c * LANES:(c + 1) * LANES, :] = total * factor

    def dest_blocks(p):
        device = lax.rem(me + p, peers)
        return [device * per_device + at for at in range(per_device)]

    def rows_of(b):
        return pl.ds(pl.multiple_of(b * block_rows, block_rows), block_rows)

    def listed_rows(table, b):
        return jnp.concatenate([table[list_ref[j, b]] for j in range(listed)], axis=0)

    def run_between(p, between):
        for at, step in between:
            pl.when(p == at)(step)

    def forward(c):
        def one_group(step, carry):
            p = step + 1
            group = dest_blocks(p)
            lefts = []
            for b in group:
                q = head_q[c, rows_of(b), :].astype(f32) * score_scale
                count = count_ref[b]
                used = lane2 < 0
                for j in range(listed):
                    used = used | (lane2 == jnp.where(j < count, list_ref[j, b], -1))
                bias = jnp.where(used, 0.0, MASKED)
                lefts.append(jnp.concatenate([stacked(q), bias], axis=1).astype(bf16))
            scores = [dot_nt(left, listed_rows(keys2[c], b)) for left, b in zip(lefts, group)]
            tops = [jnp.max(score, axis=1, keepdims=True) for score in scores]
            weights = [jnp.exp(score - top).astype(bf16) for score, top in zip(scores, tops)]
            sums = [
                jnp.dot(weight, listed_rows(values2[c], b), preferred_element_type=f32)
                for weight, b in zip(weights, group)
            ]
            for b, weight, summed in zip(group, weights, sums):
                for j in range(listed):
                    kept_weights[c, b, j] = weight[:, j * block_rows:(j + 1) * block_rows]
                inverse = 1.0 / summed[:, LANES:LANES + 1]
                kept_inverse[c, b] = jnp.broadcast_to(inverse, (2 * block_rows, LANES))
                out_stage[c, 0, rows_of(b), :] = merged(summed[:, :LANES] * inverse).astype(bf16)

            @pl.when(p < peers)
            def _():
                outward(0, c, p).start()

            return carry

        lax.fori_loop(0, peers, one_group, 0)
        keep_own(0, c).start()

    def backward(c, between):
        key_sum[...] = jnp.zeros_like(key_sum)
        value_sum[...] = jnp.zeros_like(value_sum)

        def one_group(step, carry):
            p = step + 1
            group = dest_blocks(p)
            q_sides, g_sides, rights = [], [], []
            for b in group:
                inverse = kept_inverse[c, b]
                q_pair = stacked(head_q[c, rows_of(b), :].astype(f32) * score_scale)
                g_pair = stacked(head_g[c, rows_of(b), :].astype(f32))
                attended = out_stage[c, 0, rows_of(b), :].astype(f32)
                delta = jnp.sum(
                    g_pair * jnp.concatenate([attended, attended], axis=0), axis=1, keepdims=True
                )
                high = delta.astype(bf16).astype(f32)
                middle = (delta - high).astype(bf16).astype(f32)
                low = delta - high - middle
                shift = jnp.where(
                    lane2 == 0, -high,
                    jnp.where(lane2 == 1, -middle, jnp.where(lane2 == 2, -low, 0.0)),
                )
                q_sides.append((q_pair * inverse).astype(bf16))
                g_sides.append((g_pair * inverse).astype(bf16))
                rights.append(jnp.concatenate([g_pair, shift], axis=1).astype(bf16))
            shifted = [dot_nt(right, listed_rows(values2[c], b)) for right, b in zip(rights, group)]
            for at, b in enumerate(group):
                for j in range(listed):
                    cut = slice(j * block_rows, (j + 1) * block_rows)
                    kept_logits[at, j] = (
                        kept_weights[c, b, j].astype(f32) * shifted[at][:, cut]
                    ).astype(bf16)
            wide_logits, wide_weights = [], []
            for at, b in enumerate(group):
                logits = jnp.concatenate([kept_logits[at, j] for j in range(listed)], axis=1)
                grad_q = jnp.dot(
                    logits, listed_rows(keys2[c], b)[:, :LANES],
                    preferred_element_type=f32,
                )
                grad_q = merged(grad_q * (kept_inverse[c, b] * score_scale))
                out_stage[c, 1, rows_of(b), :] = grad_q.astype(bf16)
                slots = []
                for key_block in range(blocks):
                    slot = jnp.int32(listed)
                    for j in range(listed):
                        slot = jnp.where(list_ref[j, b] == key_block, j, slot)
                    slots.append(slot)
                wide_logits.append(jnp.concatenate([kept_logits[at, i] for i in slots], axis=1))
                wide_weights.append(jnp.concatenate([kept_weights[c, b, i] for i in slots], axis=1))
            key_sum[...] += inner_rows(
                jnp.concatenate(q_sides, axis=0), jnp.concatenate(wide_logits, axis=0)
            )
            value_sum[...] += inner_rows(
                jnp.concatenate(g_sides, axis=0), jnp.concatenate(wide_weights, axis=0)
            )

            @pl.when(p < peers)
            def _():
                outward(1, c, p).start()

            run_between(p, between)
            return carry

        lax.fori_loop(0, peers, one_group, 0)
        out_stage[c, 2] = key_sum[...].T.astype(bf16)
        for p in range(1, peers):
            outward(2, c, p).start()
        out_stage[c, 3] = value_sum[...].T.astype(bf16)
        for p in range(1, peers):
            outward(3, c, p).start()
        for a in range(1, 4):
            keep_own(a, c).start()

    def project():
        mixed_ref[...] = jnp.dot(
            att_nodes[...], w_ref[...], preferred_element_type=f32
        ).astype(bf16)

    for a in range(3):
        loads[a].wait()
        start_in(a, 0)
    loads[3].wait()
    loads[4].wait()
    grad_att(0)
    start_in(3, 0)
    for c in range(1, chunks):
        grad_att(c)
    block_of = lax.broadcasted_iota(jnp.int32, (blocks, block_rows, LANES), 0)
    node_lane = lax.broadcasted_iota(jnp.int32, (blocks, block_rows, LANES), 2)
    for c in range(chunks):
        keys2[c][:, :, LANES:] = jnp.where(node_lane == block_of, 1.0, 0.0).astype(bf16)
        values2[c][:, :, LANES:] = jnp.where(node_lane < 3, 1.0, 0.0).astype(bf16)
    nothing = jnp.zeros((2 * block_rows, block_rows), bf16)
    for c in range(chunks):
        for b in range(blocks):
            kept_weights[c, b, listed] = nothing
    for at in range(per_device):
        kept_logits[at, listed] = nothing
    last = chunks - 1
    for c in range(chunks):
        for a in range(3):
            finish_in(a, c)
            if a == 1 and c < last:
                for later in range(4):
                    start_in(later, c + 1)
        forward(c)
        finish_in(3, c)
        between = [
            (2, functools.partial(gw_partial, c)),
            (3, functools.partial(gw_across_levels, c)),
        ]
        if c > 0:
            between.append((1, functools.partial(gw_across_seq, c - 1)))
        if c == last:
            between.append((4, project))
        backward(c, between)
    stores = [
        pltpu.make_async_copy(here, there, mixed_sem.at[a])
        for a, (here, there) in enumerate(
            [(mixed_ref, mixed_hbm), (gq_ref, gq_hbm), (gk_ref, gk_hbm), (gv_ref, gv_hbm)]
        )
    ]
    stores[0].start()
    for a in range(1, 4):
        for c in range(chunks):
            for p in range(1, peers):
                outward(a, c, p).wait()
            keep_own(a, c).wait()
        if a == 1:
            gw_across_seq(last)
        stores[a].start()
    for c in range(chunks):
        gw_finish(c)
    for store in stores:
        store.wait()


def copy_out(count, *refs):
    sources, targets, held = refs[:count], refs[count:2 * count], refs[2 * count]
    loaded, stored = refs[2 * count + 1:]
    loads = [pltpu.make_async_copy(sources[i], held[i], loaded.at[i]) for i in range(count)]
    stores = [pltpu.make_async_copy(held[i], targets[i], stored.at[i]) for i in range(count)]
    for load in loads:
        load.start()
    for load, store in zip(loads, stores):
        load.wait()
        store.start()
    for store in stores:
        store.wait()


def local_fused(queries, keys, values, upstream, w_out, key_blocks, block_counts):
    rows, width = queries.shape[1:]
    peers = lax.axis_size("seq")
    chunks = width // peers // LANES
    nodes = rows * peers
    bf16, f32 = jnp.bfloat16, jnp.float32
    replicas = lax.axis_size("dp")
    levels = replicas // 2
    blocks, listed = key_blocks.shape[1:]
    block_rows = nodes // blocks
    by_block = (blocks // peers, block_rows, width)
    factor = 1.0 / math.sqrt(replicas * nodes)
    vmem = pl.BlockSpec(memory_space=pltpu.VMEM)
    anywhere = pl.BlockSpec(memory_space=pl.ANY)
    smem = pl.BlockSpec(memory_space=pltpu.SMEM)
    part = jax.ShapeDtypeStruct((rows, width), bf16)
    results = pl.pallas_call(
        functools.partial(fused, peers, levels, width // HEADS, factor),
        out_shape=(part, part, part, part, jax.ShapeDtypeStruct((chunks * LANES, width // replicas), f32)),
        in_specs=[smem, smem] + [anywhere] * 5,
        out_specs=[anywhere] * 4 + [vmem],
        scratch_shapes=[
            pltpu.VMEM((chunks, nodes, LANES), bf16),
            pltpu.VMEM((chunks, nodes, LANES), bf16),
            tuple(pltpu.VMEM((blocks, block_rows, 2 * LANES), bf16) for _ in range(chunks)),
            tuple(pltpu.VMEM((blocks, block_rows, 2 * LANES), bf16) for _ in range(chunks)),
            pltpu.VMEM((rows, width), bf16),
            pltpu.VMEM((chunks, 4, nodes, LANES), bf16),
            pltpu.VMEM((LANES, nodes), f32),
            pltpu.VMEM((LANES, nodes), f32),
            pltpu.VMEM((rows, width), bf16),
            pltpu.VMEM((chunks, blocks, listed + 1, 2 * block_rows, block_rows), bf16),
            pltpu.VMEM((chunks, blocks, 2 * block_rows, LANES), f32),
            pltpu.VMEM((blocks // peers, listed + 1, 2 * block_rows, block_rows), bf16),
            pltpu.VMEM((rows, width), bf16),
            pltpu.VMEM(by_block, bf16),
            pltpu.VMEM(by_block, bf16),
            pltpu.VMEM((rows, width), bf16),
            pltpu.VMEM((width, width), bf16),
            pltpu.VMEM((rows, width), bf16),
            pltpu.VMEM((rows, width), bf16),
            pltpu.VMEM((rows, width), bf16),
            pltpu.VMEM((rows, width), bf16),
            pltpu.VMEM((chunks, levels, peers * LANES, LANES), bf16),
            pltpu.VMEM((chunks, levels, peers * LANES, LANES), f32),
            pltpu.VMEM((chunks, levels, peers * LANES, LANES), bf16),
            pltpu.VMEM((chunks, levels, peers * LANES, LANES), bf16),
            pltpu.VMEM((chunks, levels - 1, peers * LANES, LANES), bf16),
            pltpu.VMEM((chunks, peers * LANES, LANES), bf16),
            pltpu.VMEM((chunks, peers - 1, LANES, LANES), bf16),
            pltpu.SemaphoreType.DMA((chunks, 4, peers - 1)),
            pltpu.SemaphoreType.DMA((chunks, 4, peers - 1)),
            pltpu.SemaphoreType.DMA((chunks, 4, peers - 1)),
            pltpu.SemaphoreType.DMA((chunks, 4, peers - 1)),
            pltpu.SemaphoreType.DMA((chunks, 4)),
            pltpu.SemaphoreType.DMA((chunks,)),
            pltpu.SemaphoreType.DMA((chunks,)),
            pltpu.SemaphoreType.DMA((chunks, levels - 1)),
            pltpu.SemaphoreType.DMA((chunks, levels - 1)),
            pltpu.SemaphoreType.DMA((chunks, peers - 1)),
            pltpu.SemaphoreType.DMA((chunks, peers - 1)),
            pltpu.SemaphoreType.DMA((5,)),
            pltpu.SemaphoreType.DMA((chunks, 4)),
            pltpu.SemaphoreType.DMA((4,)),
        ],
        compiler_params=pltpu.CompilerParams(
            collective_id=0, has_side_effects=True, vmem_limit_bytes=56 * 1024 * 1024
        ),
        name="graph_attention",
    )(
        key_blocks[0].T, block_counts[0], queries[0], keys.reshape(by_block),
        values.reshape(by_block), upstream[0], w_out,
    )
    count = len(results)
    mixed, grad_q, grad_k, grad_v, grad_wo = pl.pallas_call(
        functools.partial(copy_out, count),
        out_shape=[jax.ShapeDtypeStruct(result.shape, result.dtype) for result in results],
        in_specs=[anywhere] * count,
        out_specs=[anywhere] * count,
        scratch_shapes=[
            tuple(pltpu.VMEM(result.shape, result.dtype) for result in results),
            pltpu.SemaphoreType.DMA((count,)),
            pltpu.SemaphoreType.DMA((count,)),
        ],
        compiler_params=pltpu.CompilerParams(vmem_limit_bytes=56 * 1024 * 1024),
        name="copy_out",
    )(*results)
    return mixed[None], grad_q[None], grad_k[None], grad_v[None], grad_wo


def local(queries, keys, values, upstream, w_out, key_blocks, block_counts):
    width = queries.shape[2]
    peers = lax.axis_size("seq")
    pair = 2 * (width // HEADS) == LANES and width % (peers * LANES) == 0
    whole_blocks = key_blocks.shape[1] % peers == 0 and key_blocks.shape[1] <= LANES
    whole_blocks = whole_blocks and peers >= 4
    columns_fit = lax.axis_size("dp") * LANES == width
    chosen = local_fused if pair and whole_blocks and columns_fit else local_plain
    return chosen(queries, keys, values, upstream, w_out, key_blocks, block_counts)


def solution(mesh):
    placed = (
        P("dp", "seq", None),
        P("dp", "seq", None),
        P("dp", "seq", None),
        P("dp", "seq", None),
        P(),
        P("dp", None, None),
        P("dp", None),
    )
    return jax.shard_map(
        local,
        mesh=mesh,
        in_specs=placed,
        out_specs=(
            P("dp", "seq", None),
            P("dp", "seq", None),
            P("dp", "seq", None),
            P("dp", "seq", None),
            P("seq", "dp"),
        ),
        check_vma=False,
    )
```

```python
import functools
import math

import jax
import jax.numpy as jnp
from jax import lax
from jax.experimental import pallas as pl
from jax.experimental.pallas import tpu as pltpu
from jax.sharding import PartitionSpec as P

HEADS = 16


blocks_per_step = 4


def product(form, left, right):
    return jnp.einsum(form, left, right, preferred_element_type=jnp.float32)


def inner_rows(left, right):
    return lax.dot_general(
        left, right, (((0,), (0,)), ((), ())), preferred_element_type=jnp.float32
    )


def block_attention(head_q, head_k, head_v, head_g, key_lists, key_counts):
    node_count, head_count, head_width = head_q.shape
    block_count, listed = key_lists.shape
    block_rows = node_count // block_count
    steps_count = block_count // blocks_per_step
    score_scale = 1.0 / math.sqrt(head_width)
    query_groups = head_q.reshape(steps_count, blocks_per_step, block_rows, head_count, head_width)
    grad_groups = head_g.reshape(steps_count, blocks_per_step, block_rows, head_count, head_width)
    key_table = head_k.reshape(block_count, block_rows, head_count, head_width)
    value_table = head_v.reshape(block_count, block_rows, head_count, head_width)
    list_groups = key_lists.reshape(steps_count, blocks_per_step, listed)
    count_groups = key_counts.reshape(steps_count, blocks_per_step)
    slot_index = jnp.arange(listed, dtype=jnp.int32)

    def one_step(accumulated, inputs):
        key_acc, value_acc = accumulated
        query_part, grad_part, list_part, count_part = inputs
        keys_near = key_table[list_part]
        values_near = value_table[list_part]
        scores = product("gqnd,gjknd->gnqjk", query_part, keys_near) * score_scale
        usable = (slot_index[None, :] < count_part[:, None])[:, None, None, :, None]
        scores = jnp.where(usable, scores, -jnp.inf)
        highest = jnp.max(scores, axis=(3, 4), keepdims=True)
        raised = jnp.exp(scores - highest)
        probability = raised / jnp.sum(raised, axis=(3, 4), keepdims=True)
        weights = probability.astype(jnp.bfloat16)
        attended = product("gnqjk,gjknd->gqnd", weights, values_near).astype(jnp.bfloat16)
        row_delta = jnp.sum(grad_part.astype(jnp.float32) * attended.astype(jnp.float32), axis=3)
        grad_scores = product("gqnd,gjknd->gnqjk", grad_part, values_near)
        shifted = grad_scores - jnp.transpose(row_delta, (0, 2, 1))[:, :, :, None, None]
        grad_logits = (probability * shifted).astype(jnp.bfloat16)
        grad_query = (product("gnqjk,gjknd->gqnd", grad_logits, keys_near) * score_scale).astype(
            jnp.bfloat16
        )
        key_terms = product("gnqjk,gqnd->gjknd", grad_logits, query_part) * score_scale
        value_terms = product("gnqjk,gqnd->gjknd", weights, grad_part)
        flat_list = list_part.reshape(-1)
        key_acc = key_acc.at[flat_list].add(
            key_terms.reshape(-1, block_rows, head_count, head_width)
        )
        value_acc = value_acc.at[flat_list].add(
            value_terms.reshape(-1, block_rows, head_count, head_width)
        )
        return ((key_acc, value_acc), (attended, grad_query))

    empty = jnp.zeros((block_count, block_rows, head_count, head_width), jnp.float32)
    (key_acc, value_acc), (attended, grad_query) = lax.scan(
        one_step, (empty, empty), (query_groups, grad_groups, list_groups, count_groups)
    )
    shape = (node_count, head_count, head_width)
    return (
        attended.reshape(shape),
        grad_query.reshape(shape),
        key_acc.astype(jnp.bfloat16).reshape(shape),
        value_acc.astype(jnp.bfloat16).reshape(shape),
    )


def project_back(up_rows, w_out):
    return lax.dot_general(
        up_rows, w_out, (((1,), (1,)), ((), ())), preferred_element_type=jnp.float32
    ).astype(jnp.bfloat16)


def local_plain(queries, keys, values, upstream, w_out, key_blocks, block_counts):
    local_rows = queries.shape[1]
    width = queries.shape[2]
    head_width = width // HEADS
    up_rows = upstream[0]

    def split_heads(array):
        return array.reshape(local_rows, HEADS, head_width)

    query_heads = split_heads(queries[0])
    key_heads = split_heads(keys[0])
    value_heads = split_heads(values[0])
    grad_att = project_back(up_rows, w_out)
    head_q, head_k, head_v, head_g = (
        lax.all_to_all(query_heads, "seq", split_axis=1, concat_axis=0, tiled=True),
        lax.all_to_all(key_heads, "seq", split_axis=1, concat_axis=0, tiled=True),
        lax.all_to_all(value_heads, "seq", split_axis=1, concat_axis=0, tiled=True),
        lax.all_to_all(split_heads(grad_att), "seq", split_axis=1, concat_axis=0, tiled=True),
    )
    attended, grad_query, grad_key, grad_value = block_attention(
        head_q, head_k, head_v, head_g, key_blocks[0], block_counts[0]
    )
    node_att, node_gq, node_gk, node_gv = (
        lax.all_to_all(attended, "seq", split_axis=0, concat_axis=1, tiled=True),
        lax.all_to_all(grad_query, "seq", split_axis=0, concat_axis=1, tiled=True),
        lax.all_to_all(grad_key, "seq", split_axis=0, concat_axis=1, tiled=True),
        lax.all_to_all(grad_value, "seq", split_axis=0, concat_axis=1, tiled=True),
    )
    att_nodes = node_att.reshape(local_rows, width)
    mixed = jnp.dot(att_nodes, w_out, preferred_element_type=jnp.float32).astype(jnp.bfloat16)
    factor = 1.0 / math.sqrt(lax.axis_size("dp") * lax.axis_size("seq") * local_rows)
    summed = lax.psum_scatter(
        inner_rows(att_nodes, up_rows), "seq", scatter_dimension=0, tiled=True
    )
    grad_wo = lax.psum_scatter(summed, "dp", scatter_dimension=1, tiled=True)
    full_shape = (1, local_rows, width)
    return (
        mixed.reshape(full_shape),
        node_gq.reshape(full_shape),
        node_gk.reshape(full_shape),
        node_gv.reshape(full_shape),
        grad_wo * factor,
    )


MESH = pl.DeviceIdType.MESH
LANES = 128
MASKED = -1e30


def dot_nt(left, right):
    return lax.dot_general(
        left, right, (((1,), (1,)), ((), ())), preferred_element_type=jnp.float32
    )


def fused(
    peers, levels, head_width, factor, list_ref, count_ref, q_hbm, k_hbm, v_hbm, u_hbm, w_hbm,
    mixed_hbm, gq_hbm, gk_hbm, gv_hbm, gw_ref,
    head_q, head_g, keys2, values2, g_local, out_stage, key_sum, value_sum, att_nodes,
    kept_weights, kept_inverse, kept_logits,
    q_ref, k_ref, v_ref, u_ref, w_ref, mixed_ref, gq_ref, gk_ref, gv_ref,
    gw_other, gw_own, gw_core, gw_seq, gw_seqs, gw_half, gw_level, gw_levels,
    send_in, recv_in, send_out, recv_out, own_sem,
    send_core, recv_core, send_level, recv_level, send_seq, recv_seq,
    load_sem, own_out, mixed_sem,
):
    me = lax.axis_index("seq")
    replica = lax.axis_index("dp")
    core = lax.rem(replica, 2)
    level = replica // 2
    rows = q_ref.shape[0]
    chunks = head_q.shape[0]
    nodes = head_q.shape[1]
    listed, blocks = list_ref.shape
    block_rows = nodes // blocks
    per_device = blocks // peers
    span = chunks * LANES
    score_scale = 1.0 / math.sqrt(head_width)
    bf16, f32 = jnp.bfloat16, jnp.float32

    loads = [
        pltpu.make_async_copy(there, here, load_sem.at[at])
        for at, (there, here) in enumerate(
            [(q_hbm, q_ref), (k_hbm, k_ref), (v_hbm, v_ref), (u_hbm, u_ref), (w_hbm, w_ref)]
        )
    ]
    for load in loads:
        load.start()
    barrier = pltpu.get_barrier_semaphore()
    for p in range(1, peers):
        pl.semaphore_signal(
            barrier, inc=1, device_id={"seq": lax.rem(me + p, peers)}, device_id_type=MESH
        )
    other_core = level * 2 + 1 - core

    def level_at(p):
        return lax.rem(level + p, levels)

    pl.semaphore_signal(barrier, inc=1, device_id={"dp": other_core}, device_id_type=MESH)
    for p in range(1, levels):
        pl.semaphore_signal(
            barrier, inc=1, device_id={"dp": level_at(p) * 2 + core}, device_id_type=MESH
        )
    pl.semaphore_wait(barrier, peers + levels - 1)

    own_rows = pl.ds(pl.multiple_of(me * rows, rows), rows)

    def columns(device, c):
        return pl.ds(pl.multiple_of(device * span + c * LANES, LANES), LANES)

    sources = (q_ref, k_ref, v_ref, g_local)
    targets = (head_q, keys2, values2, head_g)

    def landing(a, c):
        if a in (1, 2):
            return targets[a][c].at[pl.ds(me * per_device, per_device), :, pl.ds(0, LANES)]
        return targets[a].at[c, own_rows]

    def leaving(a, device, c):
        if a in (1, 2):
            return sources[a].at[:, :, columns(device, c)]
        return sources[a].at[:, columns(device, c)]

    def inward(a, c, p):
        device = lax.rem(me + p, peers)
        return pltpu.make_async_remote_copy(
            src_ref=leaving(a, device, c),
            dst_ref=landing(a, c),
            send_sem=send_in.at[c, a, p - 1],
            recv_sem=recv_in.at[c, a, p - 1],
            device_id={"seq": device},
            device_id_type=MESH,
        )

    def own_copy(a, c):
        return pltpu.make_async_copy(
            leaving(a, me, c), landing(a, c), own_sem.at[c, a]
        )

    def start_in(a, c):
        for p in range(1, peers):
            inward(a, c, p).start()
        own_copy(a, c).start()

    def finish_in(a, c):
        for p in range(1, peers):
            inward(a, c, p).wait()
        own_copy(a, c).wait()

    returns = (att_nodes, gq_ref, gk_ref, gv_ref)

    def outward(a, c, p):
        device = lax.rem(me + p, peers)
        return pltpu.make_async_remote_copy(
            src_ref=out_stage.at[c, a, pl.ds(pl.multiple_of(device * rows, rows), rows)],
            dst_ref=returns[a].at[:, columns(me, c)],
            send_sem=send_out.at[c, a, p - 1],
            recv_sem=recv_out.at[c, a, p - 1],
            device_id={"seq": device},
            device_id_type=MESH,
        )

    def keep_own(a, c):
        return pltpu.make_async_copy(
            out_stage.at[c, a, own_rows], returns[a].at[:, columns(me, c)], own_out.at[c, a]
        )

    def grad_att(c):
        def one(device, carry):
            cols = columns(device, c)
            g_local[:, cols] = dot_nt(u_ref[...], w_ref[cols, :]).astype(bf16)
            return carry

        lax.fori_loop(0, peers, one, 0)

    lane = lax.broadcasted_iota(jnp.int32, (block_rows, LANES), 1)
    lane2 = lax.broadcasted_iota(jnp.int32, (2 * block_rows, LANES), 1)
    first = lane < head_width

    def stacked(x):
        return jnp.concatenate([jnp.where(first, x, 0.0), jnp.where(first, 0.0, x)], axis=0)

    def merged(x):
        return jnp.where(first, x[:block_rows], x[block_rows:])

    def core_copy(c):
        return pltpu.make_async_remote_copy(
            src_ref=gw_other.at[c], dst_ref=gw_core.at[c],
            send_sem=send_core.at[c], recv_sem=recv_core.at[c],
            device_id={"dp": other_core}, device_id_type=MESH,
        )

    def level_copy(c, p):
        return pltpu.make_async_remote_copy(
            src_ref=gw_level.at[c, level_at(p)], dst_ref=gw_levels.at[c, p - 1],
            send_sem=send_level.at[c, p - 1], recv_sem=recv_level.at[c, p - 1],
            device_id={"dp": level_at(p) * 2 + core}, device_id_type=MESH,
        )

    def seq_copy(c, p):
        device = lax.rem(me + p, peers)
        return pltpu.make_async_remote_copy(
            src_ref=gw_seq.at[c, :, pl.ds(pl.multiple_of(device * LANES, LANES), LANES)],
            dst_ref=gw_seqs.at[c, p - 1],
            send_sem=send_seq.at[c, p - 1], recv_sem=recv_seq.at[c, p - 1],
            device_id={"seq": device}, device_id_type=MESH,
        )

    def gw_partial(c):
        for p in range(1, peers):
            outward(0, c, p).wait()
        keep_own(0, c).wait()

        def up_columns(which):
            return jnp.concatenate(
                [
                    u_ref[:, pl.ds(pl.multiple_of((at * 2 + which) * LANES, LANES), LANES)]
                    for at in range(levels)
                ],
                axis=1,
            )

        def one(device, carry):
            place = pl.ds(pl.multiple_of(device * LANES, LANES), LANES)
            att = att_nodes[:, columns(device, c)]
            theirs = inner_rows(att, up_columns(1 - core)).astype(bf16)
            ours = inner_rows(att, up_columns(core))
            for at in range(levels):
                cut = slice(at * LANES, (at + 1) * LANES)
                gw_other[c, at, place, :] = theirs[:, cut]
                gw_own[c, at, place, :] = ours[:, cut]
            return carry

        lax.fori_loop(0, peers, one, 0)
        core_copy(c).start()

    own_part = pl.ds(pl.multiple_of(me * LANES, LANES), LANES)

    def gw_across_seq(c):
        core_copy(c).wait()

        def one(at, carry):
            total = gw_own[c, at] + gw_core[c, at].astype(f32)
            gw_own[c, at] = total
            gw_seq[c, at] = total.astype(bf16)
            return carry

        lax.fori_loop(0, levels, one, 0)
        for p in range(1, peers):
            seq_copy(c, p).start()

    def gw_across_levels(c):
        total = gw_own[c, :, own_part, :]
        for p in range(1, peers):
            seq_copy(c, p).wait()
            total = total + gw_seqs[c, p - 1].astype(f32)
        gw_half[c] = total
        gw_level[c] = total.astype(bf16)
        for p in range(1, levels):
            level_copy(c, p).start()

    def gw_finish(c):
        total = gw_half[c, level]
        for p in range(1, levels):
            level_copy(c, p).wait()
            total = total + gw_levels[c, p - 1].astype(f32)
        gw_ref[c * LANES:(c + 1) * LANES, :] = total * factor

    def dest_blocks(p):
        device = lax.rem(me + p, peers)
        return [device * per_device + at for at in range(per_device)]

    def rows_of(b):
        return pl.ds(pl.multiple_of(b * block_rows, block_rows), block_rows)

    def listed_rows(table, b):
        return jnp.concatenate([table[list_ref[j, b]] for j in range(listed)], axis=0)

    def run_between(p, between):
        for at, step in between:
            pl.when(p == at)(step)

    def forward(c, between):
        def one_group(step, carry):
            p = step + 1
            group = dest_blocks(p)
            lefts = []
            for b in group:
                q = head_q[c, rows_of(b), :].astype(f32) * score_scale
                count = count_ref[b]
                used = lane2 < 0
                for j in range(listed):
                    used = used | (lane2 == jnp.where(j < count, list_ref[j, b], -1))
                bias = jnp.where(used, 0.0, MASKED)
                lefts.append(jnp.concatenate([stacked(q), bias], axis=1).astype(bf16))
            scores = [dot_nt(left, listed_rows(keys2[c], b)) for left, b in zip(lefts, group)]
            tops = [jnp.max(score, axis=1, keepdims=True) for score in scores]
            weights = [jnp.exp(score - top).astype(bf16) for score, top in zip(scores, tops)]
            sums = [
                jnp.dot(weight, listed_rows(values2[c], b), preferred_element_type=f32)
                for weight, b in zip(weights, group)
            ]
            for b, weight, summed in zip(group, weights, sums):
                for j in range(listed):
                    kept_weights[c, b, j] = weight[:, j * block_rows:(j + 1) * block_rows]
                inverse = 1.0 / summed[:, LANES:LANES + 1]
                kept_inverse[c, b] = jnp.broadcast_to(inverse, (2 * block_rows, LANES))
                out_stage[c, 0, rows_of(b), :] = merged(summed[:, :LANES] * inverse).astype(bf16)

            @pl.when(p < peers)
            def _():
                outward(0, c, p).start()

            run_between(p, between)
            return carry

        lax.fori_loop(0, peers, one_group, 0)
        keep_own(0, c).start()

    def backward(c, between):
        key_sum[...] = jnp.zeros_like(key_sum)
        value_sum[...] = jnp.zeros_like(value_sum)

        def one_group(step, carry):
            p = step + 1
            group = dest_blocks(p)
            q_sides, g_sides, rights = [], [], []
            for b in group:
                inverse = kept_inverse[c, b]
                q_pair = stacked(head_q[c, rows_of(b), :].astype(f32) * score_scale)
                g_pair = stacked(head_g[c, rows_of(b), :].astype(f32))
                attended = out_stage[c, 0, rows_of(b), :].astype(f32)
                delta = jnp.sum(
                    g_pair * jnp.concatenate([attended, attended], axis=0), axis=1, keepdims=True
                )
                high = delta.astype(bf16).astype(f32)
                middle = (delta - high).astype(bf16).astype(f32)
                low = delta - high - middle
                shift = jnp.where(
                    lane2 == 0, -high,
                    jnp.where(lane2 == 1, -middle, jnp.where(lane2 == 2, -low, 0.0)),
                )
                q_sides.append((q_pair * inverse).astype(bf16))
                g_sides.append((g_pair * inverse).astype(bf16))
                rights.append(jnp.concatenate([g_pair, shift], axis=1).astype(bf16))
            shifted = [dot_nt(right, listed_rows(values2[c], b)) for right, b in zip(rights, group)]
            for at, b in enumerate(group):
                for j in range(listed):
                    cut = slice(j * block_rows, (j + 1) * block_rows)
                    kept_logits[at, j] = (
                        kept_weights[c, b, j].astype(f32) * shifted[at][:, cut]
                    ).astype(bf16)
            wide_logits, wide_weights = [], []
            for at, b in enumerate(group):
                logits = jnp.concatenate([kept_logits[at, j] for j in range(listed)], axis=1)
                grad_q = jnp.dot(
                    logits, listed_rows(keys2[c], b)[:, :LANES],
                    preferred_element_type=f32,
                )
                grad_q = merged(grad_q * (kept_inverse[c, b] * score_scale))
                out_stage[c, 1, rows_of(b), :] = grad_q.astype(bf16)
                slots = []
                for key_block in range(blocks):
                    slot = jnp.int32(listed)
                    for j in range(listed):
                        slot = jnp.where(list_ref[j, b] == key_block, j, slot)
                    slots.append(slot)
                wide_logits.append(jnp.concatenate([kept_logits[at, i] for i in slots], axis=1))
                wide_weights.append(jnp.concatenate([kept_weights[c, b, i] for i in slots], axis=1))
            key_sum[...] += inner_rows(
                jnp.concatenate(q_sides, axis=0), jnp.concatenate(wide_logits, axis=0)
            )
            value_sum[...] += inner_rows(
                jnp.concatenate(g_sides, axis=0), jnp.concatenate(wide_weights, axis=0)
            )

            @pl.when(p < peers)
            def _():
                outward(1, c, p).start()

            run_between(p, between)
            return carry

        lax.fori_loop(0, peers, one_group, 0)
        out_stage[c, 2] = key_sum[...].T.astype(bf16)
        for p in range(1, peers):
            outward(2, c, p).start()
        out_stage[c, 3] = value_sum[...].T.astype(bf16)
        for p in range(1, peers):
            outward(3, c, p).start()
        for a in range(1, 4):
            keep_own(a, c).start()

    def project():
        mixed_ref[...] = jnp.dot(
            att_nodes[...], w_ref[...], preferred_element_type=f32
        ).astype(bf16)

    for a in range(3):
        loads[a].wait()
        start_in(a, 0)
    loads[3].wait()
    loads[4].wait()
    for c in range(chunks):
        grad_att(c)
    block_of = lax.broadcasted_iota(jnp.int32, (blocks, block_rows, LANES), 0)
    node_lane = lax.broadcasted_iota(jnp.int32, (blocks, block_rows, LANES), 2)
    for c in range(chunks):
        keys2[c][:, :, LANES:] = jnp.where(node_lane == block_of, 1.0, 0.0).astype(bf16)
        values2[c][:, :, LANES:] = jnp.where(node_lane < 3, 1.0, 0.0).astype(bf16)
    nothing = jnp.zeros((2 * block_rows, block_rows), bf16)
    for c in range(chunks):
        for b in range(blocks):
            kept_weights[c, b, listed] = nothing
    for at in range(per_device):
        kept_logits[at, listed] = nothing
    last = chunks - 1
    for c in range(chunks):
        for a in range(3):
            finish_in(a, c)
            if a == 1 and c < last:
                for later in range(3):
                    start_in(later, c + 1)
            if a == 1 and c == last:
                for every in range(chunks):
                    start_in(3, every)
        between = []
        if c > 0:
            between.append((2, functools.partial(gw_partial, c - 1)))
            between.append((4, functools.partial(gw_across_seq, c - 1)))
        forward(c, between)
    for c in range(chunks):
        finish_in(3, c)
        between = []
        if c == last:
            between.append((1, functools.partial(gw_across_levels, last)))
        if c == 0:
            for early in range(last):
                between.append((1, functools.partial(gw_across_levels, early)))
            between.append((2, functools.partial(gw_partial, last)))
            between.append((3, functools.partial(gw_across_seq, last)))
            between.append((4, project))
        backward(c, between)
    stores = [
        pltpu.make_async_copy(here, there, mixed_sem.at[a])
        for a, (here, there) in enumerate(
            [(mixed_ref, mixed_hbm), (gq_ref, gq_hbm), (gk_ref, gk_hbm), (gv_ref, gv_hbm)]
        )
    ]
    stores[0].start()
    for a in range(1, 4):
        for c in range(chunks):
            for p in range(1, peers):
                outward(a, c, p).wait()
            keep_own(a, c).wait()
        stores[a].start()
    for c in range(chunks):
        gw_finish(c)
    for store in stores:
        store.wait()


def copy_out(count, *refs):
    sources, targets, held = refs[:count], refs[count:2 * count], refs[2 * count]
    loaded, stored = refs[2 * count + 1:]
    loads = [pltpu.make_async_copy(sources[i], held[i], loaded.at[i]) for i in range(count)]
    stores = [pltpu.make_async_copy(held[i], targets[i], stored.at[i]) for i in range(count)]
    for load in loads:
        load.start()
    for load, store in zip(loads, stores):
        load.wait()
        store.start()
    for store in stores:
        store.wait()


def local_fused(queries, keys, values, upstream, w_out, key_blocks, block_counts):
    rows, width = queries.shape[1:]
    peers = lax.axis_size("seq")
    chunks = width // peers // LANES
    nodes = rows * peers
    bf16, f32 = jnp.bfloat16, jnp.float32
    replicas = lax.axis_size("dp")
    levels = replicas // 2
    blocks, listed = key_blocks.shape[1:]
    block_rows = nodes // blocks
    by_block = (blocks // peers, block_rows, width)
    factor = 1.0 / math.sqrt(replicas * nodes)
    vmem = pl.BlockSpec(memory_space=pltpu.VMEM)
    anywhere = pl.BlockSpec(memory_space=pl.ANY)
    smem = pl.BlockSpec(memory_space=pltpu.SMEM)
    part = jax.ShapeDtypeStruct((rows, width), bf16)
    results = pl.pallas_call(
        functools.partial(fused, peers, levels, width // HEADS, factor),
        out_shape=(part, part, part, part, jax.ShapeDtypeStruct((chunks * LANES, width // replicas), f32)),
        in_specs=[smem, smem] + [anywhere] * 5,
        out_specs=[anywhere] * 4 + [vmem],
        scratch_shapes=[
            pltpu.VMEM((chunks, nodes, LANES), bf16),
            pltpu.VMEM((chunks, nodes, LANES), bf16),
            tuple(pltpu.VMEM((blocks, block_rows, 2 * LANES), bf16) for _ in range(chunks)),
            tuple(pltpu.VMEM((blocks, block_rows, 2 * LANES), bf16) for _ in range(chunks)),
            pltpu.VMEM((rows, width), bf16),
            pltpu.VMEM((chunks, 4, nodes, LANES), bf16),
            pltpu.VMEM((LANES, nodes), f32),
            pltpu.VMEM((LANES, nodes), f32),
            pltpu.VMEM((rows, width), bf16),
            pltpu.VMEM((chunks, blocks, listed + 1, 2 * block_rows, block_rows), bf16),
            pltpu.VMEM((chunks, blocks, 2 * block_rows, LANES), f32),
            pltpu.VMEM((blocks // peers, listed + 1, 2 * block_rows, block_rows), bf16),
            pltpu.VMEM((rows, width), bf16),
            pltpu.VMEM(by_block, bf16),
            pltpu.VMEM(by_block, bf16),
            pltpu.VMEM((rows, width), bf16),
            pltpu.VMEM((width, width), bf16),
            pltpu.VMEM((rows, width), bf16),
            pltpu.VMEM((rows, width), bf16),
            pltpu.VMEM((rows, width), bf16),
            pltpu.VMEM((rows, width), bf16),
            pltpu.VMEM((chunks, levels, peers * LANES, LANES), bf16),
            pltpu.VMEM((chunks, levels, peers * LANES, LANES), f32),
            pltpu.VMEM((chunks, levels, peers * LANES, LANES), bf16),
            pltpu.VMEM((chunks, levels, peers * LANES, LANES), bf16),
            pltpu.VMEM((chunks, peers - 1, levels, LANES, LANES), bf16),
            pltpu.VMEM((chunks, levels, LANES, LANES), f32),
            pltpu.VMEM((chunks, levels, LANES, LANES), bf16),
            pltpu.VMEM((chunks, levels - 1, LANES, LANES), bf16),
            pltpu.SemaphoreType.DMA((chunks, 4, peers - 1)),
            pltpu.SemaphoreType.DMA((chunks, 4, peers - 1)),
            pltpu.SemaphoreType.DMA((chunks, 4, peers - 1)),
            pltpu.SemaphoreType.DMA((chunks, 4, peers - 1)),
            pltpu.SemaphoreType.DMA((chunks, 4)),
            pltpu.SemaphoreType.DMA((chunks,)),
            pltpu.SemaphoreType.DMA((chunks,)),
            pltpu.SemaphoreType.DMA((chunks, levels - 1)),
            pltpu.SemaphoreType.DMA((chunks, levels - 1)),
            pltpu.SemaphoreType.DMA((chunks, peers - 1)),
            pltpu.SemaphoreType.DMA((chunks, peers - 1)),
            pltpu.SemaphoreType.DMA((5,)),
            pltpu.SemaphoreType.DMA((chunks, 4)),
            pltpu.SemaphoreType.DMA((4,)),
        ],
        compiler_params=pltpu.CompilerParams(
            collective_id=0, has_side_effects=True, vmem_limit_bytes=56 * 1024 * 1024
        ),
        name="graph_attention",
    )(
        key_blocks[0].T, block_counts[0], queries[0], keys.reshape(by_block),
        values.reshape(by_block), upstream[0], w_out,
    )
    count = len(results)
    mixed, grad_q, grad_k, grad_v, grad_wo = pl.pallas_call(
        functools.partial(copy_out, count),
        out_shape=[jax.ShapeDtypeStruct(result.shape, result.dtype) for result in results],
        in_specs=[anywhere] * count,
        out_specs=[anywhere] * count,
        scratch_shapes=[
            tuple(pltpu.VMEM(result.shape, result.dtype) for result in results),
            pltpu.SemaphoreType.DMA((count,)),
            pltpu.SemaphoreType.DMA((count,)),
        ],
        compiler_params=pltpu.CompilerParams(vmem_limit_bytes=56 * 1024 * 1024),
        name="copy_out",
    )(*results)
    return mixed[None], grad_q[None], grad_k[None], grad_v[None], grad_wo


def local(queries, keys, values, upstream, w_out, key_blocks, block_counts):
    width = queries.shape[2]
    peers = lax.axis_size("seq")
    pair = 2 * (width // HEADS) == LANES and width % (peers * LANES) == 0
    whole_blocks = key_blocks.shape[1] % peers == 0 and key_blocks.shape[1] <= LANES
    whole_blocks = whole_blocks and peers >= 4
    columns_fit = lax.axis_size("dp") * LANES == width
    chosen = local_fused if pair and whole_blocks and columns_fit else local_plain
    return chosen(queries, keys, values, upstream, w_out, key_blocks, block_counts)


def solution(mesh):
    placed = (
        P("dp", "seq", None),
        P("dp", "seq", None),
        P("dp", "seq", None),
        P("dp", "seq", None),
        P(),
        P("dp", None, None),
        P("dp", None),
    )
    return jax.shard_map(
        local,
        mesh=mesh,
        in_specs=placed,
        out_specs=(
            P("dp", "seq", None),
            P("dp", "seq", None),
            P("dp", "seq", None),
            P("dp", "seq", None),
            P("seq", "dp"),
        ),
        check_vma=False,
    )
```

```python
import functools
import math

import jax
import jax.numpy as jnp
from jax import lax
from jax.experimental import pallas as pl
from jax.experimental.pallas import tpu as pltpu
from jax.sharding import PartitionSpec as P

HEADS = 16


blocks_per_step = 4


def product(form, left, right):
    return jnp.einsum(form, left, right, preferred_element_type=jnp.float32)


def inner_rows(left, right):
    return lax.dot_general(
        left, right, (((0,), (0,)), ((), ())), preferred_element_type=jnp.float32
    )


def block_attention(head_q, head_k, head_v, head_g, key_lists, key_counts):
    node_count, head_count, head_width = head_q.shape
    block_count, listed = key_lists.shape
    block_rows = node_count // block_count
    steps_count = block_count // blocks_per_step
    score_scale = 1.0 / math.sqrt(head_width)
    query_groups = head_q.reshape(steps_count, blocks_per_step, block_rows, head_count, head_width)
    grad_groups = head_g.reshape(steps_count, blocks_per_step, block_rows, head_count, head_width)
    key_table = head_k.reshape(block_count, block_rows, head_count, head_width)
    value_table = head_v.reshape(block_count, block_rows, head_count, head_width)
    list_groups = key_lists.reshape(steps_count, blocks_per_step, listed)
    count_groups = key_counts.reshape(steps_count, blocks_per_step)
    slot_index = jnp.arange(listed, dtype=jnp.int32)

    def one_step(accumulated, inputs):
        key_acc, value_acc = accumulated
        query_part, grad_part, list_part, count_part = inputs
        keys_near = key_table[list_part]
        values_near = value_table[list_part]
        scores = product("gqnd,gjknd->gnqjk", query_part, keys_near) * score_scale
        usable = (slot_index[None, :] < count_part[:, None])[:, None, None, :, None]
        scores = jnp.where(usable, scores, -jnp.inf)
        highest = jnp.max(scores, axis=(3, 4), keepdims=True)
        raised = jnp.exp(scores - highest)
        probability = raised / jnp.sum(raised, axis=(3, 4), keepdims=True)
        weights = probability.astype(jnp.bfloat16)
        attended = product("gnqjk,gjknd->gqnd", weights, values_near).astype(jnp.bfloat16)
        row_delta = jnp.sum(grad_part.astype(jnp.float32) * attended.astype(jnp.float32), axis=3)
        grad_scores = product("gqnd,gjknd->gnqjk", grad_part, values_near)
        shifted = grad_scores - jnp.transpose(row_delta, (0, 2, 1))[:, :, :, None, None]
        grad_logits = (probability * shifted).astype(jnp.bfloat16)
        grad_query = (product("gnqjk,gjknd->gqnd", grad_logits, keys_near) * score_scale).astype(
            jnp.bfloat16
        )
        key_terms = product("gnqjk,gqnd->gjknd", grad_logits, query_part) * score_scale
        value_terms = product("gnqjk,gqnd->gjknd", weights, grad_part)
        flat_list = list_part.reshape(-1)
        key_acc = key_acc.at[flat_list].add(
            key_terms.reshape(-1, block_rows, head_count, head_width)
        )
        value_acc = value_acc.at[flat_list].add(
            value_terms.reshape(-1, block_rows, head_count, head_width)
        )
        return ((key_acc, value_acc), (attended, grad_query))

    empty = jnp.zeros((block_count, block_rows, head_count, head_width), jnp.float32)
    (key_acc, value_acc), (attended, grad_query) = lax.scan(
        one_step, (empty, empty), (query_groups, grad_groups, list_groups, count_groups)
    )
    shape = (node_count, head_count, head_width)
    return (
        attended.reshape(shape),
        grad_query.reshape(shape),
        key_acc.astype(jnp.bfloat16).reshape(shape),
        value_acc.astype(jnp.bfloat16).reshape(shape),
    )


def project_back(up_rows, w_out):
    return lax.dot_general(
        up_rows, w_out, (((1,), (1,)), ((), ())), preferred_element_type=jnp.float32
    ).astype(jnp.bfloat16)


def local_plain(queries, keys, values, upstream, w_out, key_blocks, block_counts):
    local_rows = queries.shape[1]
    width = queries.shape[2]
    head_width = width // HEADS
    up_rows = upstream[0]

    def split_heads(array):
        return array.reshape(local_rows, HEADS, head_width)

    query_heads = split_heads(queries[0])
    key_heads = split_heads(keys[0])
    value_heads = split_heads(values[0])
    grad_att = project_back(up_rows, w_out)
    head_q, head_k, head_v, head_g = (
        lax.all_to_all(query_heads, "seq", split_axis=1, concat_axis=0, tiled=True),
        lax.all_to_all(key_heads, "seq", split_axis=1, concat_axis=0, tiled=True),
        lax.all_to_all(value_heads, "seq", split_axis=1, concat_axis=0, tiled=True),
        lax.all_to_all(split_heads(grad_att), "seq", split_axis=1, concat_axis=0, tiled=True),
    )
    attended, grad_query, grad_key, grad_value = block_attention(
        head_q, head_k, head_v, head_g, key_blocks[0], block_counts[0]
    )
    node_att, node_gq, node_gk, node_gv = (
        lax.all_to_all(attended, "seq", split_axis=0, concat_axis=1, tiled=True),
        lax.all_to_all(grad_query, "seq", split_axis=0, concat_axis=1, tiled=True),
        lax.all_to_all(grad_key, "seq", split_axis=0, concat_axis=1, tiled=True),
        lax.all_to_all(grad_value, "seq", split_axis=0, concat_axis=1, tiled=True),
    )
    att_nodes = node_att.reshape(local_rows, width)
    mixed = jnp.dot(att_nodes, w_out, preferred_element_type=jnp.float32).astype(jnp.bfloat16)
    factor = 1.0 / math.sqrt(lax.axis_size("dp") * lax.axis_size("seq") * local_rows)
    summed = lax.psum_scatter(
        inner_rows(att_nodes, up_rows), "seq", scatter_dimension=0, tiled=True
    )
    grad_wo = lax.psum_scatter(summed, "dp", scatter_dimension=1, tiled=True)
    full_shape = (1, local_rows, width)
    return (
        mixed.reshape(full_shape),
        node_gq.reshape(full_shape),
        node_gk.reshape(full_shape),
        node_gv.reshape(full_shape),
        grad_wo * factor,
    )


MESH = pl.DeviceIdType.MESH
LANES = 128
MASKED = -1e30


def dot_nt(left, right):
    return lax.dot_general(
        left, right, (((1,), (1,)), ((), ())), preferred_element_type=jnp.float32
    )


def fused(
    peers, levels, head_width, factor, list_ref, count_ref, q_ref, k_ref, v_ref, u_hbm, w_hbm,
    mixed_hbm, gq_ref, gk_ref, gv_ref, gw_ref,
    head_q, head_g, keys2, values2, g_local, out_stage, key_sum, value_sum, att_nodes,
    kept_weights, kept_inverse, kept_logits, u_ref, w_ref, mixed_ref,
    gw_other, gw_own, gw_core, gw_level, gw_levels, gw_seq, gw_seqs,
    send_in, recv_in, send_out, recv_out, own_sem,
    send_core, recv_core, send_level, recv_level, send_seq, recv_seq,
    load_sem, own_out, mixed_sem,
):
    me = lax.axis_index("seq")
    replica = lax.axis_index("dp")
    core = lax.rem(replica, 2)
    level = replica // 2
    rows = q_ref.shape[0]
    chunks = head_q.shape[0]
    nodes = head_q.shape[1]
    listed, blocks = list_ref.shape
    block_rows = nodes // blocks
    per_device = blocks // peers
    span = chunks * LANES
    score_scale = 1.0 / math.sqrt(head_width)
    bf16, f32 = jnp.bfloat16, jnp.float32

    u_load = pltpu.make_async_copy(u_hbm, u_ref, load_sem.at[0])
    w_load = pltpu.make_async_copy(w_hbm, w_ref, load_sem.at[1])
    u_load.start()
    w_load.start()
    barrier = pltpu.get_barrier_semaphore()
    for p in range(1, peers):
        pl.semaphore_signal(
            barrier, inc=1, device_id={"seq": lax.rem(me + p, peers)}, device_id_type=MESH
        )
    other_core = level * 2 + 1 - core

    def level_at(p):
        return lax.rem(level + p, levels)

    pl.semaphore_signal(barrier, inc=1, device_id={"dp": other_core}, device_id_type=MESH)
    for p in range(1, levels):
        pl.semaphore_signal(
            barrier, inc=1, device_id={"dp": level_at(p) * 2 + core}, device_id_type=MESH
        )
    pl.semaphore_wait(barrier, peers + levels - 1)

    own_rows = pl.ds(pl.multiple_of(me * rows, rows), rows)

    def columns(device, c):
        return pl.ds(pl.multiple_of(device * span + c * LANES, LANES), LANES)

    sources = (q_ref, k_ref, v_ref, g_local)
    targets = (head_q, keys2, values2, head_g)

    def landing(a, c):
        if a in (1, 2):
            return targets[a][c].at[pl.ds(me * per_device, per_device), :, pl.ds(0, LANES)]
        return targets[a].at[c, own_rows]

    def leaving(a, device, c):
        if a in (1, 2):
            return sources[a].at[:, :, columns(device, c)]
        return sources[a].at[:, columns(device, c)]

    def inward(a, c, p):
        device = lax.rem(me + p, peers)
        return pltpu.make_async_remote_copy(
            src_ref=leaving(a, device, c),
            dst_ref=landing(a, c),
            send_sem=send_in.at[c, a, p - 1],
            recv_sem=recv_in.at[c, a, p - 1],
            device_id={"seq": device},
            device_id_type=MESH,
        )

    def own_copy(a, c):
        return pltpu.make_async_copy(
            leaving(a, me, c), landing(a, c), own_sem.at[c, a]
        )

    def start_in(a, c):
        for p in range(1, peers):
            inward(a, c, p).start()
        own_copy(a, c).start()

    def finish_in(a, c):
        for p in range(1, peers):
            inward(a, c, p).wait()
        own_copy(a, c).wait()

    returns = (att_nodes, gq_ref, gk_ref, gv_ref)

    def outward(a, c, p):
        device = lax.rem(me + p, peers)
        return pltpu.make_async_remote_copy(
            src_ref=out_stage.at[c, a, pl.ds(pl.multiple_of(device * rows, rows), rows)],
            dst_ref=returns[a].at[:, columns(me, c)],
            send_sem=send_out.at[c, a, p - 1],
            recv_sem=recv_out.at[c, a, p - 1],
            device_id={"seq": device},
            device_id_type=MESH,
        )

    def keep_own(a, c):
        return pltpu.make_async_copy(
            out_stage.at[c, a, own_rows], returns[a].at[:, columns(me, c)], own_out.at[c, a]
        )

    def grad_att(c):
        def one(device, carry):
            cols = columns(device, c)
            g_local[:, cols] = dot_nt(u_ref[...], w_ref[cols, :]).astype(bf16)
            return carry

        lax.fori_loop(0, peers, one, 0)

    lane = lax.broadcasted_iota(jnp.int32, (block_rows, LANES), 1)
    lane2 = lax.broadcasted_iota(jnp.int32, (2 * block_rows, LANES), 1)
    first = lane < head_width

    def stacked(x):
        return jnp.concatenate([jnp.where(first, x, 0.0), jnp.where(first, 0.0, x)], axis=0)

    def merged(x):
        return jnp.where(first, x[:block_rows], x[block_rows:])

    def core_copy(c):
        return pltpu.make_async_remote_copy(
            src_ref=gw_other.at[c], dst_ref=gw_core.at[c],
            send_sem=send_core.at[c], recv_sem=recv_core.at[c],
            device_id={"dp": other_core}, device_id_type=MESH,
        )

    def level_copy(c, p):
        return pltpu.make_async_remote_copy(
            src_ref=gw_level.at[c, level_at(p)], dst_ref=gw_levels.at[c, p - 1],
            send_sem=send_level.at[c, p - 1], recv_sem=recv_level.at[c, p - 1],
            device_id={"dp": level_at(p) * 2 + core}, device_id_type=MESH,
        )

    def seq_copy(c, p):
        device = lax.rem(me + p, peers)
        return pltpu.make_async_remote_copy(
            src_ref=gw_seq.at[c, pl.ds(pl.multiple_of(device * LANES, LANES), LANES)],
            dst_ref=gw_seqs.at[c, p - 1],
            send_sem=send_seq.at[c, p - 1], recv_sem=recv_seq.at[c, p - 1],
            device_id={"seq": device}, device_id_type=MESH,
        )

    def gw_partial(c):
        for p in range(1, peers):
            outward(0, c, p).wait()
        keep_own(0, c).wait()

        def up_columns(which):
            return jnp.concatenate(
                [
                    u_ref[:, pl.ds(pl.multiple_of((at * 2 + which) * LANES, LANES), LANES)]
                    for at in range(levels)
                ],
                axis=1,
            )

        def one(device, carry):
            place = pl.ds(pl.multiple_of(device * LANES, LANES), LANES)
            att = att_nodes[:, columns(device, c)]
            theirs = inner_rows(att, up_columns(1 - core)).astype(bf16)
            ours = inner_rows(att, up_columns(core))
            for at in range(levels):
                cut = slice(at * LANES, (at + 1) * LANES)
                gw_other[c, at, place, :] = theirs[:, cut]
                gw_own[c, at, place, :] = ours[:, cut]
            return carry

        lax.fori_loop(0, peers, one, 0)
        core_copy(c).start()

    def gw_across_levels(c):
        core_copy(c).wait()

        def one(at, carry):
            total = gw_own[c, at] + gw_core[c, at].astype(f32)
            gw_own[c, at] = total
            gw_level[c, at] = total.astype(bf16)
            return carry

        lax.fori_loop(0, levels, one, 0)
        for p in range(1, levels):
            level_copy(c, p).start()

    def gw_across_seq(c):
        total = gw_own[c, level]
        for p in range(1, levels):
            level_copy(c, p).wait()
            total = total + gw_levels[c, p - 1].astype(f32)
        gw_own[c, level] = total
        gw_seq[c] = total.astype(bf16)
        for p in range(1, peers):
            seq_copy(c, p).start()

    def gw_finish(c):
        total = gw_own[c, level, pl.ds(pl.multiple_of(me * LANES, LANES), LANES), :]
        for p in range(1, peers):
            seq_copy(c, p).wait()
            total = total + gw_seqs[c, p - 1].astype(f32)
        gw_ref[c * LANES:(c + 1) * LANES, :] = total * factor

    def dest_blocks(p):
        device = lax.rem(me + p, peers)
        return [device * per_device + at for at in range(per_device)]

    def rows_of(b):
        return pl.ds(pl.multiple_of(b * block_rows, block_rows), block_rows)

    def listed_rows(table, b):
        return jnp.concatenate([table[list_ref[j, b]] for j in range(listed)], axis=0)

    def run_between(p, between):
        for at, step in between:
            pl.when(p == at)(step)

    def forward(c, between):
        def one_group(step, carry):
            p = step + 1
            group = dest_blocks(p)
            lefts = []
            for b in group:
                q = head_q[c, rows_of(b), :].astype(f32) * score_scale
                count = count_ref[b]
                used = lane2 < 0
                for j in range(listed):
                    used = used | (lane2 == jnp.where(j < count, list_ref[j, b], -1))
                bias = jnp.where(used, 0.0, MASKED)
                lefts.append(jnp.concatenate([stacked(q), bias], axis=1).astype(bf16))
            scores = [dot_nt(left, listed_rows(keys2[c], b)) for left, b in zip(lefts, group)]
            tops = [jnp.max(score, axis=1, keepdims=True) for score in scores]
            weights = [jnp.exp(score - top).astype(bf16) for score, top in zip(scores, tops)]
            sums = [
                jnp.dot(weight, listed_rows(values2[c], b), preferred_element_type=f32)
                for weight, b in zip(weights, group)
            ]
            for b, weight, summed in zip(group, weights, sums):
                for j in range(listed):
                    kept_weights[c, b, j] = weight[:, j * block_rows:(j + 1) * block_rows]
                inverse = 1.0 / summed[:, LANES:LANES + 1]
                kept_inverse[c, b] = jnp.broadcast_to(inverse, (2 * block_rows, LANES))
                out_stage[c, 0, rows_of(b), :] = merged(summed[:, :LANES] * inverse).astype(bf16)

            @pl.when(p < peers)
            def _():
                outward(0, c, p).start()

            run_between(p, between)
            return carry

        lax.fori_loop(0, peers, one_group, 0)
        keep_own(0, c).start()

    def backward(c, between):
        key_sum[...] = jnp.zeros_like(key_sum)
        value_sum[...] = jnp.zeros_like(value_sum)

        def one_group(step, carry):
            p = step + 1
            group = dest_blocks(p)
            q_sides, g_sides, rights = [], [], []
            for b in group:
                inverse = kept_inverse[c, b]
                q_pair = stacked(head_q[c, rows_of(b), :].astype(f32) * score_scale)
                g_pair = stacked(head_g[c, rows_of(b), :].astype(f32))
                attended = out_stage[c, 0, rows_of(b), :].astype(f32)
                delta = jnp.sum(
                    g_pair * jnp.concatenate([attended, attended], axis=0), axis=1, keepdims=True
                )
                high = delta.astype(bf16).astype(f32)
                middle = (delta - high).astype(bf16).astype(f32)
                low = delta - high - middle
                shift = jnp.where(
                    lane2 == 0, -high,
                    jnp.where(lane2 == 1, -middle, jnp.where(lane2 == 2, -low, 0.0)),
                )
                q_sides.append((q_pair * inverse).astype(bf16))
                g_sides.append((g_pair * inverse).astype(bf16))
                rights.append(jnp.concatenate([g_pair, shift], axis=1).astype(bf16))
            shifted = [dot_nt(right, listed_rows(values2[c], b)) for right, b in zip(rights, group)]
            for at, b in enumerate(group):
                for j in range(listed):
                    cut = slice(j * block_rows, (j + 1) * block_rows)
                    kept_logits[at, j] = (
                        kept_weights[c, b, j].astype(f32) * shifted[at][:, cut]
                    ).astype(bf16)
            wide_logits, wide_weights = [], []
            for at, b in enumerate(group):
                logits = jnp.concatenate([kept_logits[at, j] for j in range(listed)], axis=1)
                grad_q = jnp.dot(
                    logits, listed_rows(keys2[c], b)[:, :LANES],
                    preferred_element_type=f32,
                )
                grad_q = merged(grad_q * (kept_inverse[c, b] * score_scale))
                out_stage[c, 1, rows_of(b), :] = grad_q.astype(bf16)
                slots = []
                for key_block in range(blocks):
                    slot = jnp.int32(listed)
                    for j in range(listed):
                        slot = jnp.where(list_ref[j, b] == key_block, j, slot)
                    slots.append(slot)
                wide_logits.append(jnp.concatenate([kept_logits[at, i] for i in slots], axis=1))
                wide_weights.append(jnp.concatenate([kept_weights[c, b, i] for i in slots], axis=1))
            key_sum[...] += inner_rows(
                jnp.concatenate(q_sides, axis=0), jnp.concatenate(wide_logits, axis=0)
            )
            value_sum[...] += inner_rows(
                jnp.concatenate(g_sides, axis=0), jnp.concatenate(wide_weights, axis=0)
            )

            @pl.when(p < peers)
            def _():
                outward(1, c, p).start()

            run_between(p, between)
            return carry

        lax.fori_loop(0, peers, one_group, 0)
        out_stage[c, 2] = key_sum[...].T.astype(bf16)
        for p in range(1, peers):
            outward(2, c, p).start()
        out_stage[c, 3] = value_sum[...].T.astype(bf16)
        for p in range(1, peers):
            outward(3, c, p).start()
        for a in range(1, 4):
            keep_own(a, c).start()

    def project():
        mixed_ref[...] = jnp.dot(
            att_nodes[...], w_ref[...], preferred_element_type=f32
        ).astype(bf16)
        pltpu.make_async_copy(mixed_ref, mixed_hbm, mixed_sem.at[0]).start()

    for a in range(3):
        start_in(a, 0)
    u_load.wait()
    w_load.wait()
    for c in range(chunks):
        grad_att(c)
    block_of = lax.broadcasted_iota(jnp.int32, (blocks, block_rows, LANES), 0)
    node_lane = lax.broadcasted_iota(jnp.int32, (blocks, block_rows, LANES), 2)
    for c in range(chunks):
        keys2[c][:, :, LANES:] = jnp.where(node_lane == block_of, 1.0, 0.0).astype(bf16)
        values2[c][:, :, LANES:] = jnp.where(node_lane < 3, 1.0, 0.0).astype(bf16)
    nothing = jnp.zeros((2 * block_rows, block_rows), bf16)
    for c in range(chunks):
        for b in range(blocks):
            kept_weights[c, b, listed] = nothing
    for at in range(per_device):
        kept_logits[at, listed] = nothing
    for c in range(chunks):
        for a in range(3):
            finish_in(a, c)
            if a == 1:
                if c + 1 < chunks:
                    for later in range(3):
                        start_in(later, c + 1)
                else:
                    for every in range(chunks):
                        start_in(3, every)
        between = []
        if c > 0:
            between.append((2, functools.partial(gw_partial, c - 1)))
            between.append((4, functools.partial(gw_across_levels, c - 1)))
        forward(c, between)
    last = chunks - 1
    for c in range(chunks):
        finish_in(3, c)
        between = []
        if c == 0:
            between.append((2, functools.partial(gw_partial, last)))
            between.append((3, functools.partial(gw_across_levels, last)))
            between.append((4, project))
        else:
            between.append((3, functools.partial(gw_across_seq, c - 1)))
        backward(c, between)
    gw_across_seq(last)
    for c in range(chunks):
        gw_finish(c)
    pltpu.make_async_copy(mixed_ref, mixed_hbm, mixed_sem.at[0]).wait()
    for c in range(chunks):
        for a in range(1, 4):
            for p in range(1, peers):
                outward(a, c, p).wait()
            keep_own(a, c).wait()


def copy_out(count, *refs):
    sources, targets, held = refs[:count], refs[count:2 * count], refs[2 * count]
    loaded, stored = refs[2 * count + 1:]
    loads = [pltpu.make_async_copy(sources[i], held[i], loaded.at[i]) for i in range(count)]
    stores = [pltpu.make_async_copy(held[i], targets[i], stored.at[i]) for i in range(count)]
    for load in loads:
        load.start()
    for load, store in zip(loads, stores):
        load.wait()
        store.start()
    for store in stores:
        store.wait()


def local_fused(queries, keys, values, upstream, w_out, key_blocks, block_counts):
    rows, width = queries.shape[1:]
    peers = lax.axis_size("seq")
    chunks = width // peers // LANES
    nodes = rows * peers
    bf16, f32 = jnp.bfloat16, jnp.float32
    replicas = lax.axis_size("dp")
    levels = replicas // 2
    blocks, listed = key_blocks.shape[1:]
    block_rows = nodes // blocks
    by_block = (blocks // peers, block_rows, width)
    factor = 1.0 / math.sqrt(replicas * nodes)
    vmem = pl.BlockSpec(memory_space=pltpu.VMEM)
    anywhere = pl.BlockSpec(memory_space=pl.ANY)
    smem = pl.BlockSpec(memory_space=pltpu.SMEM)
    part = jax.ShapeDtypeStruct((rows, width), bf16)
    results = pl.pallas_call(
        functools.partial(fused, peers, levels, width // HEADS, factor),
        out_shape=(part, part, part, part, jax.ShapeDtypeStruct((chunks * LANES, width // replicas), f32)),
        in_specs=[smem, smem] + [anywhere] * 5,
        out_specs=[anywhere] * 4 + [vmem],
        scratch_shapes=[
            pltpu.VMEM((chunks, nodes, LANES), bf16),
            pltpu.VMEM((chunks, nodes, LANES), bf16),
            tuple(pltpu.VMEM((blocks, block_rows, 2 * LANES), bf16) for _ in range(chunks)),
            tuple(pltpu.VMEM((blocks, block_rows, 2 * LANES), bf16) for _ in range(chunks)),
            pltpu.VMEM((rows, width), bf16),
            pltpu.VMEM((chunks, 4, nodes, LANES), bf16),
            pltpu.VMEM((LANES, nodes), f32),
            pltpu.VMEM((LANES, nodes), f32),
            pltpu.VMEM((rows, width), bf16),
            pltpu.VMEM((chunks, blocks, listed + 1, 2 * block_rows, block_rows), bf16),
            pltpu.VMEM((chunks, blocks, 2 * block_rows, LANES), f32),
            pltpu.VMEM((blocks // peers, listed + 1, 2 * block_rows, block_rows), bf16),
            pltpu.VMEM((rows, width), bf16),
            pltpu.VMEM((width, width), bf16),
            pltpu.VMEM((rows, width), bf16),
            pltpu.VMEM((chunks, levels, peers * LANES, LANES), bf16),
            pltpu.VMEM((chunks, levels, peers * LANES, LANES), f32),
            pltpu.VMEM((chunks, levels, peers * LANES, LANES), bf16),
            pltpu.VMEM((chunks, levels, peers * LANES, LANES), bf16),
            pltpu.VMEM((chunks, levels - 1, peers * LANES, LANES), bf16),
            pltpu.VMEM((chunks, peers * LANES, LANES), bf16),
            pltpu.VMEM((chunks, peers - 1, LANES, LANES), bf16),
            pltpu.SemaphoreType.DMA((chunks, 4, peers - 1)),
            pltpu.SemaphoreType.DMA((chunks, 4, peers - 1)),
            pltpu.SemaphoreType.DMA((chunks, 4, peers - 1)),
            pltpu.SemaphoreType.DMA((chunks, 4, peers - 1)),
            pltpu.SemaphoreType.DMA((chunks, 4)),
            pltpu.SemaphoreType.DMA((chunks,)),
            pltpu.SemaphoreType.DMA((chunks,)),
            pltpu.SemaphoreType.DMA((chunks, levels - 1)),
            pltpu.SemaphoreType.DMA((chunks, levels - 1)),
            pltpu.SemaphoreType.DMA((chunks, peers - 1)),
            pltpu.SemaphoreType.DMA((chunks, peers - 1)),
            pltpu.SemaphoreType.DMA((2,)),
            pltpu.SemaphoreType.DMA((chunks, 4)),
            pltpu.SemaphoreType.DMA((1,)),
        ],
        compiler_params=pltpu.CompilerParams(
            collective_id=0, has_side_effects=True, vmem_limit_bytes=56 * 1024 * 1024
        ),
        name="graph_attention",
    )(
        key_blocks[0].T, block_counts[0], queries[0], keys.reshape(by_block),
        values.reshape(by_block), upstream[0], w_out,
    )
    count = len(results)
    mixed, grad_q, grad_k, grad_v, grad_wo = pl.pallas_call(
        functools.partial(copy_out, count),
        out_shape=[jax.ShapeDtypeStruct(result.shape, result.dtype) for result in results],
        in_specs=[anywhere] * count,
        out_specs=[anywhere] * count,
        scratch_shapes=[
            tuple(pltpu.VMEM(result.shape, result.dtype) for result in results),
            pltpu.SemaphoreType.DMA((count,)),
            pltpu.SemaphoreType.DMA((count,)),
        ],
        compiler_params=pltpu.CompilerParams(vmem_limit_bytes=56 * 1024 * 1024),
        name="copy_out",
    )(*results)
    return mixed[None], grad_q[None], grad_k[None], grad_v[None], grad_wo


def local(queries, keys, values, upstream, w_out, key_blocks, block_counts):
    width = queries.shape[2]
    peers = lax.axis_size("seq")
    pair = 2 * (width // HEADS) == LANES and width % (peers * LANES) == 0
    whole_blocks = key_blocks.shape[1] % peers == 0 and key_blocks.shape[1] <= LANES
    whole_blocks = whole_blocks and peers >= 4
    columns_fit = lax.axis_size("dp") * LANES == width
    chosen = local_fused if pair and whole_blocks and columns_fit else local_plain
    return chosen(queries, keys, values, upstream, w_out, key_blocks, block_counts)


def solution(mesh):
    placed = (
        P("dp", "seq", None),
        P("dp", "seq", None),
        P("dp", "seq", None),
        P("dp", "seq", None),
        P(),
        P("dp", None, None),
        P("dp", None),
    )
    return jax.shard_map(
        local,
        mesh=mesh,
        in_specs=placed,
        out_specs=(
            P("dp", "seq", None),
            P("dp", "seq", None),
            P("dp", "seq", None),
            P("dp", "seq", None),
            P("seq", "dp"),
        ),
        check_vma=False,
    )
```

```python
import functools
import math

import jax
import jax.numpy as jnp
from jax import lax
from jax.experimental import pallas as pl
from jax.experimental.pallas import tpu as pltpu
from jax.sharding import PartitionSpec as P

HEADS = 16


blocks_per_step = 4


def product(form, left, right):
    return jnp.einsum(form, left, right, preferred_element_type=jnp.float32)


def inner_rows(left, right):
    return lax.dot_general(
        left, right, (((0,), (0,)), ((), ())), preferred_element_type=jnp.float32
    )


def block_attention(head_q, head_k, head_v, head_g, key_lists, key_counts):
    node_count, head_count, head_width = head_q.shape
    block_count, listed = key_lists.shape
    block_rows = node_count // block_count
    steps_count = block_count // blocks_per_step
    score_scale = 1.0 / math.sqrt(head_width)
    query_groups = head_q.reshape(steps_count, blocks_per_step, block_rows, head_count, head_width)
    grad_groups = head_g.reshape(steps_count, blocks_per_step, block_rows, head_count, head_width)
    key_table = head_k.reshape(block_count, block_rows, head_count, head_width)
    value_table = head_v.reshape(block_count, block_rows, head_count, head_width)
    list_groups = key_lists.reshape(steps_count, blocks_per_step, listed)
    count_groups = key_counts.reshape(steps_count, blocks_per_step)
    slot_index = jnp.arange(listed, dtype=jnp.int32)

    def one_step(accumulated, inputs):
        key_acc, value_acc = accumulated
        query_part, grad_part, list_part, count_part = inputs
        keys_near = key_table[list_part]
        values_near = value_table[list_part]
        scores = product("gqnd,gjknd->gnqjk", query_part, keys_near) * score_scale
        usable = (slot_index[None, :] < count_part[:, None])[:, None, None, :, None]
        scores = jnp.where(usable, scores, -jnp.inf)
        highest = jnp.max(scores, axis=(3, 4), keepdims=True)
        raised = jnp.exp(scores - highest)
        probability = raised / jnp.sum(raised, axis=(3, 4), keepdims=True)
        weights = probability.astype(jnp.bfloat16)
        attended = product("gnqjk,gjknd->gqnd", weights, values_near).astype(jnp.bfloat16)
        row_delta = jnp.sum(grad_part.astype(jnp.float32) * attended.astype(jnp.float32), axis=3)
        grad_scores = product("gqnd,gjknd->gnqjk", grad_part, values_near)
        shifted = grad_scores - jnp.transpose(row_delta, (0, 2, 1))[:, :, :, None, None]
        grad_logits = (probability * shifted).astype(jnp.bfloat16)
        grad_query = (product("gnqjk,gjknd->gqnd", grad_logits, keys_near) * score_scale).astype(
            jnp.bfloat16
        )
        key_terms = product("gnqjk,gqnd->gjknd", grad_logits, query_part) * score_scale
        value_terms = product("gnqjk,gqnd->gjknd", weights, grad_part)
        flat_list = list_part.reshape(-1)
        key_acc = key_acc.at[flat_list].add(
            key_terms.reshape(-1, block_rows, head_count, head_width)
        )
        value_acc = value_acc.at[flat_list].add(
            value_terms.reshape(-1, block_rows, head_count, head_width)
        )
        return ((key_acc, value_acc), (attended, grad_query))

    empty = jnp.zeros((block_count, block_rows, head_count, head_width), jnp.float32)
    (key_acc, value_acc), (attended, grad_query) = lax.scan(
        one_step, (empty, empty), (query_groups, grad_groups, list_groups, count_groups)
    )
    shape = (node_count, head_count, head_width)
    return (
        attended.reshape(shape),
        grad_query.reshape(shape),
        key_acc.astype(jnp.bfloat16).reshape(shape),
        value_acc.astype(jnp.bfloat16).reshape(shape),
    )


def project_back(up_rows, w_out):
    return lax.dot_general(
        up_rows, w_out, (((1,), (1,)), ((), ())), preferred_element_type=jnp.float32
    ).astype(jnp.bfloat16)


def local_plain(queries, keys, values, upstream, w_out, key_blocks, block_counts):
    local_rows = queries.shape[1]
    width = queries.shape[2]
    head_width = width // HEADS
    up_rows = upstream[0]

    def split_heads(array):
        return array.reshape(local_rows, HEADS, head_width)

    query_heads = split_heads(queries[0])
    key_heads = split_heads(keys[0])
    value_heads = split_heads(values[0])
    grad_att = project_back(up_rows, w_out)
    head_q, head_k, head_v, head_g = (
        lax.all_to_all(query_heads, "seq", split_axis=1, concat_axis=0, tiled=True),
        lax.all_to_all(key_heads, "seq", split_axis=1, concat_axis=0, tiled=True),
        lax.all_to_all(value_heads, "seq", split_axis=1, concat_axis=0, tiled=True),
        lax.all_to_all(split_heads(grad_att), "seq", split_axis=1, concat_axis=0, tiled=True),
    )
    attended, grad_query, grad_key, grad_value = block_attention(
        head_q, head_k, head_v, head_g, key_blocks[0], block_counts[0]
    )
    node_att, node_gq, node_gk, node_gv = (
        lax.all_to_all(attended, "seq", split_axis=0, concat_axis=1, tiled=True),
        lax.all_to_all(grad_query, "seq", split_axis=0, concat_axis=1, tiled=True),
        lax.all_to_all(grad_key, "seq", split_axis=0, concat_axis=1, tiled=True),
        lax.all_to_all(grad_value, "seq", split_axis=0, concat_axis=1, tiled=True),
    )
    att_nodes = node_att.reshape(local_rows, width)
    mixed = jnp.dot(att_nodes, w_out, preferred_element_type=jnp.float32).astype(jnp.bfloat16)
    factor = 1.0 / math.sqrt(lax.axis_size("dp") * lax.axis_size("seq") * local_rows)
    summed = lax.psum_scatter(
        inner_rows(att_nodes, up_rows), "seq", scatter_dimension=0, tiled=True
    )
    grad_wo = lax.psum_scatter(summed, "dp", scatter_dimension=1, tiled=True)
    full_shape = (1, local_rows, width)
    return (
        mixed.reshape(full_shape),
        node_gq.reshape(full_shape),
        node_gk.reshape(full_shape),
        node_gv.reshape(full_shape),
        grad_wo * factor,
    )


MESH = pl.DeviceIdType.MESH
LANES = 128
MASKED = -1e30


def dot_nt(left, right):
    return lax.dot_general(
        left, right, (((1,), (1,)), ((), ())), preferred_element_type=jnp.float32
    )


def fused(
    peers, levels, head_width, factor, list_ref, count_ref, q_ref, k_ref, v_ref, u_hbm, w_hbm,
    mixed_hbm, gq_ref, gk_ref, gv_ref, gw_ref,
    head_q, head_g, keys2, values2, g_local, out_stage, key_sum, value_sum, att_nodes,
    kept_weights, kept_inverse, kept_logits, u_ref, w_ref, mixed_ref,
    gw_other, gw_own, gw_core, gw_level, gw_levels, gw_seq, gw_seqs,
    send_in, recv_in, send_out, recv_out, own_sem,
    send_core, recv_core, send_level, recv_level, send_seq, recv_seq,
    load_sem, own_out, mixed_sem,
):
    me = lax.axis_index("seq")
    replica = lax.axis_index("dp")
    core = lax.rem(replica, 2)
    level = replica // 2
    rows = q_ref.shape[0]
    chunks = head_q.shape[0]
    nodes = head_q.shape[1]
    listed, blocks = list_ref.shape
    block_rows = nodes // blocks
    per_device = blocks // peers
    span = chunks * LANES
    score_scale = 1.0 / math.sqrt(head_width)
    bf16, f32 = jnp.bfloat16, jnp.float32

    u_load = pltpu.make_async_copy(u_hbm, u_ref, load_sem.at[0])
    w_load = pltpu.make_async_copy(w_hbm, w_ref, load_sem.at[1])
    u_load.start()
    w_load.start()
    barrier = pltpu.get_barrier_semaphore()
    for p in range(1, peers):
        pl.semaphore_signal(
            barrier, inc=1, device_id={"seq": lax.rem(me + p, peers)}, device_id_type=MESH
        )
    other_core = level * 2 + 1 - core

    def level_at(p):
        return lax.rem(level + p, levels)

    pl.semaphore_signal(barrier, inc=1, device_id={"dp": other_core}, device_id_type=MESH)
    for p in range(1, levels):
        pl.semaphore_signal(
            barrier, inc=1, device_id={"dp": level_at(p) * 2 + core}, device_id_type=MESH
        )
    pl.semaphore_wait(barrier, peers + levels - 1)

    own_rows = pl.ds(pl.multiple_of(me * rows, rows), rows)

    def columns(device, c):
        return pl.ds(pl.multiple_of(device * span + c * LANES, LANES), LANES)

    sources = (q_ref, k_ref, v_ref, g_local)
    targets = (head_q, keys2, values2, head_g)

    def landing(a, c):
        if a in (1, 2):
            return targets[a][c].at[pl.ds(me * per_device, per_device), :, pl.ds(0, LANES)]
        return targets[a].at[c, own_rows]

    def leaving(a, device, c):
        if a in (1, 2):
            return sources[a].at[:, :, columns(device, c)]
        return sources[a].at[:, columns(device, c)]

    def inward(a, c, p):
        device = lax.rem(me + p, peers)
        return pltpu.make_async_remote_copy(
            src_ref=leaving(a, device, c),
            dst_ref=landing(a, c),
            send_sem=send_in.at[c, a, p - 1],
            recv_sem=recv_in.at[c, a, p - 1],
            device_id={"seq": device},
            device_id_type=MESH,
        )

    def own_copy(a, c):
        return pltpu.make_async_copy(
            leaving(a, me, c), landing(a, c), own_sem.at[c, a]
        )

    def start_in(a, c):
        for p in range(1, peers):
            inward(a, c, p).start()
        own_copy(a, c).start()

    def finish_in(a, c):
        for p in range(1, peers):
            inward(a, c, p).wait()
        own_copy(a, c).wait()

    returns = (att_nodes, gq_ref, gk_ref, gv_ref)

    def outward(a, c, p):
        device = lax.rem(me + p, peers)
        return pltpu.make_async_remote_copy(
            src_ref=out_stage.at[c, a, pl.ds(pl.multiple_of(device * rows, rows), rows)],
            dst_ref=returns[a].at[:, columns(me, c)],
            send_sem=send_out.at[c, a, p - 1],
            recv_sem=recv_out.at[c, a, p - 1],
            device_id={"seq": device},
            device_id_type=MESH,
        )

    def keep_own(a, c):
        return pltpu.make_async_copy(
            out_stage.at[c, a, own_rows], returns[a].at[:, columns(me, c)], own_out.at[c, a]
        )

    def grad_att(c):
        def one(device, carry):
            cols = columns(device, c)
            g_local[:, cols] = dot_nt(u_ref[...], w_ref[cols, :]).astype(bf16)
            return carry

        lax.fori_loop(0, peers, one, 0)

    lane = lax.broadcasted_iota(jnp.int32, (block_rows, LANES), 1)
    lane2 = lax.broadcasted_iota(jnp.int32, (2 * block_rows, LANES), 1)
    first = lane < head_width

    def stacked(x):
        return jnp.concatenate([jnp.where(first, x, 0.0), jnp.where(first, 0.0, x)], axis=0)

    def merged(x):
        return jnp.where(first, x[:block_rows], x[block_rows:])

    def core_copy(c):
        return pltpu.make_async_remote_copy(
            src_ref=gw_other.at[c], dst_ref=gw_core.at[c],
            send_sem=send_core.at[c], recv_sem=recv_core.at[c],
            device_id={"dp": other_core}, device_id_type=MESH,
        )

    def level_copy(c, p):
        return pltpu.make_async_remote_copy(
            src_ref=gw_level.at[c, level_at(p)], dst_ref=gw_levels.at[c, p - 1],
            send_sem=send_level.at[c, p - 1], recv_sem=recv_level.at[c, p - 1],
            device_id={"dp": level_at(p) * 2 + core}, device_id_type=MESH,
        )

    def seq_copy(c, p):
        device = lax.rem(me + p, peers)
        return pltpu.make_async_remote_copy(
            src_ref=gw_seq.at[c, pl.ds(pl.multiple_of(device * LANES, LANES), LANES)],
            dst_ref=gw_seqs.at[c, p - 1],
            send_sem=send_seq.at[c, p - 1], recv_sem=recv_seq.at[c, p - 1],
            device_id={"seq": device}, device_id_type=MESH,
        )

    def gw_partial(c):
        for p in range(1, peers):
            outward(0, c, p).wait()
        keep_own(0, c).wait()

        def up_columns(which):
            return jnp.concatenate(
                [
                    u_ref[:, pl.ds(pl.multiple_of((at * 2 + which) * LANES, LANES), LANES)]
                    for at in range(levels)
                ],
                axis=1,
            )

        def one(device, carry):
            place = pl.ds(pl.multiple_of(device * LANES, LANES), LANES)
            att = att_nodes[:, columns(device, c)]
            theirs = inner_rows(att, up_columns(1 - core)).astype(bf16)
            ours = inner_rows(att, up_columns(core))
            for at in range(levels):
                cut = slice(at * LANES, (at + 1) * LANES)
                gw_other[c, at, place, :] = theirs[:, cut]
                gw_own[c, at, place, :] = ours[:, cut]
            return carry

        lax.fori_loop(0, peers, one, 0)
        core_copy(c).start()

    def gw_across_levels(c):
        core_copy(c).wait()

        def one(at, carry):
            total = gw_own[c, at] + gw_core[c, at].astype(f32)
            gw_own[c, at] = total
            gw_level[c, at] = total.astype(bf16)
            return carry

        lax.fori_loop(0, levels, one, 0)
        for p in range(1, levels):
            level_copy(c, p).start()

    def gw_across_seq(c):
        total = gw_own[c, level]
        for p in range(1, levels):
            level_copy(c, p).wait()
            total = total + gw_levels[c, p - 1].astype(f32)
        gw_own[c, level] = total
        gw_seq[c] = total.astype(bf16)
        for p in range(1, peers):
            seq_copy(c, p).start()

    def gw_finish(c):
        total = gw_own[c, level, pl.ds(pl.multiple_of(me * LANES, LANES), LANES), :]
        for p in range(1, peers):
            seq_copy(c, p).wait()
            total = total + gw_seqs[c, p - 1].astype(f32)
        gw_ref[c * LANES:(c + 1) * LANES, :] = total * factor

    def dest_blocks(p):
        device = lax.rem(me + p, peers)
        return [device * per_device + at for at in range(per_device)]

    def rows_of(b):
        return pl.ds(pl.multiple_of(b * block_rows, block_rows), block_rows)

    def listed_rows(table, b):
        return jnp.concatenate([table[list_ref[j, b]] for j in range(listed)], axis=0)

    def run_between(p, between):
        for at, step in between:
            pl.when(p == at)(step)

    def forward(c, between):
        def one_group(step, carry):
            p = step + 1
            group = dest_blocks(p)
            lefts = []
            for b in group:
                q = head_q[c, rows_of(b), :].astype(f32) * score_scale
                count = count_ref[b]
                used = lane2 < 0
                for j in range(listed):
                    used = used | (lane2 == jnp.where(j < count, list_ref[j, b], -1))
                bias = jnp.where(used, 0.0, MASKED)
                lefts.append(jnp.concatenate([stacked(q), bias], axis=1).astype(bf16))
            scores = [dot_nt(left, listed_rows(keys2[c], b)) for left, b in zip(lefts, group)]
            tops = [jnp.max(score, axis=1, keepdims=True) for score in scores]
            weights = [jnp.exp(score - top).astype(bf16) for score, top in zip(scores, tops)]
            sums = [
                jnp.dot(weight, listed_rows(values2[c], b), preferred_element_type=f32)
                for weight, b in zip(weights, group)
            ]
            for b, weight, summed in zip(group, weights, sums):
                for j in range(listed):
                    kept_weights[c, b, j] = weight[:, j * block_rows:(j + 1) * block_rows]
                inverse = 1.0 / summed[:, LANES:LANES + 1]
                kept_inverse[c, b] = jnp.broadcast_to(inverse, (2 * block_rows, LANES))
                out_stage[c, 0, rows_of(b), :] = merged(summed[:, :LANES] * inverse).astype(bf16)

            @pl.when(p < peers)
            def _():
                outward(0, c, p).start()

            run_between(p, between)
            return carry

        lax.fori_loop(0, peers, one_group, 0)
        keep_own(0, c).start()

    def backward(c, between):
        key_sum[...] = jnp.zeros_like(key_sum)
        value_sum[...] = jnp.zeros_like(value_sum)

        def one_group(step, carry):
            p = step + 1
            group = dest_blocks(p)
            q_sides, g_sides, rights = [], [], []
            for b in group:
                inverse = kept_inverse[c, b]
                q_pair = stacked(head_q[c, rows_of(b), :].astype(f32) * score_scale)
                g_pair = stacked(head_g[c, rows_of(b), :].astype(f32))
                attended = out_stage[c, 0, rows_of(b), :].astype(f32)
                delta = jnp.sum(
                    g_pair * jnp.concatenate([attended, attended], axis=0), axis=1, keepdims=True
                )
                high = delta.astype(bf16).astype(f32)
                middle = (delta - high).astype(bf16).astype(f32)
                low = delta - high - middle
                shift = jnp.where(
                    lane2 == 0, -high,
                    jnp.where(lane2 == 1, -middle, jnp.where(lane2 == 2, -low, 0.0)),
                )
                q_sides.append((q_pair * inverse).astype(bf16))
                g_sides.append((g_pair * inverse).astype(bf16))
                rights.append(jnp.concatenate([g_pair, shift], axis=1).astype(bf16))
            shifted = [dot_nt(right, listed_rows(values2[c], b)) for right, b in zip(rights, group)]
            for at, b in enumerate(group):
                for j in range(listed):
                    cut = slice(j * block_rows, (j + 1) * block_rows)
                    kept_logits[at, j] = (
                        kept_weights[c, b, j].astype(f32) * shifted[at][:, cut]
                    ).astype(bf16)
            wide_logits, wide_weights = [], []
            for at, b in enumerate(group):
                logits = jnp.concatenate([kept_logits[at, j] for j in range(listed)], axis=1)
                grad_q = jnp.dot(
                    logits, listed_rows(keys2[c], b)[:, :LANES],
                    preferred_element_type=f32,
                )
                grad_q = merged(grad_q * (kept_inverse[c, b] * score_scale))
                out_stage[c, 1, rows_of(b), :] = grad_q.astype(bf16)
                slots = []
                for key_block in range(blocks):
                    slot = jnp.int32(listed)
                    for j in range(listed):
                        slot = jnp.where(list_ref[j, b] == key_block, j, slot)
                    slots.append(slot)
                wide_logits.append(jnp.concatenate([kept_logits[at, i] for i in slots], axis=1))
                wide_weights.append(jnp.concatenate([kept_weights[c, b, i] for i in slots], axis=1))
            key_sum[...] += inner_rows(
                jnp.concatenate(q_sides, axis=0), jnp.concatenate(wide_logits, axis=0)
            )
            value_sum[...] += inner_rows(
                jnp.concatenate(g_sides, axis=0), jnp.concatenate(wide_weights, axis=0)
            )

            @pl.when(p < peers)
            def _():
                outward(1, c, p).start()

            run_between(p, between)
            return carry

        lax.fori_loop(0, peers, one_group, 0)
        out_stage[c, 2] = key_sum[...].T.astype(bf16)
        for p in range(1, peers):
            outward(2, c, p).start()
        out_stage[c, 3] = value_sum[...].T.astype(bf16)
        for p in range(1, peers):
            outward(3, c, p).start()
        for a in range(1, 4):
            keep_own(a, c).start()

    def project():
        mixed_ref[...] = jnp.dot(
            att_nodes[...], w_ref[...], preferred_element_type=f32
        ).astype(bf16)
        pltpu.make_async_copy(mixed_ref, mixed_hbm, mixed_sem.at[0]).start()

    for a in range(3):
        start_in(a, 0)
    u_load.wait()
    w_load.wait()
    for c in range(chunks):
        grad_att(c)
    block_of = lax.broadcasted_iota(jnp.int32, (blocks, block_rows, LANES), 0)
    node_lane = lax.broadcasted_iota(jnp.int32, (blocks, block_rows, LANES), 2)
    for c in range(chunks):
        keys2[c][:, :, LANES:] = jnp.where(node_lane == block_of, 1.0, 0.0).astype(bf16)
        values2[c][:, :, LANES:] = jnp.where(node_lane < 3, 1.0, 0.0).astype(bf16)
    nothing = jnp.zeros((2 * block_rows, block_rows), bf16)
    for c in range(chunks):
        for b in range(blocks):
            kept_weights[c, b, listed] = nothing
    for at in range(per_device):
        kept_logits[at, listed] = nothing
    for c in range(chunks):
        for a in range(3):
            finish_in(a, c)
            if a == 1 and c + 1 < chunks:
                for later in range(3):
                    start_in(later, c + 1)
        between = []
        if c == 0:
            for every in range(chunks):
                between.append((2, functools.partial(start_in, 3, every)))
        if c > 0:
            between.append((2, functools.partial(gw_partial, c - 1)))
            between.append((4, functools.partial(gw_across_levels, c - 1)))
        forward(c, between)
    last = chunks - 1
    for c in range(chunks):
        finish_in(3, c)
        between = []
        if c == 0:
            between.append((2, functools.partial(gw_partial, last)))
            between.append((3, functools.partial(gw_across_levels, last)))
            between.append((4, project))
        else:
            between.append((3, functools.partial(gw_across_seq, c - 1)))
        backward(c, between)
    gw_across_seq(last)
    for c in range(chunks):
        gw_finish(c)
    pltpu.make_async_copy(mixed_ref, mixed_hbm, mixed_sem.at[0]).wait()
    for c in range(chunks):
        for a in range(1, 4):
            for p in range(1, peers):
                outward(a, c, p).wait()
            keep_own(a, c).wait()


def copy_out(count, *refs):
    sources, targets, held = refs[:count], refs[count:2 * count], refs[2 * count]
    loaded, stored = refs[2 * count + 1:]
    loads = [pltpu.make_async_copy(sources[i], held[i], loaded.at[i]) for i in range(count)]
    stores = [pltpu.make_async_copy(held[i], targets[i], stored.at[i]) for i in range(count)]
    for load in loads:
        load.start()
    for load, store in zip(loads, stores):
        load.wait()
        store.start()
    for store in stores:
        store.wait()


def local_fused(queries, keys, values, upstream, w_out, key_blocks, block_counts):
    rows, width = queries.shape[1:]
    peers = lax.axis_size("seq")
    chunks = width // peers // LANES
    nodes = rows * peers
    bf16, f32 = jnp.bfloat16, jnp.float32
    replicas = lax.axis_size("dp")
    levels = replicas // 2
    blocks, listed = key_blocks.shape[1:]
    block_rows = nodes // blocks
    by_block = (blocks // peers, block_rows, width)
    factor = 1.0 / math.sqrt(replicas * nodes)
    vmem = pl.BlockSpec(memory_space=pltpu.VMEM)
    anywhere = pl.BlockSpec(memory_space=pl.ANY)
    smem = pl.BlockSpec(memory_space=pltpu.SMEM)
    part = jax.ShapeDtypeStruct((rows, width), bf16)
    results = pl.pallas_call(
        functools.partial(fused, peers, levels, width // HEADS, factor),
        out_shape=(part, part, part, part, jax.ShapeDtypeStruct((chunks * LANES, width // replicas), f32)),
        in_specs=[smem, smem] + [anywhere] * 5,
        out_specs=[anywhere] * 4 + [vmem],
        scratch_shapes=[
            pltpu.VMEM((chunks, nodes, LANES), bf16),
            pltpu.VMEM((chunks, nodes, LANES), bf16),
            tuple(pltpu.VMEM((blocks, block_rows, 2 * LANES), bf16) for _ in range(chunks)),
            tuple(pltpu.VMEM((blocks, block_rows, 2 * LANES), bf16) for _ in range(chunks)),
            pltpu.VMEM((rows, width), bf16),
            pltpu.VMEM((chunks, 4, nodes, LANES), bf16),
            pltpu.VMEM((LANES, nodes), f32),
            pltpu.VMEM((LANES, nodes), f32),
            pltpu.VMEM((rows, width), bf16),
            pltpu.VMEM((chunks, blocks, listed + 1, 2 * block_rows, block_rows), bf16),
            pltpu.VMEM((chunks, blocks, 2 * block_rows, LANES), f32),
            pltpu.VMEM((blocks // peers, listed + 1, 2 * block_rows, block_rows), bf16),
            pltpu.VMEM((rows, width), bf16),
            pltpu.VMEM((width, width), bf16),
            pltpu.VMEM((rows, width), bf16),
            pltpu.VMEM((chunks, levels, peers * LANES, LANES), bf16),
            pltpu.VMEM((chunks, levels, peers * LANES, LANES), f32),
            pltpu.VMEM((chunks, levels, peers * LANES, LANES), bf16),
            pltpu.VMEM((chunks, levels, peers * LANES, LANES), bf16),
            pltpu.VMEM((chunks, levels - 1, peers * LANES, LANES), bf16),
            pltpu.VMEM((chunks, peers * LANES, LANES), bf16),
            pltpu.VMEM((chunks, peers - 1, LANES, LANES), bf16),
            pltpu.SemaphoreType.DMA((chunks, 4, peers - 1)),
            pltpu.SemaphoreType.DMA((chunks, 4, peers - 1)),
            pltpu.SemaphoreType.DMA((chunks, 4, peers - 1)),
            pltpu.SemaphoreType.DMA((chunks, 4, peers - 1)),
            pltpu.SemaphoreType.DMA((chunks, 4)),
            pltpu.SemaphoreType.DMA((chunks,)),
            pltpu.SemaphoreType.DMA((chunks,)),
            pltpu.SemaphoreType.DMA((chunks, levels - 1)),
            pltpu.SemaphoreType.DMA((chunks, levels - 1)),
            pltpu.SemaphoreType.DMA((chunks, peers - 1)),
            pltpu.SemaphoreType.DMA((chunks, peers - 1)),
            pltpu.SemaphoreType.DMA((2,)),
            pltpu.SemaphoreType.DMA((chunks, 4)),
            pltpu.SemaphoreType.DMA((1,)),
        ],
        compiler_params=pltpu.CompilerParams(
            collective_id=0, has_side_effects=True, vmem_limit_bytes=56 * 1024 * 1024
        ),
        name="graph_attention",
    )(
        key_blocks[0].T, block_counts[0], queries[0], keys.reshape(by_block),
        values.reshape(by_block), upstream[0], w_out,
    )
    count = len(results)
    mixed, grad_q, grad_k, grad_v, grad_wo = pl.pallas_call(
        functools.partial(copy_out, count),
        out_shape=[jax.ShapeDtypeStruct(result.shape, result.dtype) for result in results],
        in_specs=[anywhere] * count,
        out_specs=[anywhere] * count,
        scratch_shapes=[
            tuple(pltpu.VMEM(result.shape, result.dtype) for result in results),
            pltpu.SemaphoreType.DMA((count,)),
            pltpu.SemaphoreType.DMA((count,)),
        ],
        compiler_params=pltpu.CompilerParams(vmem_limit_bytes=56 * 1024 * 1024),
        name="copy_out",
    )(*results)
    return mixed[None], grad_q[None], grad_k[None], grad_v[None], grad_wo


def local(queries, keys, values, upstream, w_out, key_blocks, block_counts):
    width = queries.shape[2]
    peers = lax.axis_size("seq")
    pair = 2 * (width // HEADS) == LANES and width % (peers * LANES) == 0
    whole_blocks = key_blocks.shape[1] % peers == 0 and key_blocks.shape[1] <= LANES
    whole_blocks = whole_blocks and peers >= 4
    columns_fit = lax.axis_size("dp") * LANES == width
    chosen = local_fused if pair and whole_blocks and columns_fit else local_plain
    return chosen(queries, keys, values, upstream, w_out, key_blocks, block_counts)


def solution(mesh):
    placed = (
        P("dp", "seq", None),
        P("dp", "seq", None),
        P("dp", "seq", None),
        P("dp", "seq", None),
        P(),
        P("dp", None, None),
        P("dp", None),
    )
    return jax.shard_map(
        local,
        mesh=mesh,
        in_specs=placed,
        out_specs=(
            P("dp", "seq", None),
            P("dp", "seq", None),
            P("dp", "seq", None),
            P("dp", "seq", None),
            P("seq", "dp"),
        ),
        check_vma=False,
    )
```
